32 devices in a mesh: gx: 8 (over z, y), gy: 4 (over x, core).
Axes of the slice: x: 2, y: 2, z: 4, core: 2. Of those that a mesh axis runs over, the one named last changes fastest.
Arguments:
- dual_ops: bfloat16 [8, 4, 1200, 1200], P('gx', 'gy'), as said below
- mode_traces: float32 [8, 4, 4, 6, 300], P('gx', 'gy')
- primal_trace: float32 [8, 4, 16, 1200], P('gx', 'gy')
- mode_loads: float32 [8, 4, 6, 16], P('gx', 'gy'), may hold values from -6 to 6
- face_maps: int32 [8, 4, 4, 300], P('gx', 'gy'), may hold values from 0 to 299, each once within a row
- face_live: int32 [8, 4, 4], P('gx', 'gy'), may hold values from 150 to 300, as said below
Outputs:
- multipliers: float32 [8, 4, 4, 16, 300], P('gx', 'gy')
- residual: float32 [8, 4, 4, 16, 300], P('gx', 'gy')
The draws below stay inside these ranges and needn't reach their ends.
Inputs may be any that keep to these rules, and one draw needn't show every extreme that they name: `dual_ops`: each subdomain's matrix is symmetric. `face_maps`: each face's map is a permutation of the 300 slots. `face_live`: the two faces that meet at an interface carry the same count; faces on the outer boundary of the subdomain grid are fully coupled.
All inputs are finite; a program needn't handle non-finite values.
Results may differ from the reference program's by a relative error of at most 0.019.
Values sent between devices are 32-bit elements; how exact they have to be, the bound alone decides.
No kernel may reach another device: no remote copies, remote signals or barrier semaphores. Data moves between devices by JAX's collectives and lax.ppermute only.
A program may use at most 64 MiB of HBM per device.

```python
import math
import jax
import jax.numpy as jnp
from jax import lax

FACE = 300
M = 1200
MODES = 6
LOADS = 16
SWEEPS = 2
ITERS = 2
NSX = 8
NSY = 4


def draw_dual_ops(key, part):
    key = jax.random.fold_in(key, 11)
    row_position = jnp.arange(NSY).astype(jnp.float32) / (NSY - 1)
    row_factor = jnp.exp(math.log(8.0) * (row_position - 0.5))

    def one_slab(index):
        slab_key = jax.random.fold_in(key, index)
        diag_key, off_key = jax.random.split(slab_key)
        position = index.astype(jnp.float32) / (NSX - 1)
        parity_factor = jnp.where(index % 2 == 1, 2.0, 0.5).astype(jnp.float32)
        raw = jnp.clip(jax.random.normal(off_key, (NSY, M, M), jnp.float32), -4.0, 4.0)
        diag_values = jax.random.uniform(diag_key, (NSY, M), jnp.float32, 2.2, 4.0)
        rising = jnp.exp(math.log(3.0) * position)
        scale = 0.7 / math.sqrt(M) / math.sqrt(2.0)
        symmetric = (raw + jnp.swapaxes(raw, 1, 2)) * scale
        identity = jnp.eye(M, dtype=jnp.float32)
        factor = (rising * parity_factor * row_factor)[:, None, None]
        matrices = (symmetric * (1.0 - identity) + diag_values[:, :, None] * identity) * factor
        return matrices.astype(jnp.bfloat16)
    return lax.map(one_slab, jnp.arange(NSX))


def draw_mode_traces(key, part):
    key = jax.random.fold_in(key, 23)
    base_key, rough_key = jax.random.split(key, 2)
    common = jnp.clip(jax.random.normal(base_key, (MODES, FACE), jnp.float32), -4.0, 4.0)
    rough = 0.5 * jnp.clip(jax.random.normal(rough_key, (NSX, NSY, 4, MODES, FACE), jnp.float32), -4.0, 4.0)
    return (common + rough) / math.sqrt(FACE)


def draw_primal_trace(key, part):
    key = jax.random.fold_in(key, 51)
    position = lax.broadcasted_iota(jnp.float32, (NSX, 1, 1, 1), 0) / (NSX - 1)
    values = jnp.clip(jax.random.normal(key, (NSX, NSY, LOADS, M), jnp.float32), -6.0, 6.0)
    rising = jnp.exp(math.log(3.0) * position)
    return values * rising


def draw_face_live(key, part):
    key = jax.random.fold_in(key, 37)
    first_key, second_key = jax.random.split(key)
    counts_x = jax.random.randint(first_key, (NSX + 1, NSY), FACE // 2, FACE + 1)
    counts_x = counts_x.at[0].set(FACE).at[NSX].set(FACE)
    counts_y = jax.random.randint(second_key, (NSX, NSY + 1), FACE // 2, FACE + 1)
    counts_y = counts_y.at[:, 0].set(FACE).at[:, NSY].set(FACE)
    return jnp.stack([counts_x[:-1], counts_x[1:], counts_y[:, :-1], counts_y[:, 1:]], axis=-1).astype(jnp.int32)


def levels(own_key, extent, cuts, least, top_value):
    factor_of = 1.0
    for axis_at, shards_of in cuts:
        heights = jax.random.uniform(jax.random.fold_in(jax.random.fold_in(own_key, 6), axis_at), (shards_of,), jnp.float32, least / len(cuts), top_value / len(cuts))
        factor_of = factor_of * jnp.repeat(jnp.exp(heights), extent[axis_at] // shards_of).reshape((-1,) + (1,) * (len(extent) - 1 - axis_at))
    return factor_of


def scatter_about(key, dims, deviation, reach, cuts=(), kind=jnp.bfloat16):
    values = jax.random.normal(key, dims, jnp.float32) * deviation
    if len(cuts) > 0:
        values = levels(key, dims, cuts, -0.22, 0.18) * values
    return jnp.clip(values, min=-reach, max=reach).astype(kind)


def setup_inputs(seed: int = 0) -> dict:
    keys = jax.random.split(jax.random.key(seed), 7)
    dual_ops = draw_dual_ops(jax.random.fold_in(keys[6], 71), 0)
    mode_traces = draw_mode_traces(jax.random.fold_in(keys[6], 71), 0)
    primal_trace = draw_primal_trace(jax.random.fold_in(keys[6], 71), 0)
    mode_loads = scatter_about(keys[3], (NSX, NSY, MODES, LOADS), 1.0, 6.0, ((0, 8), (1, 4)), jnp.float32)
    face_maps = jax.vmap(lambda own: jax.random.permutation(own, FACE))(jax.random.split(keys[4], NSX * NSY * 4)).reshape((NSX, NSY, 4, FACE)).astype(jnp.int32)
    face_live = draw_face_live(jax.random.fold_in(keys[6], 71), 0)
    return dict(dual_ops=dual_ops, mode_traces=mode_traces, primal_trace=primal_trace, mode_loads=mode_loads, face_maps=face_maps, face_live=face_live)


SIGNS = (-1.0, 1.0, -1.0, 1.0)
HIGHEST = lax.Precision.HIGHEST


def sign_column():
    return jnp.array(SIGNS, jnp.float32)[:, None, None]


def invert_blocks(matrix):
    block_order = matrix.shape[-1]
    inverse = jnp.broadcast_to(jnp.eye(block_order, dtype=jnp.float32), matrix.shape)
    reduced = matrix
    for pivot_index in range(block_order):
        unit_column = (jnp.arange(block_order) == pivot_index).astype(jnp.float32)[:, None]
        pivot_value = reduced[..., pivot_index:pivot_index + 1, pivot_index:pivot_index + 1]
        scaled_row = reduced[..., pivot_index:pivot_index + 1, :] / pivot_value
        scaled_inverse = inverse[..., pivot_index:pivot_index + 1, :] / pivot_value
        column = reduced[..., :, pivot_index:pivot_index + 1] - unit_column
        reduced = reduced - column * scaled_row
        inverse = inverse - column * scaled_inverse
    return inverse


def live_mask(face_live):
    slots = lax.broadcasted_iota(jnp.int32, face_live.shape + (1, FACE), 4)
    return (slots < face_live[..., None, None]).astype(jnp.float32)


def face_weights():
    shape_three = (NSX, NSY, 4)
    column = lax.broadcasted_iota(jnp.int32, shape_three, 0)
    row_index = lax.broadcasted_iota(jnp.int32, shape_three, 1)
    facet = lax.broadcasted_iota(jnp.int32, shape_three, 2)
    on_boundary = ((facet == 0) & (column == 0)) | ((facet == 1) & (column == NSX - 1)) | ((facet == 2) & (row_index == 0)) | ((facet == 3) & (row_index == NSY - 1))
    return jnp.where(on_boundary, 1.0, 0.5).astype(jnp.float32)[..., None, None]


def neighbours(canonical):
    empty_x = jnp.zeros_like(canonical[:1, :, 0])
    below_x = jnp.concatenate([empty_x, canonical[:-1, :, 1]], axis=0)
    above_x = jnp.concatenate([canonical[1:, :, 0], empty_x], axis=0)
    empty_y = jnp.zeros_like(canonical[:, :1, 2])
    below_y = jnp.concatenate([empty_y, canonical[:, :-1, 3]], axis=1)
    above_y = jnp.concatenate([canonical[:, 1:, 2], empty_y], axis=1)
    return jnp.stack([below_x, above_x, below_y, above_y], axis=2)


def jump_of(canonical, live):
    return live * sign_column() * (canonical - neighbours(canonical))


def to_local(field, face_maps):
    signed = field * sign_column()
    indices = jnp.broadcast_to(face_maps[..., None, :], signed.shape)
    picked = jnp.take_along_axis(signed, indices, axis=-1)
    moved = jnp.moveaxis(picked, -2, -3)
    return moved.reshape(moved.shape[:-2] + (moved.shape[-2] * moved.shape[-1],))


def to_canonical(local, inverse_maps):
    split = local.reshape(local.shape[:-1] + (4, local.shape[-1] // 4))
    moved = jnp.moveaxis(split, -2, -3)
    indices = jnp.broadcast_to(inverse_maps[..., None, :], moved.shape)
    return jnp.take_along_axis(moved, indices, axis=-1)


def apply_operators(local, dual_ops):
    rounded = lax.optimization_barrier(local.astype(jnp.bfloat16))

    def one_slab(pair):
        vectors, matrices = pair
        return jnp.einsum("ylm,ymn->yln", vectors.astype(jnp.float32), matrices.astype(jnp.float32), precision=HIGHEST)

    return lax.map(one_slab, (rounded, dual_ops))


def coarse_of(field, mode_traces):
    return jnp.einsum("xyfjc,xyflc->xyjl", mode_traces * sign_column(), field, precision=HIGHEST)


def trace_of(coarse_field, mode_traces):
    return jnp.einsum("xyfjc,xyjl->xyflc", mode_traces, coarse_field, precision=HIGHEST)


def blocks_apply(matrices, coarse_field):
    return jnp.einsum("xyjk,xykl->xyjl", matrices, coarse_field, precision=HIGHEST)


def reference(dual_ops, mode_traces, primal_trace, mode_loads, face_maps, face_live):
    live = live_mask(face_live)
    weights = face_weights()
    inverse_maps = jnp.argsort(face_maps, axis=-1).astype(jnp.int32)
    diagonal = jnp.einsum("xyfjc,xyfkc->xyjk", mode_traces * live, mode_traces, precision=HIGHEST)
    block_inverse = invert_blocks(diagonal)

    def lift(coarse_field):
        return jump_of(trace_of(coarse_field, mode_traces), live)

    def coarse_solve(loads):
        coarse_field = blocks_apply(block_inverse, loads)
        for sweep_index in range(SWEEPS):
            coarse_field = coarse_field + blocks_apply(block_inverse, loads - coarse_of(lift(coarse_field), mode_traces))
        return coarse_field

    def project(field):
        return field - lift(coarse_solve(coarse_of(field, mode_traces)))

    def inner(first, second):
        return jnp.sum(weights * first * second)

    multipliers = lift(coarse_solve(mode_loads))
    local_rest = primal_trace - apply_operators(to_local(multipliers, face_maps), dual_ops)
    residual = jump_of(to_canonical(local_rest, inverse_maps), live)
    projected = project(residual)
    gamma_now = inner(residual, projected)
    direction = projected
    for iteration in range(ITERS):
        image_field = jump_of(to_canonical(apply_operators(to_local(direction, face_maps), dual_ops), inverse_maps), live)
        step_size = gamma_now / inner(direction, image_field)
        multipliers = multipliers + step_size * direction
        residual = residual - step_size * image_field
        if iteration + 1 < ITERS:
            projected = project(residual)
            gamma_fresh = inner(residual, projected)
            direction = projected + (gamma_fresh / gamma_now) * direction
            gamma_now = gamma_fresh
    return multipliers, residual
```

```python
import jax
import jax.numpy as jnp
from jax import lax
from jax.sharding import PartitionSpec as P

SIGNS = (-1.0, 1.0, -1.0, 1.0)
HIGHEST = lax.Precision.HIGHEST
AXES = ("gx", "gy")
SWEEPS = 2


def exchange(faces):
    parts = []
    for axis, low, high in (("gx", 0, 1), ("gy", 2, 3)):
        count = lax.axis_size(axis)
        forward = [(i, i + 1) for i in range(count - 1)]
        backward = [(i + 1, i) for i in range(count - 1)]
        parts.append(lax.ppermute(faces[high], axis, forward))
        parts.append(lax.ppermute(faces[low], axis, backward))
    return jnp.stack(parts)


def gather(values):
    count = lax.axis_size("gx") * lax.axis_size("gy")
    copies = jnp.broadcast_to(values, (count,) + values.shape)
    return lax.all_to_all(copies, AXES, 0, 0, tiled=True)


def doubling_gather(values):
    rows = values[None]
    for axis in ("gy", "gx"):
        count, unit = lax.axis_size(axis), rows.shape[0]
        held = 1
        while held < count:
            step = min(held, count - held)
            pairs = [(i, (i - held) % count) for i in range(count)]
            rows = jnp.concatenate([rows, lax.ppermute(rows[: step * unit], axis, pairs)])
            held += step
    return rows


def invert(matrix):
    order = matrix.shape[-1]
    inverse = jnp.eye(order, dtype=jnp.float32)
    reduced = matrix
    for pivot in range(order):
        unit = (jnp.arange(order) == pivot).astype(jnp.float32)[:, None]
        value = reduced[pivot : pivot + 1, pivot : pivot + 1]
        row = reduced[pivot : pivot + 1, :] / value
        inverse_row = inverse[pivot : pivot + 1, :] / value
        column = reduced[:, pivot : pivot + 1] - unit
        reduced = reduced - column * row
        inverse = inverse - column * inverse_row
    return inverse


def shifted(field, face, row):
    return jnp.roll(field, (row, -row, 1, -1)[face], axis=-1)


def body(dual_ops, mode_traces, primal_trace, mode_loads, face_maps, face_live):
    nx, ny = lax.axis_size("gx"), lax.axis_size("gy")
    ix, iy = lax.axis_index("gx"), lax.axis_index("gy")
    ops, traces, primal, loads = dual_ops[0, 0], mode_traces[0, 0], primal_trace[0, 0], mode_loads[0, 0]
    maps, counts = face_maps[0, 0], face_live[0, 0]
    modes, size = traces.shape[1:]
    cases = loads.shape[1]
    signs = jnp.array(SIGNS, jnp.float32)[:, None, None]
    slots = lax.broadcasted_iota(jnp.int32, (4, 1, size), 2)
    live = (slots < counts[:, None, None]).astype(jnp.float32)
    signed_live = live * signs
    table = (maps[..., None] == lax.broadcasted_iota(jnp.int32, (4, size, size), 2)).astype(jnp.float32)
    boundary = jnp.stack([ix == 0, ix == nx - 1, iy == 0, iy == ny - 1])
    weights = jnp.where(boundary, 1.0, 0.5).astype(jnp.float32)[:, None, None]

    def to_local(field):
        picked = jnp.einsum("fkc,flc->lfk", table, field * signs, precision=HIGHEST)
        return picked.reshape(cases, 4 * size)

    def to_canonical(local):
        return jnp.einsum("fkc,lfk->flc", table, local.reshape(cases, 4, size), precision=HIGHEST)

    def apply(local):
        return jnp.einsum("lm,mn->ln", local.astype(jnp.bfloat16), ops, preferred_element_type=jnp.float32)

    live_traces = traces * live
    next_traces = exchange(traces)
    inverse = invert(jnp.einsum("fjc,fkc->jk", live_traces, traces, precision=HIGHEST))
    coupling = jnp.einsum("fjc,fkc->fjk", live_traces, next_traces, precision=HIGHEST)
    coupling = jnp.einsum("ij,fjk->fik", inverse, coupling, precision=HIGHEST)
    first = jnp.einsum("jk,kl->jl", inverse, loads, precision=HIGHEST)
    everyone = gather(jnp.concatenate([inverse.reshape(-1), coupling.reshape(-1), first.reshape(-1)])).T
    square = modes * modes
    all_inverse = everyone[:square].reshape(modes, modes, -1)
    all_coupling = everyone[square : 5 * square].reshape(4, modes, modes, 1, -1)
    all_first = everyone[5 * square :].reshape(modes, cases, -1)
    spot = ix * ny + iy

    def pick(field, face):
        moved = shifted(field, face, ny) if face >= 0 else field
        return lax.dynamic_slice_in_dim(moved, spot, 1, axis=2)[..., 0]

    near_inverse = jnp.stack([pick(all_inverse, face) for face in range(4)])
    own_rows = jnp.einsum("ij,fjc->fic", inverse, live_traces, precision=HIGHEST)
    next_rows = jnp.einsum("fij,fjc->fic", near_inverse, next_traces * live, precision=HIGHEST)
    rows = jnp.concatenate([own_rows, next_rows], axis=1)
    lift_rows = jnp.concatenate([traces * signed_live, -next_traces * signed_live], axis=1)

    def coarse_lift(start):
        field = start
        for sweep in range(SWEEPS):
            update = start
            for face in range(4):
                near = shifted(field, face, ny)
                for k in range(modes):
                    update = update + all_coupling[face, :, k] * near[k][None]
            field = update
        own = jnp.broadcast_to(pick(field, -1), (4, modes, cases))
        near = jnp.stack([pick(field, face) for face in range(4)])
        return jnp.einsum("fjc,fjl->flc", lift_rows, jnp.concatenate([own, near], axis=1), precision=HIGHEST)

    def jump_and_lift(canonical, scalars):
        parts = jnp.einsum("fjc,flc->fjl", rows, canonical, precision=HIGHEST)
        mine = jnp.sum(parts[:, :modes], axis=0)
        sent = jnp.concatenate([mine.reshape(-1), parts[:, modes:].reshape(-1)] + [s.reshape(1) for s in scalars])
        received = gather(sent).T
        field = signed_live * (canonical - exchange(canonical))
        block = modes * cases
        start = received[:block]
        for face in range(4):
            across = received[(1 + (face ^ 1)) * block : (2 + (face ^ 1)) * block]
            start = start - shifted(across, face, ny)
        lifted = coarse_lift(start.reshape(modes, cases, -1))
        sums = jnp.sum(received[5 * block :], axis=1)
        return field, lifted, sums

    multipliers = coarse_lift(all_first)
    residual, lifted, _ = jump_and_lift(to_canonical(primal - apply(to_local(multipliers))), [])
    direction = residual - lifted
    local_direction = to_local(direction)
    image_local = apply(local_direction)
    image, lifted, sums = jump_and_lift(
        to_canonical(image_local),
        [jnp.sum(weights * residual * direction), jnp.sum(local_direction * image_local)],
    )
    gamma, curvature = sums[0], sums[1]
    alpha = gamma / curvature
    multipliers = multipliers + alpha * direction
    residual = residual - alpha * image
    projected = direction - alpha * (image - lifted)
    local_projected = to_local(projected)
    fresh_local = apply(local_projected)
    fresh_canonical = to_canonical(fresh_local)
    sums = doubling_gather(jnp.stack([
        jnp.sum(weights * residual * projected),
        jnp.sum(local_projected * fresh_local),
        jnp.sum(weights * projected * image) + jnp.sum(local_direction * fresh_local),
    ])).sum(axis=0)
    fresh_image = signed_live * (fresh_canonical - exchange(fresh_canonical))
    beta = sums[0] / gamma
    alpha = sums[0] / (sums[1] + beta * sums[2] + beta * beta * curvature)
    multipliers = multipliers + alpha * (projected + beta * direction)
    residual = residual - alpha * (fresh_image + beta * image)
    return multipliers[None, None], residual[None, None]


def solution(mesh):
    in_specs = (
        P("gx", "gy", None, None),
        P("gx", "gy", None, None, None),
        P("gx", "gy", None, None),
        P("gx", "gy", None, None),
        P("gx", "gy", None, None),
        P("gx", "gy", None),
    )
    out_specs = (P("gx", "gy", None, None, None), P("gx", "gy", None, None, None))
    return jax.shard_map(body, mesh=mesh, in_specs=in_specs, out_specs=out_specs, check_vma=False)
```

```python
import functools

import jax
import jax.numpy as jnp
from jax import lax
from jax.experimental import pallas as pl
from jax.experimental.pallas import tpu as pltpu
from jax.sharding import PartitionSpec as P

SIGNS = (-1.0, 1.0, -1.0, 1.0)
HIGHEST = lax.Precision.HIGHEST
AXES = ("gx", "gy")
F32 = jnp.float32
BF16 = jnp.bfloat16
VMEM = pltpu.VMEM
SMEM = pltpu.SMEM
FIRST_LANE = 32
INVERSE_LANE = 48
SCALAR_LANE = 96


class Sizes:
    def __init__(self, nx, ny, traces, loads):
        self.nx, self.ny = nx, ny
        self.count = nx * ny
        self.modes, self.face = traces.shape[-2:]
        self.cases = loads.shape[-1]
        self.order = 4 * self.face
        self.lanes = -(-self.face // 128) * 128
        self.starts = [f * self.face // 128 * 128 for f in range(4)]
        ends = [-(-(f + 1) * self.face // 128) * 128 for f in range(4)]
        self.width = max(e - s for s, e in zip(self.starts, ends))
        self.padded = max(s + self.width for s in self.starts)
        self.wide = min(nx, 9)
        self.rows = self.wide * ny * 8
        self.steps = (-ny, ny, -1, 1)


def dot(a, b, contract=(1, 0), precision=HIGHEST):
    dims = (((contract[0],), (contract[1],)), ((), ()))
    return lax.dot_general(a, b, dims, precision=precision, preferred_element_type=F32)


def iota(shape, dim):
    return lax.broadcasted_iota(jnp.int32, shape, dim)


def place():
    return lax.axis_index("gx"), lax.axis_index("gy")


def window_start(z, ix):
    return jnp.clip(ix - 4, 0, z.nx - z.wide) if z.wide < z.nx else 0


def spots(z, ix, iy):
    own = (ix - window_start(z, ix)) * z.ny + iy
    return [own] + [jnp.clip(own + step, 0, z.wide * z.ny - 1) for step in z.steps]


def live_row(z, counts, face):
    return (iota((1, z.lanes), 1) < counts[0, 0, face]).astype(F32)


def send_faces(z, faces, to_x, to_y):
    ix, iy = place()
    for ref, at, size, low, high in ((to_x, ix, z.nx, 0, 1), (to_y, iy, z.ny, 2, 3)):
        up = jnp.where(at + 1 < size, at + 1, at)
        down = jnp.where(at > 0, at - 1, at)
        ref[pl.ds(up, 1)] = faces[high][None]
        ref[pl.ds(down, 1)] = faces[low][None]


def faces_across(z, from_x, from_y):
    ix, iy = place()
    found = []
    for ref, at, size in ((from_x, ix, z.nx), (from_y, iy, z.ny)):
        for there, valid in ((at - 1, at > 0), (at + 1, at + 1 < size)):
            values = ref[pl.ds(jnp.clip(there, 0, size - 1), 1)][0]
            found.append(jnp.where(valid, values, jnp.zeros_like(values)))
    return found


def pack_traces(z, traces, padded, to_x, to_y):
    padded[...] = jnp.zeros_like(padded)
    for f in range(4):
        padded[f, 0 : z.modes, 0 : z.face] = traces[0, 0, f]
    send_faces(z, [padded[f] for f in range(4)], to_x, to_y)


def set_up(z, padded, counts, maps, loads, forward, backward, local_tile, flat, aug, small):
    flat[...] = jnp.zeros_like(flat)
    flat[0:4, 0 : z.face] = maps[0, 0]
    lane = iota((1, z.padded), 1)
    line = jnp.full((1, z.padded), -1, jnp.int32)
    for f in range(4):
        moved = pltpu.roll(flat[...], f * z.face, 1)[f : f + 1] if f else flat[0:1]
        line = jnp.where((lane >= f * z.face) & (lane < (f + 1) * z.face), moved, line)
    column = jnp.transpose(jnp.broadcast_to(line, (8, z.padded)))[:, 0:1]
    place_of = iota((z.padded, 1), 0)
    for f in range(4):
        low, high = f * z.face, (f + 1) * z.face
        window = slice(z.starts[f], z.starts[f] + z.width)
        here = jnp.where((lane >= low) & (lane < high), line, -1)[:, window]
        forward[f] = (iota((z.lanes, z.width), 0) == here).astype(F32).astype(BF16)
        there = jnp.where((place_of >= low) & (place_of < high), column, -1)[window]
        backward[f] = (iota((z.width, z.lanes), 1) == there).astype(F32).astype(BF16)
    diagonal = sum(dot(padded[f] * live_row(z, counts, f), padded[f], (1, 1)) for f in range(4))
    row, col = iota((8, 128), 0), iota((8, 128), 1)
    aug[...] = jnp.where((col == row + 8) & (row < z.modes), 1.0, 0.0).astype(F32)
    aug[:, 0:8] = diagonal
    matrix = aug[...]
    for p in range(z.modes):
        scaled = matrix[p : p + 1, :] / matrix[p : p + 1, p : p + 1]
        taken = matrix[:, p : p + 1] - (row[:, 0:1] == p).astype(F32)
        matrix = matrix - taken * scaled
    inverse = matrix[:, 8:16]
    small[...] = jnp.zeros_like(small)
    small[0 : z.modes, :] = loads[0, 0]
    local_tile[...] = jnp.zeros_like(local_tile)
    local_tile[:, FIRST_LANE : FIRST_LANE + z.cases] = dot(inverse, small[...])
    local_tile[:, INVERSE_LANE : INVERSE_LANE + 8] = inverse


def couple(z, padded, counts, from_x, from_y, local_tile, across, sent, tile):
    near = faces_across(z, from_x, from_y)
    inverse = local_tile[:, INVERSE_LANE : INVERSE_LANE + 8]
    tile[...] = local_tile[...]
    for f in range(4):
        across[f] = near[f]
        coupling = dot(padded[f] * live_row(z, counts, f), near[f], (1, 1))
        tile[:, 8 * f : 8 * f + 8] = dot(inverse, coupling)
    sent[...] = jnp.broadcast_to(tile[...][None], sent.shape)


def lifted(z, amplitudes, lift_rows, f):
    pair = jnp.concatenate([amplitudes[0:8], amplitudes[8 * f + 8 : 8 * f + 16]], axis=0)
    return dot(pair, lift_rows[f], (0, 0))


def apply(z, faces, ops, forward, backward, local, product):
    local[...] = jnp.zeros_like(local)
    for f in range(4):
        window = slice(z.starts[f], z.starts[f] + z.width)
        signed = (faces[f] * SIGNS[f]).astype(BF16)
        local[:, window] += dot(signed, forward[f], precision=None)
    operand = local[:, 0 : z.order].astype(BF16)
    return dot(operand, ops[0, 0], precision=None)


def canonical(z, values, backward, product):
    product[...] = jnp.zeros_like(product)
    product[:, 0 : z.order] = values
    found = []
    for f in range(4):
        part = product[:, z.starts[f] : z.starts[f] + z.width]
        high = part.astype(BF16)
        low = (part - high.astype(F32)).astype(BF16)
        both = dot(jnp.concatenate([high, low], axis=0), backward[f], precision=None)
        found.append(both[0 : z.cases] + both[z.cases :])
    return found


def send_coarse(z, faces, rows, scalars, sent, tile):
    tile[...] = jnp.zeros_like(tile)
    mine = jnp.zeros((8, z.cases), F32)
    for f in range(4):
        both = dot(rows[f], faces[f], (1, 1))
        mine = mine + both[0:8]
        tile[:, (1 + f) * z.cases : (2 + f) * z.cases] = both[8:16]
    tile[:, 0 : z.cases] = mine
    send_tile(tile[...], scalars, sent)


def send_tile(values, scalars, sent):
    row, col = iota((8, 128), 0), iota((8, 128), 1)
    for i, scalar in enumerate(scalars):
        values = jnp.where((row == 0) & (col == SCALAR_LANE + i), scalar, values)
    sent[...] = jnp.broadcast_to(values[None], sent.shape)


def scalar_of(total, i):
    row, col = iota((8, 128), 0), iota((8, 128), 1)
    return jnp.sum(jnp.where((row == 0) & (col == SCALAR_LANE + i), total, 0.0), keepdims=True)


def received_window(z, received):
    ix, _ = place()
    start = window_start(z, ix) * z.ny
    return received[pl.ds(start, z.wide * z.ny)].reshape(z.rows, 128)


def coarse_amplitudes(z, received, solve_rows):
    values = received_window(z, received)
    start = values
    for f in range(4):
        across = pltpu.roll(values, 128 - (1 + (f ^ 1)) * z.cases, 1)
        step = 8 * z.steps[f]
        empty = jnp.zeros((abs(step), 128), F32)
        if step > 0:
            moved = jnp.concatenate([across[step:], empty], axis=0)
        else:
            moved = jnp.concatenate([empty, across[: z.rows + step]], axis=0)
        start = start - moved
    return dot(solve_rows[...], start)[:, 0 : z.cases]


def total(values):
    return jnp.sum(values, keepdims=True)


def face_weights(z):
    ix, iy = place()
    edges = (ix == 0, ix == z.nx - 1, iy == 0, iy == z.ny - 1)
    return [jnp.where(edge, 1.0, 0.5).astype(F32) for edge in edges]


def begin(
    z, received, padded, across, counts, primal, ops, forward, backward, local_tile,
    solve_rows, rows, lift_rows, multipliers, faces, sent, to_x, to_y,
    matrix, local, product, tile,
):
    ix, iy = place()
    near_spots = spots(z, ix, iy)
    values = received_window(z, received)
    lane = iota((z.rows, 128), 1)
    row = iota((z.rows, 128), 0)
    tiled = []
    for f in range(4):
        part = jnp.where(lane // 8 == f, values, 0.0)
        for shift in (64, 32, 16, 8):
            part = part + pltpu.roll(part, shift, 1)
        tiled.append(part)
    for block in range(-(-z.rows // 128)):
        target = (lane + 128 * block) // 8 - row // 8
        part = jnp.zeros((z.rows, 128), F32)
        for f in range(4):
            part = part + jnp.where(target == z.steps[f], tiled[f], 0.0)
        matrix[:, 128 * block : 128 * block + 128] = part
    once = jnp.concatenate([matrix[pl.ds(pl.multiple_of(s * 8, 8), 8), 0 : z.rows] for s in near_spots], axis=0)
    twice = dot(once, matrix[:, 0 : z.rows])
    cols = z.rows
    unit = jnp.concatenate([
        (iota((8, cols), 1) == iota((8, cols), 0) + s * 8).astype(F32) for s in near_spots
    ], axis=0)
    solve = unit + once + twice
    solve_rows[...] = solve
    amplitudes = dot(solve, values)[:, FIRST_LANE : FIRST_LANE + z.cases]
    inverse = local_tile[:, INVERSE_LANE : INVERSE_LANE + 8]
    start = window_start(z, ix) * z.ny
    fields = []
    for f in range(4):
        live = live_row(z, counts, f)
        near_inverse = received[pl.ds(start + near_spots[1 + f], 1)][0][:, INVERSE_LANE : INVERSE_LANE + 8]
        own, near = padded[f] * live, across[f] * live
        rows[f] = jnp.concatenate([dot(inverse, own), dot(near_inverse, near)], axis=0)
        lift_rows[f] = jnp.concatenate([own * SIGNS[f], near * -SIGNS[f]], axis=0)
        fields.append(lifted(z, amplitudes, lift_rows, f))
        multipliers[f] = fields[f]
    image = primal[0, 0] - apply(z, fields, ops, forward, backward, local, product)
    image = canonical(z, image, backward, product)
    for f in range(4):
        faces[f] = image[f]
    send_faces(z, image, to_x, to_y)
    send_coarse(z, image, rows, [], sent, tile)


def jumped(z, counts, faces, from_x, from_y):
    near = faces_across(z, from_x, from_y)
    return [live_row(z, counts, f) * SIGNS[f] * (faces[f] - near[f]) for f in range(4)]


def first_direction(
    z, received, from_x, from_y, faces, counts, ops, forward, backward, solve_rows, rows, lift_rows,
    residual, direction, image, sent, to_x, to_y,
    local, product, tile,
):
    amplitudes = coarse_amplitudes(z, received, solve_rows)
    field = jumped(z, counts, faces, from_x, from_y)
    weights = face_weights(z)
    moved = [field[f] - lifted(z, amplitudes, lift_rows, f) for f in range(4)]
    found = canonical(z, apply(z, moved, ops, forward, backward, local, product), backward, product)
    for f in range(4):
        residual[f] = field[f]
        direction[f] = moved[f]
        image[f] = found[f]
    gamma = sum(weights[f] * total(field[f] * moved[f]) for f in range(4))
    curvature = sum(SIGNS[f] * total(moved[f] * found[f]) for f in range(4))
    send_faces(z, found, to_x, to_y)
    send_coarse(z, found, rows, [gamma, curvature], sent, tile)


def second_direction(
    z, received, from_x, from_y, faces, counts, ops, forward, backward, solve_rows, lift_rows,
    multipliers, residual, direction,
    next_multipliers, next_residual, projected, image, fresh, sums, sent, to_x, to_y,
    local, product,
):
    amplitudes = coarse_amplitudes(z, received, solve_rows)
    summed = jnp.sum(received[...], axis=0)
    sums[...] = summed
    alpha = scalar_of(summed, 0) / scalar_of(summed, 1)
    field = jumped(z, counts, faces, from_x, from_y)
    weights = face_weights(z)
    left, moved = [], []
    for f in range(4):
        image[f] = field[f]
        next_multipliers[f] = multipliers[f] + alpha * direction[f]
        left.append(residual[f] - alpha * field[f])
        moved.append(direction[f] - alpha * (field[f] - lifted(z, amplitudes, lift_rows, f)))
        next_residual[f] = left[f]
        projected[f] = moved[f]
    found = canonical(z, apply(z, moved, ops, forward, backward, local, product), backward, product)
    for f in range(4):
        fresh[f] = found[f]
    send_faces(z, found, to_x, to_y)
    gamma = sum(weights[f] * total(left[f] * moved[f]) for f in range(4))
    straight = sum(SIGNS[f] * total(moved[f] * found[f]) for f in range(4))
    crossed = sum(
        weights[f] * total(moved[f] * field[f]) + SIGNS[f] * total(direction[f] * found[f]) for f in range(4)
    )
    send_tile(jnp.zeros((8, 128), F32), [gamma, straight, crossed], sent)


def finish(
    z, received, from_x, from_y, faces, counts, sums, multipliers, residual, direction, projected, image,
    out_multipliers, out_residual,
):
    summed = jnp.sum(received[...], axis=0)
    field = jumped(z, counts, faces, from_x, from_y)
    gamma, curvature = scalar_of(sums[...], 0), scalar_of(sums[...], 1)
    fresh, straight, crossed = (scalar_of(summed, i) for i in range(3))
    beta = fresh / gamma
    alpha = fresh / (straight + beta * crossed + beta * beta * curvature)
    for f in range(4):
        step = projected[f] + beta * direction[f]
        out_multipliers[0, 0, f] = (multipliers[f] + alpha * step)[:, 0 : z.face]
        out_residual[0, 0, f] = (residual[f] - alpha * (field[f] + beta * image[f]))[:, 0 : z.face]


def call(z, kernel, outs, args, scratch=(), flops=0):
    shapes = [jax.ShapeDtypeStruct(shape, dtype) for shape, dtype in outs]
    moved = sum(a.size * a.dtype.itemsize for a in args) + sum(s.size * s.dtype.itemsize for s in shapes)
    return pl.pallas_call(
        functools.partial(kernel, z),
        out_shape=shapes,
        in_specs=[pl.BlockSpec(memory_space=SMEM if a.ndim == 3 and a.size == 4 else VMEM) for a in args],
        out_specs=[pl.BlockSpec(memory_space=VMEM) for _ in shapes],
        scratch_shapes=[VMEM(shape, dtype) for shape, dtype in scratch],
        compiler_params=pltpu.CompilerParams(vmem_limit_bytes=40 * 2**20),
        cost_estimate=pl.CostEstimate(flops=flops, bytes_accessed=moved, transcendentals=0),
        name=kernel.__name__,
    )(*args)


def swap(values, axis):
    return lax.all_to_all(values, axis, 0, 0, tiled=True)


def body(ops, traces, primal, loads, maps, counts):
    z = Sizes(lax.axis_size("gx"), lax.axis_size("gy"), traces, loads)
    field = ((4, z.cases, z.lanes), F32)
    mode_rows = ((4, 8, z.lanes), F32)
    pair_rows = ((4, 16, z.lanes), F32)
    tile = ((8, 128), F32)
    sent = ((z.count, 8, 128), F32)
    to_x, to_y = ((z.nx, z.cases, z.lanes), F32), ((z.ny, z.cases, z.lanes), F32)
    padded_rows = ((z.cases, z.padded), F32)
    columns = -(-z.rows // 128) * 128
    product_flops = 2 * z.cases * z.order * z.order

    padded, trace_x, trace_y = call(
        z, pack_traces,
        [mode_rows, ((z.nx, 8, z.lanes), F32), ((z.ny, 8, z.lanes), F32)], [traces],
    )
    trace_x, trace_y = swap(trace_x, "gx"), swap(trace_y, "gy")
    forward, backward, local_tile = call(
        z, set_up,
        [((4, z.lanes, z.width), BF16), ((4, z.width, z.lanes), BF16), tile], [padded, counts, maps, loads],
        [((8, z.padded), jnp.int32), tile, ((8, z.cases), F32)], product_flops,
    )
    across, blocks = call(z, couple, [mode_rows, sent], [padded, counts, trace_x, trace_y, local_tile], [tile])
    blocks = swap(blocks, AXES)
    solve_rows, rows, lift_rows, multipliers, faces, coarse, face_x, face_y = call(
        z, begin,
        [((40, z.rows), F32), pair_rows, pair_rows, field, field, sent, to_x, to_y],
        [blocks, padded, across, counts, primal, ops, forward, backward, local_tile],
        [((z.rows, columns), F32), padded_rows, padded_rows, tile], product_flops,
    )
    coarse, face_x, face_y = swap(coarse, AXES), swap(face_x, "gx"), swap(face_y, "gy")
    residual, direction, faces, coarse, face_x, face_y = call(
        z, first_direction,
        [field, field, field, sent, to_x, to_y],
        [coarse, face_x, face_y, faces, counts, ops, forward, backward, solve_rows, rows, lift_rows],
        [padded_rows, padded_rows, tile], product_flops,
    )
    coarse, face_x, face_y = swap(coarse, AXES), swap(face_x, "gx"), swap(face_y, "gy")
    multipliers, residual, projected, image, faces, sums, coarse, face_x, face_y = call(
        z, second_direction,
        [field, field, field, field, field, tile, sent, to_x, to_y],
        [coarse, face_x, face_y, faces, counts, ops, forward, backward, solve_rows, lift_rows,
         multipliers, residual, direction],
        [padded_rows, padded_rows], product_flops,
    )
    coarse, face_x, face_y = swap(coarse, AXES), swap(face_x, "gx"), swap(face_y, "gy")
    whole = ((1, 1, 4, z.cases, z.face), F32)
    multipliers, residual = call(
        z, finish, [whole, whole],
        [coarse, face_x, face_y, faces, counts, sums, multipliers, residual, direction, projected, image],
    )
    return multipliers, residual


def solution(mesh):
    in_specs = (
        P("gx", "gy", None, None),
        P("gx", "gy", None, None, None),
        P("gx", "gy", None, None),
        P("gx", "gy", None, None),
        P("gx", "gy", None, None),
        P("gx", "gy", None),
    )
    out_specs = (P("gx", "gy", None, None, None), P("gx", "gy", None, None, None))
    return jax.shard_map(body, mesh=mesh, in_specs=in_specs, out_specs=out_specs, check_vma=False)
```

```python
import functools

import jax
import jax.numpy as jnp
from jax import lax
from jax.experimental import pallas as pl
from jax.experimental.pallas import tpu as pltpu
from jax.sharding import PartitionSpec as P

SIGNS = (-1.0, 1.0, -1.0, 1.0)
HIGHEST = lax.Precision.HIGHEST
AXES = ("gx", "gy")
F32 = jnp.float32
BF16 = jnp.bfloat16
VMEM = pltpu.VMEM
SMEM = pltpu.SMEM
FIRST_LANE = 32
INVERSE_LANE = 48
SCALAR_LANE = 96


class Sizes:
    def __init__(self, nx, ny, traces, loads):
        self.nx, self.ny = nx, ny
        self.count = nx * ny
        self.modes, self.face = traces.shape[-2:]
        self.cases = loads.shape[-1]
        self.order = 4 * self.face
        self.lanes = -(-self.face // 128) * 128
        self.starts = [f * self.face // 128 * 128 for f in range(4)]
        ends = [-(-(f + 1) * self.face // 128) * 128 for f in range(4)]
        self.width = max(e - s for s, e in zip(self.starts, ends))
        self.padded = max(s + self.width for s in self.starts)
        self.wide = min(nx, 9)
        self.rows = self.wide * ny * 8
        self.steps = (-ny, ny, -1, 1)


def dot(a, b, contract=(1, 0), precision=HIGHEST):
    dims = (((contract[0],), (contract[1],)), ((), ()))
    return lax.dot_general(a, b, dims, precision=precision, preferred_element_type=F32)


def iota(shape, dim):
    return lax.broadcasted_iota(jnp.int32, shape, dim)


def place():
    return lax.axis_index("gx"), lax.axis_index("gy")


def window_start(z, ix):
    return jnp.clip(ix - 4, 0, z.nx - z.wide) if z.wide < z.nx else 0


def spots(z, ix, iy):
    own = (ix - window_start(z, ix)) * z.ny + iy
    return [own] + [jnp.clip(own + step, 0, z.wide * z.ny - 1) for step in z.steps]


def send_faces(z, faces, sent):
    for i, at in enumerate(place()):
        even = at % 2 == 0
        low, high = faces[2 * i], faces[2 * i + 1]
        sent[2 * i][...] = jnp.where(even, high, low)
        sent[2 * i + 1][...] = jnp.where(even, low, high)


def across_faces(z, got):
    found = []
    for i, at in enumerate(place()):
        even = at % 2 == 0
        first, second = got[2 * i][...], got[2 * i + 1][...]
        found += [jnp.where(even, second, first), jnp.where(even, first, second)]
    return found


def exchange(sent):
    got = []
    for i, values in enumerate(sent):
        axis = AXES[i // 2]
        pairs = []
        for low in range(i % 2, lax.axis_size(axis) - 1, 2):
            pairs += [(low, low + 1), (low + 1, low)]
        got.append(lax.ppermute(values, axis, pairs))
    return got


def prepare(z, traces, counts, padded, masks, *sent):
    padded[...] = jnp.zeros_like(padded)
    for f in range(4):
        for j in range(z.modes):
            padded[f, j : j + 1, 0 : z.face] = traces[0, 0, j, f : f + 1]
        live = (iota((8, z.lanes), 1) < counts[0, 0, f]).astype(F32)
        masks[f] = live
    send_faces(z, [padded[f] for f in range(4)], sent)


def tables(z, maps, forward, backward, flat):
    flat[...] = jnp.zeros_like(flat)
    flat[0:4, 0 : z.face] = maps[0, 0]
    lane = iota((1, z.padded), 1)
    line = jnp.full((1, z.padded), -1, jnp.int32)
    for f in range(4):
        moved = pltpu.roll(flat[...], f * z.face, 1)[f : f + 1] if f else flat[0:1]
        line = jnp.where((lane >= f * z.face) & (lane < (f + 1) * z.face), moved, line)
    column = jnp.transpose(jnp.broadcast_to(line, (8, z.padded)))[:, 0:1]
    place_of = iota((z.padded, 1), 0)
    for f in range(4):
        low, high = f * z.face, (f + 1) * z.face
        window = slice(z.starts[f], z.starts[f] + z.width)
        here = jnp.where((lane >= low) & (lane < high), line, -1)[:, window]
        forward[f] = (iota((z.lanes, z.width), 0) == here).astype(F32).astype(BF16)
        there = jnp.where((place_of >= low) & (place_of < high), column, -1)[window]
        backward[f] = (iota((z.width, z.lanes), 1) == there).astype(F32).astype(BF16)


def couple(z, padded, masks, loads, got0, got1, got2, got3, across, local_tile, sent, aug, small):
    near = across_faces(z, (got0, got1, got2, got3))
    live = [padded[f] * masks[f] for f in range(4)]
    diagonal = sum(dot(live[f], padded[f], (1, 1)) for f in range(4))
    row, col = iota((8, 128), 0), iota((8, 128), 1)
    aug[...] = jnp.where((col == row + 8) & (row < z.modes), 1.0, 0.0).astype(F32)
    aug[:, 0:8] = diagonal
    matrix = aug[...]
    for p in range(z.modes):
        scaled = matrix[p : p + 1, :] / matrix[p : p + 1, p : p + 1]
        taken = matrix[:, p : p + 1] - (row[:, 0:1] == p).astype(F32)
        matrix = matrix - taken * scaled
    inverse = matrix[:, 8:16]
    small[...] = jnp.zeros_like(small)
    for j in range(z.modes):
        small[j : j + 1, :] = loads[0, j]
    local_tile[...] = jnp.zeros_like(local_tile)
    local_tile[:, FIRST_LANE : FIRST_LANE + z.cases] = dot(inverse, small[...])
    local_tile[:, INVERSE_LANE : INVERSE_LANE + 8] = inverse
    for f in range(4):
        across[f] = near[f]
        coupling = dot(live[f], near[f], (1, 1))
        local_tile[:, 8 * f : 8 * f + 8] = dot(inverse, coupling)
    sent[...] = jnp.broadcast_to(local_tile[...][None], sent.shape)


def lifted(z, amplitudes, lift_rows, f):
    pair = jnp.concatenate([amplitudes[0:8], amplitudes[8 * f + 8 : 8 * f + 16]], axis=0)
    return dot(pair, lift_rows[f], (0, 0))


def apply(z, faces, ops, forward, local):
    local[...] = jnp.zeros_like(local)
    for f in range(4):
        window = slice(z.starts[f], z.starts[f] + z.width)
        signed = (faces[f] * SIGNS[f]).astype(BF16)
        local[:, window] += dot(signed, forward[f], precision=None)
    operand = local[:, 0 : z.order].astype(BF16)
    return dot(operand, ops[0, 0], precision=None)


def canonical(z, values, backward, product):
    product[...] = jnp.zeros_like(product)
    product[:, 0 : z.order] = values
    found = []
    for f in range(4):
        part = product[:, z.starts[f] : z.starts[f] + z.width]
        high = part.astype(BF16)
        low = (part - high.astype(F32)).astype(BF16)
        both = dot(jnp.concatenate([high, low], axis=0), backward[f], precision=None)
        found.append(both[0 : z.cases] + both[z.cases :])
    return found


def send_coarse(z, faces, rows, scalars, sent, tile):
    tile[...] = jnp.zeros_like(tile)
    mine = jnp.zeros((8, z.cases), F32)
    for f in range(4):
        both = dot(rows[f], faces[f], (1, 1))
        mine = mine + both[0:8]
        tile[:, (1 + f) * z.cases : (2 + f) * z.cases] = both[8:16]
    tile[:, 0 : z.cases] = mine
    send_tile(tile[...], scalars, sent)


def send_tile(values, scalars, sent):
    row, col = iota((8, 128), 0), iota((8, 128), 1)
    for i, scalar in enumerate(scalars):
        values = jnp.where((row == 0) & (col == SCALAR_LANE + i), scalar, values)
    sent[...] = jnp.broadcast_to(values[None], sent.shape)


def scalar_of(total, i):
    row, col = iota((8, 128), 0), iota((8, 128), 1)
    return jnp.sum(jnp.where((row == 0) & (col == SCALAR_LANE + i), total, 0.0), keepdims=True)


def received_window(z, received):
    ix, _ = place()
    start = window_start(z, ix) * z.ny
    return received[pl.ds(start, z.wide * z.ny)].reshape(z.rows, 128)


def coarse_amplitudes(z, received, solve_rows):
    values = received_window(z, received)
    start = values
    for f in range(4):
        across = pltpu.roll(values, 128 - (1 + (f ^ 1)) * z.cases, 1)
        step = 8 * z.steps[f]
        empty = jnp.zeros((abs(step), 128), F32)
        if step > 0:
            moved = jnp.concatenate([across[step:], empty], axis=0)
        else:
            moved = jnp.concatenate([empty, across[: z.rows + step]], axis=0)
        start = start - moved
    return dot(solve_rows[...], start)[:, 0 : z.cases]


def total(values):
    return jnp.sum(values, keepdims=True)


def face_weights(z):
    ix, iy = place()
    edges = (ix == 0, ix == z.nx - 1, iy == 0, iy == z.ny - 1)
    return [jnp.where(edge, 1.0, 0.5).astype(F32) for edge in edges]


def begin(
    z, received, padded, across, masks, primal, ops, forward, backward, local_tile,
    solve_rows, rows, lift_rows, multipliers, faces, sent, to0, to1, to2, to3,
    matrix, local, product, tile,
):
    ix, iy = place()
    near_spots = spots(z, ix, iy)
    values = received_window(z, received)
    lane = iota((z.rows, 128), 1)
    row = iota((z.rows, 128), 0)
    tiled = []
    for f in range(4):
        part = jnp.where(lane // 8 == f, values, 0.0)
        for shift in (64, 32, 16, 8):
            part = part + pltpu.roll(part, shift, 1)
        tiled.append(part)
    for block in range(-(-z.rows // 128)):
        target = (lane + 128 * block) // 8 - row // 8
        part = jnp.zeros((z.rows, 128), F32)
        for f in range(4):
            part = part + jnp.where(target == z.steps[f], tiled[f], 0.0)
        matrix[:, 128 * block : 128 * block + 128] = part
    once = jnp.concatenate([matrix[pl.ds(pl.multiple_of(s * 8, 8), 8), 0 : z.rows] for s in near_spots], axis=0)
    twice = dot(once, matrix[:, 0 : z.rows])
    cols = z.rows
    unit = jnp.concatenate([
        (iota((8, cols), 1) == iota((8, cols), 0) + s * 8).astype(F32) for s in near_spots
    ], axis=0)
    solve = unit + once + twice
    solve_rows[...] = solve
    amplitudes = dot(solve, values)[:, FIRST_LANE : FIRST_LANE + z.cases]
    inverse = local_tile[:, INVERSE_LANE : INVERSE_LANE + 8]
    start = window_start(z, ix) * z.ny
    fields = []
    for f in range(4):
        live = masks[f]
        near_inverse = received[pl.ds(start + near_spots[1 + f], 1)][0][:, INVERSE_LANE : INVERSE_LANE + 8]
        own, near = padded[f] * live, across[f] * live
        rows[f] = jnp.concatenate([dot(inverse, own), dot(near_inverse, near)], axis=0)
        lift_rows[f] = jnp.concatenate([own * SIGNS[f], near * -SIGNS[f]], axis=0)
        fields.append(lifted(z, amplitudes, lift_rows, f))
        multipliers[f] = fields[f]
    image = primal[0, 0] - apply(z, fields, ops, forward, local)
    image = canonical(z, image, backward, product)
    for f in range(4):
        faces[f] = image[f]
    send_faces(z, image, (to0, to1, to2, to3))
    send_coarse(z, image, rows, [], sent, tile)


def jumped(z, masks, faces, got):
    near = across_faces(z, got)
    return [masks[f, 0:1] * SIGNS[f] * (faces[f] - near[f]) for f in range(4)]


def first_direction(
    z, received, got0, got1, got2, got3, faces, masks, ops, forward, backward, solve_rows, rows, lift_rows,
    residual, direction, image, sent, to0, to1, to2, to3,
    local, product, tile,
):
    amplitudes = coarse_amplitudes(z, received, solve_rows)
    field = jumped(z, masks, faces, (got0, got1, got2, got3))
    weights = face_weights(z)
    moved = [field[f] - lifted(z, amplitudes, lift_rows, f) for f in range(4)]
    found = canonical(z, apply(z, moved, ops, forward, local), backward, product)
    for f in range(4):
        residual[f] = field[f]
        direction[f] = moved[f]
        image[f] = found[f]
    gamma = sum(weights[f] * total(field[f] * moved[f]) for f in range(4))
    curvature = sum(SIGNS[f] * total(moved[f] * found[f]) for f in range(4))
    send_faces(z, found, (to0, to1, to2, to3))
    send_coarse(z, found, rows, [gamma, curvature], sent, tile)


def second_direction(
    z, received, got0, got1, got2, got3, faces, masks, ops, forward, backward, solve_rows, lift_rows,
    multipliers, residual, direction,
    next_multipliers, next_residual, projected, image, fresh, sums, sent, to0, to1, to2, to3,
    local, product,
):
    amplitudes = coarse_amplitudes(z, received, solve_rows)
    summed = jnp.sum(received[...], axis=0)
    sums[...] = summed
    alpha = scalar_of(summed, 0) / scalar_of(summed, 1)
    field = jumped(z, masks, faces, (got0, got1, got2, got3))
    weights = face_weights(z)
    left, moved = [], []
    for f in range(4):
        image[f] = field[f]
        next_multipliers[f] = multipliers[f] + alpha * direction[f]
        left.append(residual[f] - alpha * field[f])
        moved.append(direction[f] - alpha * (field[f] - lifted(z, amplitudes, lift_rows, f)))
        next_residual[f] = left[f]
        projected[f] = moved[f]
    found = canonical(z, apply(z, moved, ops, forward, local), backward, product)
    for f in range(4):
        fresh[f] = found[f]
    send_faces(z, found, (to0, to1, to2, to3))
    gamma = sum(weights[f] * total(left[f] * moved[f]) for f in range(4))
    straight = sum(SIGNS[f] * total(moved[f] * found[f]) for f in range(4))
    crossed = sum(
        weights[f] * total(moved[f] * field[f]) + SIGNS[f] * total(direction[f] * found[f]) for f in range(4)
    )
    send_tile(jnp.zeros((8, 128), F32), [gamma, straight, crossed], sent)


def finish(
    z, received, got0, got1, got2, got3, faces, masks, sums, multipliers, residual, direction, projected, image,
    out_multipliers, out_residual,
):
    summed = jnp.sum(received[...], axis=0)
    field = jumped(z, masks, faces, (got0, got1, got2, got3))
    gamma, curvature = scalar_of(sums[...], 0), scalar_of(sums[...], 1)
    fresh, straight, crossed = (scalar_of(summed, i) for i in range(3))
    beta = fresh / gamma
    alpha = fresh / (straight + beta * crossed + beta * beta * curvature)
    for f in range(4):
        step = projected[f] + beta * direction[f]
        out_multipliers[0, 0, f] = (multipliers[f] + alpha * step)[:, 0 : z.face]
        out_residual[0, 0, f] = (residual[f] - alpha * (field[f] + beta * image[f]))[:, 0 : z.face]


def call(z, kernel, outs, args, scratch=(), flops=0):
    shapes = [jax.ShapeDtypeStruct(shape, dtype) for shape, dtype in outs]
    moved = sum(a.size * a.dtype.itemsize for a in args) + sum(s.size * s.dtype.itemsize for s in shapes)
    return pl.pallas_call(
        functools.partial(kernel, z),
        out_shape=shapes,
        in_specs=[pl.BlockSpec(memory_space=SMEM if a.ndim == 3 and a.size == 4 else VMEM) for a in args],
        out_specs=[pl.BlockSpec(memory_space=VMEM) for _ in shapes],
        scratch_shapes=[VMEM(shape, dtype) for shape, dtype in scratch],
        compiler_params=pltpu.CompilerParams(vmem_limit_bytes=40 * 2**20),
        cost_estimate=pl.CostEstimate(flops=flops, bytes_accessed=moved, transcendentals=0),
        name=kernel.__name__,
    )(*args)


def gather(values):
    return lax.all_to_all(values, AXES, 0, 0, tiled=True)


def body(ops, traces, primal, loads, maps, counts):
    z = Sizes(lax.axis_size("gx"), lax.axis_size("gy"), traces, loads)
    field = ((4, z.cases, z.lanes), F32)
    mode_rows = ((4, 8, z.lanes), F32)
    pair_rows = ((4, 16, z.lanes), F32)
    tile = ((8, 128), F32)
    sent = ((z.count, 8, 128), F32)
    to_faces = [((z.cases, z.lanes), F32)] * 4
    padded_rows = ((z.cases, z.padded), F32)
    columns = -(-z.rows // 128) * 128
    product_flops = 2 * z.cases * z.order * z.order

    padded, masks, *trace_faces = call(
        z, prepare, [mode_rows, mode_rows] + [((8, z.lanes), F32)] * 4,
        [jnp.transpose(traces, (0, 1, 3, 2, 4)), counts],
    )
    got = exchange(trace_faces)
    across, local_tile, blocks = call(
        z, couple, [mode_rows, tile, sent],
        [padded, masks, jnp.transpose(loads, (0, 2, 1, 3)), *got],
        [tile, ((8, z.cases), F32)],
    )
    blocks = gather(blocks)
    forward, backward = call(
        z, tables, [((4, z.lanes, z.width), BF16), ((4, z.width, z.lanes), BF16)], [maps],
        [((8, z.padded), jnp.int32)], product_flops,
    )
    solve_rows, rows, lift_rows, multipliers, faces, coarse, *sent_faces = call(
        z, begin,
        [((40, z.rows), F32), pair_rows, pair_rows, field, field, sent] + to_faces,
        [blocks, padded, across, masks, primal, ops, forward, backward, local_tile],
        [((z.rows, columns), F32), padded_rows, padded_rows, tile], product_flops,
    )
    coarse, got = gather(coarse), exchange(sent_faces)
    residual, direction, faces, coarse, *sent_faces = call(
        z, first_direction,
        [field, field, field, sent] + to_faces,
        [coarse, *got, faces, masks, ops, forward, backward, solve_rows, rows, lift_rows],
        [padded_rows, padded_rows, tile], product_flops,
    )
    coarse, got = gather(coarse), exchange(sent_faces)
    multipliers, residual, projected, image, faces, sums, coarse, *sent_faces = call(
        z, second_direction,
        [field, field, field, field, field, tile, sent] + to_faces,
        [coarse, *got, faces, masks, ops, forward, backward, solve_rows, lift_rows,
         multipliers, residual, direction],
        [padded_rows, padded_rows], product_flops,
    )
    coarse, got = gather(coarse), exchange(sent_faces)
    whole = ((1, 1, 4, z.cases, z.face), F32)
    multipliers, residual = call(
        z, finish, [whole, whole],
        [coarse, *got, faces, masks, sums, multipliers, residual, direction, projected, image],
    )
    return multipliers, residual


def solution(mesh):
    in_specs = (
        P("gx", "gy", None, None),
        P("gx", "gy", None, None, None),
        P("gx", "gy", None, None),
        P("gx", "gy", None, None),
        P("gx", "gy", None, None),
        P("gx", "gy", None),
    )
    out_specs = (P("gx", "gy", None, None, None), P("gx", "gy", None, None, None))
    return jax.shard_map(body, mesh=mesh, in_specs=in_specs, out_specs=out_specs, check_vma=False)
```

```python
import functools

import jax
import jax.numpy as jnp
from jax import lax
from jax.experimental import pallas as pl
from jax.experimental.pallas import tpu as pltpu
from jax.sharding import PartitionSpec as P

SIGNS = (-1.0, 1.0, -1.0, 1.0)
HIGHEST = lax.Precision.HIGHEST
AXES = ("gx", "gy")
F32 = jnp.float32
BF16 = jnp.bfloat16
VMEM = pltpu.VMEM
SMEM = pltpu.SMEM
FIRST_LANE = 32
INVERSE_LANE = 48
SCALAR_LANE = 96


class Sizes:
    def __init__(self, nx, ny, traces, loads):
        self.nx, self.ny = nx, ny
        self.count = nx * ny
        self.modes, self.face = traces.shape[-2:]
        self.cases = loads.shape[-1]
        self.order = 4 * self.face
        self.lanes = -(-self.face // 128) * 128
        self.starts = [f * self.face // 128 * 128 for f in range(4)]
        ends = [-(-(f + 1) * self.face // 128) * 128 for f in range(4)]
        self.width = max(e - s for s, e in zip(self.starts, ends))
        self.padded = max(s + self.width for s in self.starts)
        self.wide = min(nx, 9)
        self.rows = self.wide * ny * 8
        self.steps = (-ny, ny, -1, 1)


def dot(a, b, contract=(1, 0), precision=HIGHEST):
    dims = (((contract[0],), (contract[1],)), ((), ()))
    return lax.dot_general(a, b, dims, precision=precision, preferred_element_type=F32)


def iota(shape, dim):
    return lax.broadcasted_iota(jnp.int32, shape, dim)


def place():
    return lax.axis_index("gx"), lax.axis_index("gy")


def window_start(z, ix):
    return jnp.clip(ix - 4, 0, z.nx - z.wide) if z.wide < z.nx else 0


def spots(z, ix, iy):
    own = (ix - window_start(z, ix)) * z.ny + iy
    return [own] + [jnp.clip(own + step, 0, z.wide * z.ny - 1) for step in z.steps]


def send_faces(z, faces, sent):
    for i, at in enumerate(place()):
        even = at % 2 == 0
        low, high = faces[2 * i], faces[2 * i + 1]
        sent[2 * i][...] = jnp.where(even, high, low)
        sent[2 * i + 1][...] = jnp.where(even, low, high)
        sent[2 * i].push()
        sent[2 * i + 1].push()


def across_faces(z, got):
    found = []
    for i, at in enumerate(place()):
        even = at % 2 == 0
        first, second = got[2 * i][...], got[2 * i + 1][...]
        found += [jnp.where(even, second, first), jnp.where(even, first, second)]
    return found


def exchange(sent):
    got = []
    for i, values in enumerate(sent):
        axis = AXES[i // 2]
        pairs = []
        for low in range(i % 2, lax.axis_size(axis) - 1, 2):
            pairs += [(low, low + 1), (low + 1, low)]
        got.append(lax.ppermute(values, axis, pairs))
    return got


def prepare(z, traces, counts, padded, masks, *sent):
    padded[...] = jnp.zeros(padded.shape, F32)
    for f in range(4):
        for j in range(z.modes):
            padded[f, j : j + 1, 0 : z.face] = traces[0, 0, j, f : f + 1]
        live = (iota((8, z.lanes), 1) < counts[0, 0, f]).astype(F32)
        masks[f] = live
    send_faces(z, [padded[f] for f in range(4)], sent)


def tables(z, maps, forward, backward, flat):
    flat[...] = jnp.zeros_like(flat)
    flat[0:4, 0 : z.face] = maps[0, 0]
    lane = iota((1, z.padded), 1)
    line = jnp.full((1, z.padded), -1, jnp.int32)
    for f in range(4):
        moved = pltpu.roll(flat[...], f * z.face, 1)[f : f + 1] if f else flat[0:1]
        line = jnp.where((lane >= f * z.face) & (lane < (f + 1) * z.face), moved, line)
    column = jnp.transpose(jnp.broadcast_to(line, (8, z.padded)))[:, 0:1]
    place_of = iota((z.padded, 1), 0)
    for f in range(4):
        low, high = f * z.face, (f + 1) * z.face
        window = slice(z.starts[f], z.starts[f] + z.width)
        here = jnp.where((lane >= low) & (lane < high), line, -1)[:, window]
        forward[f] = (iota((z.lanes, z.width), 0) == here).astype(F32).astype(BF16)
        there = jnp.where((place_of >= low) & (place_of < high), column, -1)[window]
        backward[f] = (iota((z.width, z.lanes), 1) == there).astype(F32).astype(BF16)


def couple(z, padded, masks, got0, got1, got2, got3, loads, across, local_tile, sent, aug, small):
    near = across_faces(z, (got0, got1, got2, got3))
    live = [padded[f] * masks[f] for f in range(4)]
    diagonal = sum(dot(live[f], padded[f], (1, 1)) for f in range(4))
    row, col = iota((8, 128), 0), iota((8, 128), 1)
    aug[...] = jnp.where((col == row + 8) & (row < z.modes), 1.0, 0.0).astype(F32)
    aug[:, 0:8] = diagonal
    matrix = aug[...]
    for p in range(z.modes):
        scaled = matrix[p : p + 1, :] / matrix[p : p + 1, p : p + 1]
        taken = matrix[:, p : p + 1] - (row[:, 0:1] == p).astype(F32)
        matrix = matrix - taken * scaled
    inverse = matrix[:, 8:16]
    small[...] = jnp.zeros_like(small)
    for j in range(z.modes):
        small[j : j + 1, :] = loads[0, j]
    local_tile[...] = jnp.zeros(local_tile.shape, F32)
    local_tile[:, FIRST_LANE : FIRST_LANE + z.cases] = dot(inverse, small[...])
    local_tile[:, INVERSE_LANE : INVERSE_LANE + 8] = inverse
    for f in range(4):
        across[f] = near[f]
        coupling = dot(live[f], near[f], (1, 1))
        local_tile[:, 8 * f : 8 * f + 8] = dot(inverse, coupling)
    sent[...] = jnp.broadcast_to(local_tile[...][None], sent.shape)
    sent.push()


def lifted(z, amplitudes, lift_rows, f):
    pair = jnp.concatenate([amplitudes[0:8], amplitudes[8 * f + 8 : 8 * f + 16]], axis=0)
    return dot(pair, lift_rows[f], (0, 0))


def apply(z, faces, ops, forward, local):
    local[...] = jnp.zeros_like(local)
    for f in range(4):
        window = slice(z.starts[f], z.starts[f] + z.width)
        signed = (faces[f] * SIGNS[f]).astype(BF16)
        local[:, window] += dot(signed, forward[f], precision=None)
    operand = local[:, 0 : z.order].astype(BF16)
    return dot(operand, ops[0, 0], precision=None)


def canonical(z, values, backward, product):
    product[...] = jnp.zeros_like(product)
    product[:, 0 : z.order] = values
    found = []
    for f in range(4):
        part = product[:, z.starts[f] : z.starts[f] + z.width]
        high = part.astype(BF16)
        low = (part - high.astype(F32)).astype(BF16)
        both = dot(jnp.concatenate([high, low], axis=0), backward[f], precision=None)
        found.append(both[0 : z.cases] + both[z.cases :])
    return found


def send_coarse(z, faces, rows, scalars, sent, tile):
    tile[...] = jnp.zeros_like(tile)
    mine = jnp.zeros((8, z.cases), F32)
    for f in range(4):
        both = dot(rows[f], faces[f], (1, 1))
        mine = mine + both[0:8]
        tile[:, (1 + f) * z.cases : (2 + f) * z.cases] = both[8:16]
    tile[:, 0 : z.cases] = mine
    send_tile(tile[...], scalars, sent)


def send_tile(values, scalars, sent):
    row, col = iota((8, 128), 0), iota((8, 128), 1)
    for i, scalar in enumerate(scalars):
        values = jnp.where((row == 0) & (col == SCALAR_LANE + i), scalar, values)
    sent[...] = jnp.broadcast_to(values[None], sent.shape)
    sent.push()


def scalar_of(total, i):
    row, col = iota((8, 128), 0), iota((8, 128), 1)
    return jnp.sum(jnp.where((row == 0) & (col == SCALAR_LANE + i), total, 0.0), keepdims=True)


def received_window(z, received):
    ix, _ = place()
    start = window_start(z, ix) * z.ny
    return received[pl.ds(start, z.wide * z.ny)].reshape(z.rows, 128)


def coarse_amplitudes(z, received, solve_rows):
    values = received_window(z, received)
    start = values
    for f in range(4):
        across = pltpu.roll(values, 128 - (1 + (f ^ 1)) * z.cases, 1)
        step = 8 * z.steps[f]
        empty = jnp.zeros((abs(step), 128), F32)
        if step > 0:
            moved = jnp.concatenate([across[step:], empty], axis=0)
        else:
            moved = jnp.concatenate([empty, across[: z.rows + step]], axis=0)
        start = start - moved
    return dot(solve_rows[...], start)[:, 0 : z.cases]


def total(values):
    return jnp.sum(values, keepdims=True)


def face_weights(z):
    ix, iy = place()
    edges = (ix == 0, ix == z.nx - 1, iy == 0, iy == z.ny - 1)
    return [jnp.where(edge, 1.0, 0.5).astype(F32) for edge in edges]


def begin(
    z, received, padded, across, masks, local_tile, forward, ops, primal, backward,
    solve_rows, rows, lift_rows, multipliers, faces, sent, to0, to1, to2, to3,
    matrix, local, product, tile,
):
    ix, iy = place()
    near_spots = spots(z, ix, iy)
    values = received_window(z, received)
    lane = iota((z.rows, 128), 1)
    row = iota((z.rows, 128), 0)
    tiled = []
    for f in range(4):
        part = jnp.where(lane // 8 == f, values, 0.0)
        for shift in (64, 32, 16, 8):
            part = part + pltpu.roll(part, shift, 1)
        tiled.append(part)
    for block in range(-(-z.rows // 128)):
        target = (lane + 128 * block) // 8 - row // 8
        part = jnp.zeros((z.rows, 128), F32)
        for f in range(4):
            part = part + jnp.where(target == z.steps[f], tiled[f], 0.0)
        matrix[:, 128 * block : 128 * block + 128] = part
    once = jnp.concatenate([matrix[pl.ds(pl.multiple_of(s * 8, 8), 8), 0 : z.rows] for s in near_spots], axis=0)
    twice = dot(once, matrix[:, 0 : z.rows])
    cols = z.rows
    unit = jnp.concatenate([
        (iota((8, cols), 1) == iota((8, cols), 0) + s * 8).astype(F32) for s in near_spots
    ], axis=0)
    solve = unit + once + twice
    solve_rows[...] = solve
    amplitudes = dot(solve, values)[:, FIRST_LANE : FIRST_LANE + z.cases]
    inverse = local_tile[:, INVERSE_LANE : INVERSE_LANE + 8]
    start = window_start(z, ix) * z.ny
    fields = []
    for f in range(4):
        live = masks[f]
        near_inverse = received[pl.ds(start + near_spots[1 + f], 1)][0][:, INVERSE_LANE : INVERSE_LANE + 8]
        own, near = padded[f] * live, across[f] * live
        rows[f] = jnp.concatenate([dot(inverse, own), dot(near_inverse, near)], axis=0)
        lift_rows[f] = jnp.concatenate([own * SIGNS[f], near * -SIGNS[f]], axis=0)
        fields.append(lifted(z, amplitudes, lift_rows, f))
        multipliers[f] = fields[f]
    for item in (solve_rows, rows, lift_rows, multipliers):
        item.push()
    image = primal[0, 0] - apply(z, fields, ops, forward, local)
    image = canonical(z, image, backward, product)
    for f in range(4):
        faces[f] = image[f]
    faces.push()
    send_faces(z, image, (to0, to1, to2, to3))
    send_coarse(z, image, rows, [], sent, tile)


def jumped(z, masks, faces, got):
    near = across_faces(z, got)
    return [masks[f, 0:1] * SIGNS[f] * (faces[f] - near[f]) for f in range(4)]


def first_direction(
    z, received, got0, got1, got2, got3, faces, masks, solve_rows, lift_rows, forward, ops, backward, rows,
    residual, direction, image, sent, to0, to1, to2, to3,
    local, product, tile,
):
    amplitudes = coarse_amplitudes(z, received, solve_rows)
    field = jumped(z, masks, faces, (got0, got1, got2, got3))
    weights = face_weights(z)
    moved = [field[f] - lifted(z, amplitudes, lift_rows, f) for f in range(4)]
    for f in range(4):
        residual[f] = field[f]
        direction[f] = moved[f]
    residual.push()
    direction.push()
    found = canonical(z, apply(z, moved, ops, forward, local), backward, product)
    for f in range(4):
        image[f] = found[f]
    image.push()
    gamma = sum(weights[f] * total(field[f] * moved[f]) for f in range(4))
    curvature = sum(SIGNS[f] * total(moved[f] * found[f]) for f in range(4))
    send_faces(z, found, (to0, to1, to2, to3))
    send_coarse(z, found, rows, [gamma, curvature], sent, tile)


def second_direction(
    z, received, got0, got1, got2, got3, faces, masks, solve_rows, lift_rows,
    multipliers, residual, direction, forward, ops, backward,
    next_multipliers, next_residual, projected, image, fresh, sums, sent, to0, to1, to2, to3,
    local, product,
):
    amplitudes = coarse_amplitudes(z, received, solve_rows)
    summed = jnp.sum(received[...], axis=0)
    sums[...] = summed
    alpha = scalar_of(summed, 0) / scalar_of(summed, 1)
    field = jumped(z, masks, faces, (got0, got1, got2, got3))
    weights = face_weights(z)
    left, moved = [], []
    for f in range(4):
        image[f] = field[f]
        next_multipliers[f] = multipliers[f] + alpha * direction[f]
        left.append(residual[f] - alpha * field[f])
        moved.append(direction[f] - alpha * (field[f] - lifted(z, amplitudes, lift_rows, f)))
        next_residual[f] = left[f]
        projected[f] = moved[f]
    for item in (sums, image, next_multipliers, next_residual, projected):
        item.push()
    found = canonical(z, apply(z, moved, ops, forward, local), backward, product)
    for f in range(4):
        fresh[f] = found[f]
    fresh.push()
    send_faces(z, found, (to0, to1, to2, to3))
    gamma = sum(weights[f] * total(left[f] * moved[f]) for f in range(4))
    straight = sum(SIGNS[f] * total(moved[f] * found[f]) for f in range(4))
    crossed = sum(
        weights[f] * total(moved[f] * field[f]) + SIGNS[f] * total(direction[f] * found[f]) for f in range(4)
    )
    send_tile(jnp.zeros((8, 128), F32), [gamma, straight, crossed], sent)


def finish(
    z, received, got0, got1, got2, got3, faces, masks, sums, multipliers, residual, direction, projected, image,
    out_multipliers, out_residual,
):
    summed = jnp.sum(received[...], axis=0)
    field = jumped(z, masks, faces, (got0, got1, got2, got3))
    gamma, curvature = scalar_of(sums[...], 0), scalar_of(sums[...], 1)
    fresh, straight, crossed = (scalar_of(summed, i) for i in range(3))
    beta = fresh / gamma
    alpha = fresh / (straight + beta * crossed + beta * beta * curvature)
    for f in range(4):
        step = projected[f] + beta * direction[f]
        out_multipliers[0, 0, f] = (multipliers[f] + alpha * step)[:, 0 : z.face]
        out_residual[0, 0, f] = (residual[f] - alpha * (field[f] + beta * image[f]))[:, 0 : z.face]


class Coming:
    def __init__(self, source, held, semaphore):
        self.held = held
        self.copy = pltpu.make_async_copy(source, held, semaphore)
        self.copy.start()

    def ready(self):
        if self.copy is not None:
            self.copy.wait()
            self.copy = None
        return self.held

    def __getitem__(self, index):
        return self.ready()[index]


class Going:
    def __init__(self, held, target, semaphore):
        self.held = held
        self.copy = pltpu.make_async_copy(held, target, semaphore)
        self.shape, self.dtype = held.shape, held.dtype
        self.started = False

    def __getitem__(self, index):
        return self.held[index]

    def __setitem__(self, index, values):
        self.held[index] = values

    def push(self):
        if not self.started:
            self.copy.start()
            self.started = True


def call(z, kernel, outs, args, scratch=(), flops=0, near=0):
    shapes = [jax.ShapeDtypeStruct(shape, dtype) for shape, dtype in outs]
    moved = sum(a.size * a.dtype.itemsize for a in args) + sum(s.size * s.dtype.itemsize for s in shapes)
    far = len(args) - near

    def run(*refs):
        refs = list(refs)
        take = lambda n: [refs.pop(0) for _ in range(n)]
        sources, others, targets = take(far), take(near), take(len(outs))
        held, made, work, semaphores = take(far), take(len(outs)), take(len(scratch)), refs[0]
        coming = [Coming(a, b, semaphores.at[i]) for i, (a, b) in enumerate(zip(sources, held))]
        going = [Going(a, b, semaphores.at[far + i]) for i, (a, b) in enumerate(zip(made, targets))]
        kernel(z, *coming, *others, *going, *work)
        for item in going:
            item.push()
        for item in coming:
            item.ready()
        for item in going:
            item.copy.wait()

    specs = [pl.BlockSpec(memory_space=pltpu.HBM)] * far
    specs += [pl.BlockSpec(memory_space=SMEM if a.ndim == 3 and a.size == 4 else VMEM) for a in args[far:]]
    buffers = [VMEM(a.shape, a.dtype) for a in args[:far]] + [VMEM(shape, dtype) for shape, dtype in outs]
    return pl.pallas_call(
        run,
        out_shape=shapes,
        in_specs=specs,
        out_specs=[pl.BlockSpec(memory_space=pltpu.HBM) for _ in shapes],
        scratch_shapes=buffers
        + [VMEM(shape, dtype) for shape, dtype in scratch]
        + [pltpu.SemaphoreType.DMA((far + len(outs),))],
        compiler_params=pltpu.CompilerParams(vmem_limit_bytes=32 * 2**20),
        cost_estimate=pl.CostEstimate(flops=flops, bytes_accessed=moved, transcendentals=0),
        name=kernel.__name__,
    )(*args)


def gather(values):
    return lax.all_to_all(values, AXES, 0, 0, tiled=True)


def body(ops, traces, primal, loads, maps, counts):
    z = Sizes(lax.axis_size("gx"), lax.axis_size("gy"), traces, loads)
    field = ((4, z.cases, z.lanes), F32)
    mode_rows = ((4, 8, z.lanes), F32)
    pair_rows = ((4, 16, z.lanes), F32)
    tile = ((8, 128), F32)
    sent = ((z.count, 8, 128), F32)
    to_faces = [((z.cases, z.lanes), F32)] * 4
    padded_rows = ((z.cases, z.padded), F32)
    columns = -(-z.rows // 128) * 128
    product_flops = 2 * z.cases * z.order * z.order

    padded, masks, *trace_faces = call(
        z, prepare, [mode_rows, mode_rows] + [((8, z.lanes), F32)] * 4,
        [jnp.transpose(traces, (0, 1, 3, 2, 4)), counts], near=2,
    )
    got = exchange(trace_faces)
    across, local_tile, blocks = call(
        z, couple, [mode_rows, tile, sent],
        [padded, masks, *got, jnp.transpose(loads, (0, 2, 1, 3))],
        [tile, ((8, z.cases), F32)], near=1,
    )
    blocks = gather(blocks)
    forward, backward = call(
        z, tables, [((4, z.lanes, z.width), BF16), ((4, z.width, z.lanes), BF16)], [maps],
        [((8, z.padded), jnp.int32)], product_flops, near=1,
    )
    solve_rows, rows, lift_rows, multipliers, faces, coarse, *sent_faces = call(
        z, begin,
        [((40, z.rows), F32), pair_rows, pair_rows, field, field, sent] + to_faces,
        [blocks, padded, across, masks, local_tile, forward, ops, primal, backward],
        [((z.rows, columns), F32), padded_rows, padded_rows, tile], product_flops,
    )
    coarse, got = gather(coarse), exchange(sent_faces)
    residual, direction, faces, coarse, *sent_faces = call(
        z, first_direction,
        [field, field, field, sent] + to_faces,
        [coarse, *got, faces, masks, solve_rows, lift_rows, forward, ops, backward, rows],
        [padded_rows, padded_rows, tile], product_flops,
    )
    coarse, got = gather(coarse), exchange(sent_faces)
    multipliers, residual, projected, image, faces, sums, coarse, *sent_faces = call(
        z, second_direction,
        [field, field, field, field, field, tile, sent] + to_faces,
        [coarse, *got, faces, masks, solve_rows, lift_rows,
         multipliers, residual, direction, forward, ops, backward],
        [padded_rows, padded_rows], product_flops,
    )
    coarse, got = gather(coarse), exchange(sent_faces)
    whole = ((1, 1, 4, z.cases, z.face), F32)
    multipliers, residual = call(
        z, finish, [whole, whole],
        [coarse, *got, faces, masks, sums, multipliers, residual, direction, projected, image],
    )
    return multipliers, residual


def solution(mesh):
    in_specs = (
        P("gx", "gy", None, None),
        P("gx", "gy", None, None, None),
        P("gx", "gy", None, None),
        P("gx", "gy", None, None),
        P("gx", "gy", None, None),
        P("gx", "gy", None),
    )
    out_specs = (P("gx", "gy", None, None, None), P("gx", "gy", None, None, None))
    return jax.shard_map(body, mesh=mesh, in_specs=in_specs, out_specs=out_specs, check_vma=False)
```

```python
import functools

import jax
import jax.numpy as jnp
from jax import lax
from jax.experimental import pallas as pl
from jax.experimental.pallas import tpu as pltpu
from jax.sharding import PartitionSpec as P

SIGNS = (-1.0, 1.0, -1.0, 1.0)
HIGHEST = lax.Precision.HIGHEST
AXES = ("gx", "gy")
F32 = jnp.float32
BF16 = jnp.bfloat16
VMEM = pltpu.VMEM
SMEM = pltpu.SMEM
FIRST_LANE = 32
INVERSE_LANE = 48
SCALAR_LANE = 96


class Sizes:
    def __init__(self, nx, ny, traces, loads):
        self.nx, self.ny = nx, ny
        self.count = nx * ny
        self.modes, self.face = traces.shape[-2:]
        self.cases = loads.shape[-1]
        self.order = 4 * self.face
        self.lanes = -(-self.face // 128) * 128
        self.starts = [f * self.face // 128 * 128 for f in range(4)]
        ends = [-(-(f + 1) * self.face // 128) * 128 for f in range(4)]
        self.width = max(e - s for s, e in zip(self.starts, ends))
        self.padded = max(s + self.width for s in self.starts)
        self.wide = min(nx, 9)
        self.rows = self.wide * ny * 8
        self.steps = (-ny, ny, -1, 1)


def dot(a, b, contract=(1, 0), precision=HIGHEST):
    dims = (((contract[0],), (contract[1],)), ((), ()))
    return lax.dot_general(a, b, dims, precision=precision, preferred_element_type=F32)


def iota(shape, dim):
    return lax.broadcasted_iota(jnp.int32, shape, dim)


def place():
    return lax.axis_index("gx"), lax.axis_index("gy")


def window_start(z, ix):
    return jnp.clip(ix - 4, 0, z.nx - z.wide) if z.wide < z.nx else 0


def spots(z, ix, iy):
    own = (ix - window_start(z, ix)) * z.ny + iy
    return [own] + [jnp.clip(own + step, 0, z.wide * z.ny - 1) for step in z.steps]


def send_faces(z, faces, sent):
    for i, at in enumerate(place()):
        even = at % 2 == 0
        low, high = faces[2 * i], faces[2 * i + 1]
        sent[2 * i][...] = jnp.where(even, high, low)
        sent[2 * i + 1][...] = jnp.where(even, low, high)
        sent[2 * i].push()
        sent[2 * i + 1].push()


def across_faces(z, got):
    found = []
    for i, at in enumerate(place()):
        even = at % 2 == 0
        first, second = got[2 * i][...], got[2 * i + 1][...]
        found += [jnp.where(even, second, first), jnp.where(even, first, second)]
    return found


def exchange(sent):
    got = []
    for i, values in enumerate(sent):
        axis = AXES[i // 2]
        pairs = []
        for low in range(i % 2, lax.axis_size(axis) - 1, 2):
            pairs += [(low, low + 1), (low + 1, low)]
        got.append(lax.ppermute(values, axis, pairs))
    return got


def prepare(z, traces, counts, padded, masks, *sent):
    padded[...] = jnp.zeros(padded.shape, F32)
    for f in range(4):
        for j in range(z.modes):
            padded[f, j : j + 1, 0 : z.face] = traces[0, 0, j, f : f + 1]
        live = (iota((8, z.lanes), 1) < counts[0, 0, f]).astype(F32)
        masks[f] = live
    send_faces(z, [padded[f] for f in range(4)], sent)


def arrange(z, ops, primal, maps, arranged, primal_faces, flat, half):
    flat[...] = jnp.zeros_like(flat)
    flat[0:4, 0 : z.face] = maps[0, 0]
    lane = iota((1, z.padded), 1)
    line = jnp.full((1, z.padded), -1, jnp.int32)
    for f in range(4):
        moved = pltpu.roll(flat[...], f * z.face, 1)[f : f + 1] if f else flat[0:1]
        line = jnp.where((lane >= f * z.face) & (lane < (f + 1) * z.face), moved, line)
    column = jnp.transpose(jnp.broadcast_to(line, (8, z.padded)))[:, 0:1]
    place_of = iota((z.padded, 1), 0)
    half[:, z.order :] = jnp.zeros((4 * z.lanes, z.padded - z.order), BF16)
    for f in range(4):
        low, high = f * z.face, (f + 1) * z.face
        size = min(z.width, z.order - z.starts[f])
        here = jnp.where((lane >= low) & (lane < high), line, -1)[:, z.starts[f] : z.starts[f] + size]
        forward = jnp.where(iota((z.lanes, size), 0) == here, SIGNS[f], 0.0).astype(BF16)
        rows = ops[0, 0, z.starts[f] : z.starts[f] + size, :]
        half[f * z.lanes : (f + 1) * z.lanes, 0 : z.order] = dot(forward, rows, precision=None).astype(BF16)
    values = primal[0, 0]
    parts = []
    for _ in range(3):
        parts.append(values.astype(BF16))
        values = values - parts[-1].astype(F32)
    pieces = jnp.concatenate(parts, axis=0)
    for f in range(4):
        low, high = f * z.face, (f + 1) * z.face
        size = min(z.width, z.order - z.starts[f])
        window = slice(z.starts[f], z.starts[f] + z.width)
        there = jnp.where((place_of >= low) & (place_of < high), column, -1)[window]
        backward = (iota((z.width, z.lanes), 1) == there).astype(F32).astype(BF16)
        block = slice(f * z.lanes, (f + 1) * z.lanes)
        arranged[:, block] = dot(half[:, window], backward, precision=None).astype(BF16)
        three = dot(pieces[:, z.starts[f] : z.starts[f] + size], backward[0:size], precision=None)
        n = z.cases
        primal_faces[f] = three[0:n] + (three[n : 2 * n] + three[2 * n :])


def couple(z, padded, masks, got0, got1, got2, got3, loads, across, local_tile, sent, aug, small):
    near = across_faces(z, (got0, got1, got2, got3))
    live = [padded[f] * masks[f] for f in range(4)]
    diagonal = sum(dot(live[f], padded[f], (1, 1)) for f in range(4))
    row, col = iota((8, 128), 0), iota((8, 128), 1)
    aug[...] = jnp.where((col == row + 8) & (row < z.modes), 1.0, 0.0).astype(F32)
    aug[:, 0:8] = diagonal
    matrix = aug[...]
    for p in range(z.modes):
        scaled = matrix[p : p + 1, :] / matrix[p : p + 1, p : p + 1]
        taken = matrix[:, p : p + 1] - (row[:, 0:1] == p).astype(F32)
        matrix = matrix - taken * scaled
    inverse = matrix[:, 8:16]
    small[...] = jnp.zeros_like(small)
    for j in range(z.modes):
        small[j : j + 1, :] = loads[0, j]
    local_tile[...] = jnp.zeros(local_tile.shape, F32)
    local_tile[:, FIRST_LANE : FIRST_LANE + z.cases] = dot(inverse, small[...])
    local_tile[:, INVERSE_LANE : INVERSE_LANE + 8] = inverse
    for f in range(4):
        across[f] = near[f]
        coupling = dot(live[f], near[f], (1, 1))
        local_tile[:, 8 * f : 8 * f + 8] = dot(inverse, coupling)
    sent[...] = jnp.broadcast_to(local_tile[...][None], sent.shape)
    sent.push()


def lifted(z, amplitudes, lift_rows, f):
    pair = jnp.concatenate([amplitudes[0:8], amplitudes[8 * f + 8 : 8 * f + 16]], axis=0)
    return dot(pair, lift_rows[f], (0, 0))


def apply(z, faces, arranged):
    operand = jnp.concatenate([face.astype(BF16) for face in faces], axis=1)
    image = dot(operand, arranged[...], precision=None)
    return [image[:, f * z.lanes : (f + 1) * z.lanes] for f in range(4)]


def send_coarse(z, faces, rows, scalars, sent, tile):
    tile[...] = jnp.zeros_like(tile)
    mine = jnp.zeros((8, z.cases), F32)
    for f in range(4):
        both = dot(rows[f], faces[f], (1, 1))
        mine = mine + both[0:8]
        tile[:, (1 + f) * z.cases : (2 + f) * z.cases] = both[8:16]
    tile[:, 0 : z.cases] = mine
    send_tile(tile[...], scalars, sent)


def send_tile(values, scalars, sent):
    row, col = iota((8, 128), 0), iota((8, 128), 1)
    for i, scalar in enumerate(scalars):
        values = jnp.where((row == 0) & (col == SCALAR_LANE + i), scalar, values)
    sent[...] = jnp.broadcast_to(values[None], sent.shape)
    sent.push()


def scalar_of(total, i):
    row, col = iota((8, 128), 0), iota((8, 128), 1)
    return jnp.sum(jnp.where((row == 0) & (col == SCALAR_LANE + i), total, 0.0), keepdims=True)


def received_window(z, received):
    ix, _ = place()
    start = window_start(z, ix) * z.ny
    return received[pl.ds(start, z.wide * z.ny)].reshape(z.rows, 128)


def coarse_amplitudes(z, received, solve_rows):
    values = received_window(z, received)
    start = values
    for f in range(4):
        across = pltpu.roll(values, 128 - (1 + (f ^ 1)) * z.cases, 1)
        step = 8 * z.steps[f]
        empty = jnp.zeros((abs(step), 128), F32)
        if step > 0:
            moved = jnp.concatenate([across[step:], empty], axis=0)
        else:
            moved = jnp.concatenate([empty, across[: z.rows + step]], axis=0)
        start = start - moved
    return dot(solve_rows[...], start)[:, 0 : z.cases]


def total(values):
    return jnp.sum(values, keepdims=True)


def face_weights(z):
    ix, iy = place()
    edges = (ix == 0, ix == z.nx - 1, iy == 0, iy == z.ny - 1)
    return [jnp.where(edge, 1.0, 0.5).astype(F32) for edge in edges]


def begin(
    z, received, padded, across, masks, local_tile, arranged, primal,
    solve_rows, rows, lift_rows, multipliers, faces, sent, to0, to1, to2, to3,
    matrix, tile,
):
    ix, iy = place()
    near_spots = spots(z, ix, iy)
    values = received_window(z, received)
    lane = iota((z.rows, 128), 1)
    row = iota((z.rows, 128), 0)
    tiled = []
    for f in range(4):
        part = jnp.where(lane // 8 == f, values, 0.0)
        for shift in (64, 32, 16, 8):
            part = part + pltpu.roll(part, shift, 1)
        tiled.append(part)
    for block in range(-(-z.rows // 128)):
        target = (lane + 128 * block) // 8 - row // 8
        part = jnp.zeros((z.rows, 128), F32)
        for f in range(4):
            part = part + jnp.where(target == z.steps[f], tiled[f], 0.0)
        matrix[:, 128 * block : 128 * block + 128] = part
    once = jnp.concatenate([matrix[pl.ds(pl.multiple_of(s * 8, 8), 8), 0 : z.rows] for s in near_spots], axis=0)
    twice = dot(once, matrix[:, 0 : z.rows])
    cols = z.rows
    unit = jnp.concatenate([
        (iota((8, cols), 1) == iota((8, cols), 0) + s * 8).astype(F32) for s in near_spots
    ], axis=0)
    solve = unit + once + twice
    solve_rows[...] = solve
    amplitudes = dot(solve, values)[:, FIRST_LANE : FIRST_LANE + z.cases]
    inverse = local_tile[:, INVERSE_LANE : INVERSE_LANE + 8]
    start = window_start(z, ix) * z.ny
    fields = []
    for f in range(4):
        live = masks[f]
        near_inverse = received[pl.ds(start + near_spots[1 + f], 1)][0][:, INVERSE_LANE : INVERSE_LANE + 8]
        own, near = padded[f] * live, across[f] * live
        rows[f] = jnp.concatenate([dot(inverse, own), dot(near_inverse, near)], axis=0)
        lift_rows[f] = jnp.concatenate([own * SIGNS[f], near * -SIGNS[f]], axis=0)
        fields.append(lifted(z, amplitudes, lift_rows, f))
        multipliers[f] = fields[f]
    for item in (solve_rows, rows, lift_rows, multipliers):
        item.push()
    image = [primal[f] - part for f, part in enumerate(apply(z, fields, arranged))]
    for f in range(4):
        faces[f] = image[f]
    faces.push()
    send_faces(z, image, (to0, to1, to2, to3))
    send_coarse(z, image, rows, [], sent, tile)


def jumped(z, masks, faces, got):
    near = across_faces(z, got)
    return [masks[f, 0:1] * SIGNS[f] * (faces[f] - near[f]) for f in range(4)]


def first_direction(
    z, received, got0, got1, got2, got3, faces, masks, solve_rows, lift_rows, arranged, rows,
    residual, direction, image, sent, to0, to1, to2, to3,
    tile,
):
    amplitudes = coarse_amplitudes(z, received, solve_rows)
    field = jumped(z, masks, faces, (got0, got1, got2, got3))
    weights = face_weights(z)
    moved = [field[f] - lifted(z, amplitudes, lift_rows, f) for f in range(4)]
    for f in range(4):
        residual[f] = field[f]
        direction[f] = moved[f]
    residual.push()
    direction.push()
    found = apply(z, moved, arranged)
    for f in range(4):
        image[f] = found[f]
    image.push()
    gamma = sum(weights[f] * total(field[f] * moved[f]) for f in range(4))
    curvature = sum(SIGNS[f] * total(moved[f] * found[f]) for f in range(4))
    send_faces(z, found, (to0, to1, to2, to3))
    send_coarse(z, found, rows, [gamma, curvature], sent, tile)


def second_direction(
    z, received, got0, got1, got2, got3, faces, masks, solve_rows, lift_rows,
    multipliers, residual, direction, arranged,
    next_multipliers, next_residual, projected, image, fresh, sums, sent, to0, to1, to2, to3,
):
    amplitudes = coarse_amplitudes(z, received, solve_rows)
    summed = jnp.sum(received[...], axis=0)
    sums[...] = summed
    alpha = scalar_of(summed, 0) / scalar_of(summed, 1)
    field = jumped(z, masks, faces, (got0, got1, got2, got3))
    weights = face_weights(z)
    left, moved = [], []
    for f in range(4):
        image[f] = field[f]
        next_multipliers[f] = multipliers[f] + alpha * direction[f]
        left.append(residual[f] - alpha * field[f])
        moved.append(direction[f] - alpha * (field[f] - lifted(z, amplitudes, lift_rows, f)))
        next_residual[f] = left[f]
        projected[f] = moved[f]
    for item in (sums, image, next_multipliers, next_residual, projected):
        item.push()
    found = apply(z, moved, arranged)
    for f in range(4):
        fresh[f] = found[f]
    fresh.push()
    send_faces(z, found, (to0, to1, to2, to3))
    gamma = sum(weights[f] * total(left[f] * moved[f]) for f in range(4))
    straight = sum(SIGNS[f] * total(moved[f] * found[f]) for f in range(4))
    crossed = sum(
        weights[f] * total(moved[f] * field[f]) + SIGNS[f] * total(direction[f] * found[f]) for f in range(4)
    )
    send_tile(jnp.zeros((8, 128), F32), [gamma, straight, crossed], sent)


def finish(
    z, received, got0, got1, got2, got3, faces, masks, sums, multipliers, residual, direction, projected, image,
    out_multipliers, out_residual,
):
    summed = jnp.sum(received[...], axis=0)
    field = jumped(z, masks, faces, (got0, got1, got2, got3))
    gamma, curvature = scalar_of(sums[...], 0), scalar_of(sums[...], 1)
    fresh, straight, crossed = (scalar_of(summed, i) for i in range(3))
    beta = fresh / gamma
    alpha = fresh / (straight + beta * crossed + beta * beta * curvature)
    for f in range(4):
        step = projected[f] + beta * direction[f]
        out_multipliers[0, 0, f] = (multipliers[f] + alpha * step)[:, 0 : z.face]
        out_residual[0, 0, f] = (residual[f] - alpha * (field[f] + beta * image[f]))[:, 0 : z.face]


class Coming:
    def __init__(self, source, held, semaphore):
        self.held = held
        self.copy = pltpu.make_async_copy(source, held, semaphore)
        self.copy.start()

    def ready(self):
        if self.copy is not None:
            self.copy.wait()
            self.copy = None
        return self.held

    def __getitem__(self, index):
        return self.ready()[index]


class Going:
    def __init__(self, held, target, semaphore):
        self.held = held
        self.copy = pltpu.make_async_copy(held, target, semaphore)
        self.shape, self.dtype = held.shape, held.dtype
        self.started = False

    def __getitem__(self, index):
        return self.held[index]

    def __setitem__(self, index, values):
        self.held[index] = values

    def push(self):
        if not self.started:
            self.copy.start()
            self.started = True


def call(z, kernel, outs, args, scratch=(), flops=0, near=0):
    shapes = [jax.ShapeDtypeStruct(shape, dtype) for shape, dtype in outs]
    moved = sum(a.size * a.dtype.itemsize for a in args) + sum(s.size * s.dtype.itemsize for s in shapes)
    far = len(args) - near

    def run(*refs):
        refs = list(refs)
        take = lambda n: [refs.pop(0) for _ in range(n)]
        sources, others, targets = take(far), take(near), take(len(outs))
        held, made, work, semaphores = take(far), take(len(outs)), take(len(scratch)), refs[0]
        coming = [Coming(a, b, semaphores.at[i]) for i, (a, b) in enumerate(zip(sources, held))]
        going = [Going(a, b, semaphores.at[far + i]) for i, (a, b) in enumerate(zip(made, targets))]
        kernel(z, *coming, *others, *going, *work)
        for item in going:
            item.push()
        for item in coming:
            item.ready()
        for item in going:
            item.copy.wait()

    specs = [pl.BlockSpec(memory_space=pltpu.HBM)] * far
    specs += [pl.BlockSpec(memory_space=SMEM if a.ndim == 3 and a.size == 4 else VMEM) for a in args[far:]]
    buffers = [VMEM(a.shape, a.dtype) for a in args[:far]] + [VMEM(shape, dtype) for shape, dtype in outs]
    return pl.pallas_call(
        run,
        out_shape=shapes,
        in_specs=specs,
        out_specs=[pl.BlockSpec(memory_space=pltpu.HBM) for _ in shapes],
        scratch_shapes=buffers
        + [VMEM(shape, dtype) for shape, dtype in scratch]
        + [pltpu.SemaphoreType.DMA((far + len(outs),))],
        compiler_params=pltpu.CompilerParams(vmem_limit_bytes=60 * 2**20),
        cost_estimate=pl.CostEstimate(flops=flops, bytes_accessed=moved, transcendentals=0),
        name=kernel.__name__,
    )(*args)


def gather(values):
    return lax.all_to_all(values, AXES, 0, 0, tiled=True)


def body(ops, traces, primal, loads, maps, counts):
    z = Sizes(lax.axis_size("gx"), lax.axis_size("gy"), traces, loads)
    field = ((4, z.cases, z.lanes), F32)
    mode_rows = ((4, 8, z.lanes), F32)
    pair_rows = ((4, 16, z.lanes), F32)
    tile = ((8, 128), F32)
    sent = ((z.count, 8, 128), F32)
    to_faces = [((z.cases, z.lanes), F32)] * 4
    columns = -(-z.rows // 128) * 128
    product_flops = 2 * z.cases * (4 * z.lanes) ** 2

    padded, masks, *trace_faces = call(
        z, prepare, [mode_rows, mode_rows] + [((8, z.lanes), F32)] * 4,
        [jnp.transpose(traces, (0, 1, 3, 2, 4)), counts], near=2,
    )
    got = exchange(trace_faces)
    across, local_tile, blocks = call(
        z, couple, [mode_rows, tile, sent],
        [padded, masks, *got, jnp.transpose(loads, (0, 2, 1, 3))],
        [tile, ((8, z.cases), F32)], near=1,
    )
    blocks = gather(blocks)
    side = 4 * z.lanes
    arranged, primal_faces = call(
        z, arrange, [((side, side), BF16), field], [ops, primal, maps],
        [((8, z.padded), jnp.int32), ((side, z.padded), BF16)], 2 * side * side * z.width, near=1,
    )
    solve_rows, rows, lift_rows, multipliers, faces, coarse, *sent_faces = call(
        z, begin,
        [((40, z.rows), F32), pair_rows, pair_rows, field, field, sent] + to_faces,
        [blocks, padded, across, masks, local_tile, arranged, primal_faces],
        [((z.rows, columns), F32), tile], product_flops,
    )
    coarse, got = gather(coarse), exchange(sent_faces)
    residual, direction, faces, coarse, *sent_faces = call(
        z, first_direction,
        [field, field, field, sent] + to_faces,
        [coarse, *got, faces, masks, solve_rows, lift_rows, arranged, rows],
        [tile], product_flops,
    )
    coarse, got = gather(coarse), exchange(sent_faces)
    multipliers, residual, projected, image, faces, sums, coarse, *sent_faces = call(
        z, second_direction,
        [field, field, field, field, field, tile, sent] + to_faces,
        [coarse, *got, faces, masks, solve_rows, lift_rows,
         multipliers, residual, direction, arranged],
        [], product_flops,
    )
    coarse, got = gather(coarse), exchange(sent_faces)
    whole = ((1, 1, 4, z.cases, z.face), F32)
    multipliers, residual = call(
        z, finish, [whole, whole],
        [coarse, *got, faces, masks, sums, multipliers, residual, direction, projected, image],
    )
    return multipliers, residual


def solution(mesh):
    in_specs = (
        P("gx", "gy", None, None),
        P("gx", "gy", None, None, None),
        P("gx", "gy", None, None),
        P("gx", "gy", None, None),
        P("gx", "gy", None, None),
        P("gx", "gy", None),
    )
    out_specs = (P("gx", "gy", None, None, None), P("gx", "gy", None, None, None))
    return jax.shard_map(body, mesh=mesh, in_specs=in_specs, out_specs=out_specs, check_vma=False)
```

```python
import functools

import jax
import jax.numpy as jnp
from jax import lax
from jax.experimental import pallas as pl
from jax.experimental.pallas import tpu as pltpu
from jax.sharding import PartitionSpec as P

SIGNS = (-1.0, 1.0, -1.0, 1.0)
HIGHEST = lax.Precision.HIGHEST
AXES = ("gx", "gy")
F32 = jnp.float32
BF16 = jnp.bfloat16
VMEM = pltpu.VMEM
SMEM = pltpu.SMEM
FIRST_LANE = 32
INVERSE_LANE = 48
SCALAR_LANE = 96
BLOCK = 512


class Sizes:
    def __init__(self, nx, ny, traces, loads):
        self.nx, self.ny = nx, ny
        self.count = nx * ny
        self.modes, self.face = traces.shape[-2:]
        self.cases = loads.shape[-1]
        self.order = 4 * self.face
        self.lanes = -(-self.face // 128) * 128
        self.starts = [f * self.face // 128 * 128 for f in range(4)]
        ends = [-(-(f + 1) * self.face // 128) * 128 for f in range(4)]
        self.width = max(e - s for s, e in zip(self.starts, ends))
        self.padded = max(s + self.width for s in self.starts)
        self.wide = min(nx, 9)
        self.rows = self.wide * ny * 8
        self.steps = (-ny, ny, -1, 1)


def dot(a, b, contract=(1, 0), precision=HIGHEST):
    dims = (((contract[0],), (contract[1],)), ((), ()))
    return lax.dot_general(a, b, dims, precision=precision, preferred_element_type=F32)


def iota(shape, dim):
    return lax.broadcasted_iota(jnp.int32, shape, dim)


def place():
    return lax.axis_index("gx"), lax.axis_index("gy")


def window_start(z, ix):
    return jnp.clip(ix - 4, 0, z.nx - z.wide) if z.wide < z.nx else 0


def spots(z, ix, iy):
    own = (ix - window_start(z, ix)) * z.ny + iy
    return [own] + [jnp.clip(own + step, 0, z.wide * z.ny - 1) for step in z.steps]


def send_faces(z, faces, sent):
    for i, at in enumerate(place()):
        even = at % 2 == 0
        low, high = faces[2 * i], faces[2 * i + 1]
        sent[2 * i][...] = jnp.where(even, high, low)
        sent[2 * i + 1][...] = jnp.where(even, low, high)
        sent[2 * i].push()
        sent[2 * i + 1].push()


def across_faces(z, got):
    found = []
    for i, at in enumerate(place()):
        even = at % 2 == 0
        first, second = got[2 * i][...], got[2 * i + 1][...]
        found += [jnp.where(even, second, first), jnp.where(even, first, second)]
    return found


def exchange(sent):
    got = [None] * 4
    for i in (1, 3, 0, 2):
        axis = AXES[i // 2]
        pairs = []
        for low in range(i % 2, lax.axis_size(axis) - 1, 2):
            pairs += [(low, low + 1), (low + 1, low)]
        got[i] = lax.ppermute(sent[i], axis, pairs)
    return got


def prepare(z, traces, counts, padded, masks, *sent):
    padded[...] = jnp.zeros(padded.shape, F32)
    for f in range(4):
        for j in range(z.modes):
            padded[f, j : j + 1, 0 : z.face] = traces[0, 0, j, f : f + 1]
    for i, at in enumerate(place()):
        even = at % 2 == 0
        low, high = padded[2 * i], padded[2 * i + 1]
        sent[2 * i][...] = jnp.where(even, high, low)
        sent[2 * i + 1][...] = jnp.where(even, low, high)
    row, lane = iota(masks.shape, 0), iota(masks.shape, 1)
    live = jnp.zeros(masks.shape, F32)
    for f in range(4):
        live = jnp.where((row == f) & (lane < counts[0, 0, f]), 1.0, live)
    masks[...] = live


def arrange(z, ops, primal, maps, arranged, primal_faces, flat, half):
    flat[...] = jnp.zeros_like(flat)
    flat[0:4, 0 : z.face] = maps[0, 0]
    lane = iota((1, z.padded), 1)
    line = jnp.full((1, z.padded), -1, jnp.int32)
    for f in range(4):
        moved = pltpu.roll(flat[...], f * z.face, 1)[f : f + 1] if f else flat[0:1]
        line = jnp.where((lane >= f * z.face) & (lane < (f + 1) * z.face), moved, line)
    column = jnp.transpose(jnp.broadcast_to(line, (8, z.padded)))[:, 0:1]
    place_of = iota((z.padded, 1), 0)
    half[:, z.order :] = jnp.zeros((4 * z.lanes, z.padded - z.order), BF16)
    for f in range(4):
        low, high = f * z.face, (f + 1) * z.face
        size = min(z.width, z.order - z.starts[f])
        here = jnp.where((lane >= low) & (lane < high), line, -1)[:, z.starts[f] : z.starts[f] + size]
        forward = jnp.where(iota((z.lanes, size), 0) == here, SIGNS[f], 0.0).astype(BF16)
        rows = ops[0, 0, z.starts[f] : z.starts[f] + size, :]
        half[f * z.lanes : (f + 1) * z.lanes, 0 : z.order] = dot(forward, rows, precision=None).astype(BF16)
    values = primal[0, 0]
    parts = []
    for _ in range(3):
        parts.append(values.astype(BF16))
        values = values - parts[-1].astype(F32)
    pieces = jnp.concatenate(parts, axis=0)
    for f in range(4):
        low, high = f * z.face, (f + 1) * z.face
        size = min(z.width, z.order - z.starts[f])
        window = slice(z.starts[f], z.starts[f] + z.width)
        there = jnp.where((place_of >= low) & (place_of < high), column, -1)[window]
        backward = (iota((z.width, z.lanes), 1) == there).astype(F32).astype(BF16)
        block = slice(f * z.lanes, (f + 1) * z.lanes)
        arranged[:, block] = dot(half[:, window], backward, precision=None).astype(BF16)
        arranged.push(f)
        three = dot(pieces[:, z.starts[f] : z.starts[f] + size], backward[0:size], precision=None)
        n = z.cases
        primal_faces[f] = three[0:n] + (three[n : 2 * n] + three[2 * n :])


def invert(z, padded, masks, loads, local_tile, aug, small):
    diagonal = sum(dot(padded[f] * masks[f : f + 1], padded[f], (1, 1)) for f in range(4))
    row, col = iota((8, 128), 0), iota((8, 128), 1)
    aug[...] = jnp.where((col == row + 8) & (row < z.modes), 1.0, 0.0).astype(F32)
    aug[:, 0:8] = diagonal
    matrix = aug[...]
    for p in range(z.modes):
        scaled = matrix[p : p + 1, :] / matrix[p : p + 1, p : p + 1]
        taken = matrix[:, p : p + 1] - (row[:, 0:1] == p).astype(F32)
        matrix = matrix - taken * scaled
    inverse = matrix[:, 8:16]
    small[...] = jnp.zeros(small.shape, F32)
    for j in range(z.modes):
        small[j : j + 1, :] = loads[0, j]
    local_tile[...] = jnp.zeros(local_tile.shape, F32)
    local_tile[:, FIRST_LANE : FIRST_LANE + z.cases] = dot(inverse, small[...])
    local_tile[:, INVERSE_LANE : INVERSE_LANE + 8] = inverse


def couple(z, padded, masks, local_tile, got0, got1, got2, got3, sent, live_rows, lift_rows, tile):
    near = across_faces(z, (got0, got1, got2, got3))
    inverse = local_tile[:, INVERSE_LANE : INVERSE_LANE + 8]
    tile[...] = local_tile[...]
    for f in range(4):
        live = padded[f] * masks[f : f + 1]
        lift_rows[f] = jnp.concatenate([live * SIGNS[f], near[f] * masks[f : f + 1] * -SIGNS[f]], axis=0)
        tile[:, 8 * f : 8 * f + 8] = dot(inverse, dot(live, near[f], (1, 1)))
    sent[...] = jnp.broadcast_to(tile[...][None], sent.shape)
    sent.push()
    live_rows[...] = masks[...]


def lifted(z, amplitudes, lift_rows, f):
    pair = jnp.concatenate([amplitudes[0:8], amplitudes[8 * f + 8 : 8 * f + 16]], axis=0)
    return dot(pair, lift_rows[f], (0, 0))


def apply(z, faces, arranged):
    operand = jnp.concatenate([face.astype(BF16) for face in faces], axis=1)
    image = sum(
        dot(operand[:, low : low + BLOCK], arranged[low : low + BLOCK, :], precision=None)
        for low in range(0, 4 * z.lanes, BLOCK)
    )
    return [image[:, f * z.lanes : (f + 1) * z.lanes] for f in range(4)]


def send_coarse(z, faces, rows, scalars, sent, tile):
    tile[...] = jnp.zeros_like(tile)
    mine = jnp.zeros((8, z.cases), F32)
    for f in range(4):
        both = dot(rows[f], faces[f], (1, 1))
        mine = mine + both[0:8]
        tile[:, (1 + f) * z.cases : (2 + f) * z.cases] = both[8:16]
    tile[:, 0 : z.cases] = mine
    send_tile(tile[...], scalars, sent)


def send_tile(values, scalars, sent):
    row, col = iota((8, 128), 0), iota((8, 128), 1)
    for i, scalar in enumerate(scalars):
        values = jnp.where((row == 0) & (col == SCALAR_LANE + i), scalar, values)
    sent[...] = jnp.broadcast_to(values[None], sent.shape)
    sent.push()


def scalar_of(total, i):
    row, col = iota((8, 128), 0), iota((8, 128), 1)
    return jnp.sum(jnp.where((row == 0) & (col == SCALAR_LANE + i), total, 0.0), keepdims=True)


def received_window(z, received):
    ix, _ = place()
    start = window_start(z, ix) * z.ny
    return received[pl.ds(start, z.wide * z.ny)].reshape(z.rows, 128)


def coarse_amplitudes(z, received, solve_rows):
    values = received_window(z, received)
    start = values
    for f in range(4):
        across = pltpu.roll(values, 128 - (1 + (f ^ 1)) * z.cases, 1)
        step = 8 * z.steps[f]
        empty = jnp.zeros((abs(step), 128), F32)
        if step > 0:
            moved = jnp.concatenate([across[step:], empty], axis=0)
        else:
            moved = jnp.concatenate([empty, across[: z.rows + step]], axis=0)
        start = start - moved
    return dot(solve_rows[...], start)[:, 0 : z.cases]


def total(values):
    return jnp.sum(values, keepdims=True)


def face_weights(z):
    ix, iy = place()
    edges = (ix == 0, ix == z.nx - 1, iy == 0, iy == z.ny - 1)
    return [jnp.where(edge, 1.0, 0.5).astype(F32) for edge in edges]


def begin(
    z, received, lift_rows, primal, arranged,
    solve_rows, rows, multipliers, faces, sent, to0, to1, to2, to3,
    matrix, tile,
):
    ix, iy = place()
    near_spots = spots(z, ix, iy)
    values = received_window(z, received)
    lane = iota((z.rows, 128), 1)
    row = iota((z.rows, 128), 0)
    tiled = []
    for f in range(4):
        part = jnp.where(lane // 8 == f, values, 0.0)
        for shift in (64, 32, 16, 8):
            part = part + pltpu.roll(part, shift, 1)
        tiled.append(part)
    for block in range(-(-z.rows // 128)):
        target = (lane + 128 * block) // 8 - row // 8
        part = jnp.zeros((z.rows, 128), F32)
        for f in range(4):
            part = part + jnp.where(target == z.steps[f], tiled[f], 0.0)
        matrix[:, 128 * block : 128 * block + 128] = part
    once = jnp.concatenate([matrix[pl.ds(pl.multiple_of(s * 8, 8), 8), 0 : z.rows] for s in near_spots], axis=0)
    twice = dot(once, matrix[:, 0 : z.rows])
    cols = z.rows
    unit = jnp.concatenate([
        (iota((8, cols), 1) == iota((8, cols), 0) + s * 8).astype(F32) for s in near_spots
    ], axis=0)
    solve = unit + once + twice
    solve_rows[...] = solve
    amplitudes = dot(solve, values)[:, FIRST_LANE : FIRST_LANE + z.cases]
    start = window_start(z, ix) * z.ny
    inverses = [received[pl.ds(start + spot, 1)][0][:, INVERSE_LANE : INVERSE_LANE + 8] for spot in near_spots]
    fields = []
    for f in range(4):
        both = lift_rows[f]
        own, near = both[0:8] * SIGNS[f], both[8:16] * -SIGNS[f]
        rows[f] = jnp.concatenate([dot(inverses[0], own), dot(inverses[1 + f], near)], axis=0)
        fields.append(lifted(z, amplitudes, lift_rows, f))
        multipliers[f] = fields[f]
    for item in (solve_rows, rows, multipliers):
        item.push()
    image = [primal[f] - part for f, part in enumerate(apply(z, fields, arranged))]
    for f in range(4):
        faces[f] = image[f]
    faces.push()
    send_faces(z, image, (to0, to1, to2, to3))
    send_coarse(z, image, rows, [], sent, tile)


def jumped(z, masks, faces, got):
    near = across_faces(z, got)
    return [masks[f : f + 1] * SIGNS[f] * (faces[f] - near[f]) for f in range(4)]


def first_direction(
    z, received, solve_rows, lift_rows, faces, masks, rows, arranged, got0, got1, got2, got3,
    residual, direction, image, sent, to0, to1, to2, to3,
    tile,
):
    amplitudes = coarse_amplitudes(z, received, solve_rows)
    field = jumped(z, masks, faces, (got0, got1, got2, got3))
    weights = face_weights(z)
    moved = [field[f] - lifted(z, amplitudes, lift_rows, f) for f in range(4)]
    for f in range(4):
        residual[f] = field[f]
        direction[f] = moved[f]
    residual.push()
    direction.push()
    found = apply(z, moved, arranged)
    for f in range(4):
        image[f] = found[f]
    image.push()
    gamma = sum(weights[f] * total(field[f] * moved[f]) for f in range(4))
    curvature = sum(SIGNS[f] * total(moved[f] * found[f]) for f in range(4))
    send_faces(z, found, (to0, to1, to2, to3))
    send_coarse(z, found, rows, [gamma, curvature], sent, tile)


def second_direction(
    z, received, solve_rows, lift_rows, faces, masks, residual, direction, multipliers, arranged,
    got0, got1, got2, got3,
    next_multipliers, next_residual, projected, image, fresh, sums, sent, to0, to1, to2, to3,
):
    amplitudes = coarse_amplitudes(z, received, solve_rows)
    summed = jnp.sum(received[...], axis=0)
    sums[...] = summed
    alpha = scalar_of(summed, 0) / scalar_of(summed, 1)
    field = jumped(z, masks, faces, (got0, got1, got2, got3))
    weights = face_weights(z)
    left, moved = [], []
    for f in range(4):
        image[f] = field[f]
        next_multipliers[f] = multipliers[f] + alpha * direction[f]
        left.append(residual[f] - alpha * field[f])
        moved.append(direction[f] - alpha * (field[f] - lifted(z, amplitudes, lift_rows, f)))
        next_residual[f] = left[f]
        projected[f] = moved[f]
    for item in (sums, image, next_multipliers, next_residual, projected):
        item.push()
    found = apply(z, moved, arranged)
    for f in range(4):
        fresh[f] = found[f]
    fresh.push()
    send_faces(z, found, (to0, to1, to2, to3))
    gamma = sum(weights[f] * total(left[f] * moved[f]) for f in range(4))
    straight = sum(SIGNS[f] * total(moved[f] * found[f]) for f in range(4))
    crossed = sum(
        weights[f] * total(moved[f] * field[f]) + SIGNS[f] * total(direction[f] * found[f]) for f in range(4)
    )
    send_tile(jnp.zeros((8, 128), F32), [gamma, straight, crossed], sent)


def finish(
    z, received, sums, faces, masks, residual, image, multipliers, projected, direction,
    got0, got1, got2, got3,
    out_multipliers, out_residual,
):
    summed = jnp.sum(received[...], axis=0)
    field = jumped(z, masks, faces, (got0, got1, got2, got3))
    gamma, curvature = scalar_of(sums[...], 0), scalar_of(sums[...], 1)
    fresh, straight, crossed = (scalar_of(summed, i) for i in range(3))
    beta = fresh / gamma
    alpha = fresh / (straight + beta * crossed + beta * beta * curvature)
    for f in range(4):
        step = projected[f] + beta * direction[f]
        out_multipliers[0, 0, f] = (multipliers[f] + alpha * step)[:, 0 : z.face]
        out_residual[0, 0, f] = (residual[f] - alpha * (field[f] + beta * image[f]))[:, 0 : z.face]


class Coming:
    def __init__(self, source, held, semaphores):
        self.held = held
        size = len(semaphores)
        step = -(-held.shape[0] // size) if size > 1 else 0
        self.copies = []
        for i, semaphore in enumerate(semaphores):
            part = pl.ds(i * step, step)
            pair = (source, held) if size == 1 else (source.at[part], held.at[part])
            self.copies.append(pltpu.make_async_copy(*pair, semaphore))
            self.copies[-1].start()
        self.step = step

    def ready(self, only=None):
        for i, copy in enumerate(self.copies):
            if copy is not None and only in (None, i):
                copy.wait()
                self.copies[i] = None
        return self.held

    def __getitem__(self, index):
        return self.ready(index[0].start // self.step if self.step else None)[index]


class Going:
    def __init__(self, held, target, semaphores):
        self.held = held
        self.shape, self.dtype = held.shape, held.dtype
        size = len(semaphores)
        self.copies = []
        for i, semaphore in enumerate(semaphores):
            step = held.shape[-1] // size
            part = (slice(None), pl.ds(i * step, step))
            pair = (held, target) if size == 1 else (held.at[part], target.at[part])
            self.copies.append(pltpu.make_async_copy(*pair, semaphore))
        self.started = [False] * size

    def __getitem__(self, index):
        return self.held[index]

    def __setitem__(self, index, values):
        self.held[index] = values

    def push(self, only=None):
        for i, copy in enumerate(self.copies):
            if not self.started[i] and only in (None, i):
                copy.start()
                self.started[i] = True


def call(z, kernel, outs, args, scratch=(), flops=0, near=0, kept=0):
    shapes = [jax.ShapeDtypeStruct(shape, dtype) for shape, dtype in outs]
    moved = sum(a.size * a.dtype.itemsize for a in args) + sum(s.size * s.dtype.itemsize for s in shapes)
    far, sent = len(args) - near, len(outs) - kept
    large = (4 * z.lanes, 4 * z.lanes)
    parts_in = [large[0] // BLOCK if a.shape == large else 1 for a in args[:far]]
    parts_out = [4 if a.shape == large else 1 for a in shapes[:sent]]

    def run(*refs):
        refs = list(refs)
        take = lambda n: [refs.pop(0) for _ in range(n)]
        sources, others, targets, direct = take(far), take(near), take(sent), take(kept)
        held, made, work = take(far), take(sent), take(len(scratch))
        flags = [refs[0].at[i] for i in range(sum(parts_in) + sum(parts_out))] if refs else []
        some = lambda n: [flags.pop(0) for _ in range(n)]
        coming = [Coming(a, b, some(n)) for a, b, n in zip(sources, held, parts_in)]
        going = [Going(a, b, some(n)) for a, b, n in zip(made, targets, parts_out)]
        kernel(z, *coming, *others, *going, *direct, *work)
        for item in going:
            item.push()
        for item in coming:
            item.ready()
        for item in going:
            for copy in item.copies:
                copy.wait()

    near_spec = lambda a: pl.BlockSpec(memory_space=SMEM if a.ndim == 3 and a.size == 4 else VMEM)
    far_spec = pl.BlockSpec(memory_space=pltpu.HBM)
    buffers = [VMEM(a.shape, a.dtype) for a in list(args[:far]) + shapes[:sent]]
    semaphores = [pltpu.SemaphoreType.DMA((sum(parts_in) + sum(parts_out),))] if far + sent else []
    return pl.pallas_call(
        run,
        out_shape=shapes,
        in_specs=[far_spec] * far + [near_spec(a) for a in args[far:]],
        out_specs=[far_spec] * sent + [near_spec(a) for a in shapes[sent:]],
        scratch_shapes=buffers + [VMEM(shape, dtype) for shape, dtype in scratch] + semaphores,
        compiler_params=pltpu.CompilerParams(vmem_limit_bytes=60 * 2**20),
        cost_estimate=pl.CostEstimate(flops=flops, bytes_accessed=moved, transcendentals=0),
        name=kernel.__name__,
    )(*args)


def gather(values):
    return lax.all_to_all(values, AXES, 0, 0, tiled=True)


def body(ops, traces, primal, loads, maps, counts):
    z = Sizes(lax.axis_size("gx"), lax.axis_size("gy"), traces, loads)
    field = ((4, z.cases, z.lanes), F32)
    mode_rows = ((4, 8, z.lanes), F32)
    pair_rows = ((4, 16, z.lanes), F32)
    live_rows = ((8, z.lanes), F32)
    tile = ((8, 128), F32)
    sent = ((z.count, 8, 128), F32)
    to_faces = [((z.cases, z.lanes), F32)] * 4
    columns = -(-z.rows // 128) * 128
    product_flops = 2 * z.cases * (4 * z.lanes) ** 2

    padded, masks, *trace_faces = call(
        z, prepare, [mode_rows, live_rows] + [((8, z.lanes), F32)] * 4,
        [jnp.transpose(traces, (0, 1, 3, 2, 4)), counts], near=2, kept=6,
    )
    got = exchange(trace_faces)
    (local_tile,) = call(
        z, invert, [tile], [padded, masks, jnp.transpose(loads, (0, 2, 1, 3))],
        [tile, ((8, z.cases), F32)], product_flops, near=3, kept=1,
    )
    blocks, masks, lift_rows = call(
        z, couple, [sent, live_rows, pair_rows], [padded, masks, local_tile, *got], [tile], near=7,
    )
    blocks = gather(blocks)
    side = 4 * z.lanes
    arranged, primal_faces = call(
        z, arrange, [((side, side), BF16), field], [ops, primal, maps],
        [((8, z.padded), jnp.int32), ((side, z.padded), BF16)], 2 * side * side * z.width, near=1,
    )
    solve_rows, rows, multipliers, faces, coarse, *sent_faces = call(
        z, begin, [((40, z.rows), F32), pair_rows, field, field, sent] + to_faces,
        [blocks, lift_rows, primal_faces, arranged],
        [((z.rows, columns), F32), tile], product_flops,
    )
    coarse, got = gather(coarse), exchange(sent_faces)
    residual, direction, faces, coarse, *sent_faces = call(
        z, first_direction, [field, field, field, sent] + to_faces,
        [coarse, solve_rows, lift_rows, faces, masks, rows, arranged, *got],
        [tile], product_flops, near=4,
    )
    coarse, got = gather(coarse), exchange(sent_faces)
    multipliers, residual, projected, image, faces, sums, coarse, *sent_faces = call(
        z, second_direction, [field, field, field, field, field, tile, sent] + to_faces,
        [coarse, solve_rows, lift_rows, faces, masks, residual, direction, multipliers, arranged, *got],
        [], product_flops, near=4,
    )
    coarse, got = gather(coarse), exchange(sent_faces)
    whole = ((1, 1, 4, z.cases, z.face), F32)
    multipliers, residual = call(
        z, finish, [whole, whole],
        [coarse, sums, faces, masks, residual, image, multipliers, projected, direction, *got], near=4,
    )
    return multipliers, residual


def solution(mesh):
    in_specs = (
        P("gx", "gy", None, None),
        P("gx", "gy", None, None, None),
        P("gx", "gy", None, None),
        P("gx", "gy", None, None),
        P("gx", "gy", None, None),
        P("gx", "gy", None),
    )
    out_specs = (P("gx", "gy", None, None, None), P("gx", "gy", None, None, None))
    return jax.shard_map(body, mesh=mesh, in_specs=in_specs, out_specs=out_specs, check_vma=False)
```

```python
import functools

import jax
import jax.numpy as jnp
from jax import lax
from jax.experimental import pallas as pl
from jax.experimental.pallas import tpu as pltpu
from jax.sharding import PartitionSpec as P

SIGNS = (-1.0, 1.0, -1.0, 1.0)
HIGHEST = lax.Precision.HIGHEST
AXES = ("gx", "gy")
F32 = jnp.float32
BF16 = jnp.bfloat16
VMEM = pltpu.VMEM
SMEM = pltpu.SMEM
FIRST_LANE = 32
INVERSE_LANE = 48
SCALAR_LANE = 96
BLOCK = 256


class Sizes:
    def __init__(self, nx, ny, traces, loads):
        self.nx, self.ny = nx, ny
        self.count = nx * ny
        self.modes, self.face = traces.shape[-2:]
        self.cases = loads.shape[-1]
        self.order = 4 * self.face
        self.lanes = -(-self.face // 128) * 128
        self.starts = [f * self.face // 128 * 128 for f in range(4)]
        ends = [-(-(f + 1) * self.face // 128) * 128 for f in range(4)]
        self.width = max(e - s for s, e in zip(self.starts, ends))
        self.padded = max(s + self.width for s in self.starts)
        self.wide = min(nx, 9)
        self.rows = self.wide * ny * 8
        self.steps = (-ny, ny, -1, 1)


def dot(a, b, contract=(1, 0), precision=HIGHEST):
    dims = (((contract[0],), (contract[1],)), ((), ()))
    return lax.dot_general(a, b, dims, precision=precision, preferred_element_type=F32)


def iota(shape, dim):
    return lax.broadcasted_iota(jnp.int32, shape, dim)


def place():
    return lax.axis_index("gx"), lax.axis_index("gy")


def window_start(z, ix):
    return jnp.clip(ix - 4, 0, z.nx - z.wide) if z.wide < z.nx else 0


def spots(z, ix, iy):
    own = (ix - window_start(z, ix)) * z.ny + iy
    return [own] + [jnp.clip(own + step, 0, z.wide * z.ny - 1) for step in z.steps]


def send_faces(z, faces, sent):
    for i, at in enumerate(place()):
        even = at % 2 == 0
        low, high = faces[2 * i], faces[2 * i + 1]
        sent[2 * i][...] = jnp.where(even, high, low)
        sent[2 * i + 1][...] = jnp.where(even, low, high)
        sent[2 * i].push()
        sent[2 * i + 1].push()


def across_faces(z, got):
    found = []
    for i, at in enumerate(place()):
        even = at % 2 == 0
        first, second = got[2 * i][...], got[2 * i + 1][...]
        found += [jnp.where(even, second, first), jnp.where(even, first, second)]
    return found


def exchange(sent):
    got = [None] * 4
    for i in (1, 3, 0, 2):
        axis = AXES[i // 2]
        pairs = []
        for low in range(i % 2, lax.axis_size(axis) - 1, 2):
            pairs += [(low, low + 1), (low + 1, low)]
        got[i] = lax.ppermute(sent[i], axis, pairs)
    return got


def prepare(z, traces, counts, padded, masks, *sent):
    padded[...] = jnp.zeros(padded.shape, F32)
    for f in range(4):
        for j in range(z.modes):
            padded[f, j : j + 1, 0 : z.face] = traces[0, 0, j, f : f + 1]
    for i, at in enumerate(place()):
        even = at % 2 == 0
        low, high = padded[2 * i], padded[2 * i + 1]
        sent[2 * i][...] = jnp.where(even, high, low)
        sent[2 * i + 1][...] = jnp.where(even, low, high)
    row, lane = iota(masks.shape, 0), iota(masks.shape, 1)
    live = jnp.zeros(masks.shape, F32)
    for f in range(4):
        live = jnp.where((row == f) & (lane < counts[0, 0, f]), 1.0, live)
    masks[...] = live


def blocks_of(z):
    found = []
    for low in range(0, z.order, BLOCK):
        high = min(low + BLOCK, z.order)
        first, last = low // z.face, (high - 1) // z.face
        found.append((low, high, first * z.face // 128 * 128, min(-(-(last + 1) * z.face // 128) * 128, z.order)))
    return found


def arrange(z, ops, primal, maps, primal_packed, arranged, flat, half):
    flat[...] = jnp.zeros_like(flat)
    flat[0:4, 0 : z.face] = maps[0, 0]
    lane = iota((1, z.padded), 1)
    line = jnp.full((1, z.padded), -1, jnp.int32)
    signs = jnp.zeros((1, z.padded), F32)
    for f in range(4):
        moved = pltpu.roll(flat[...], f * z.face, 1)[f : f + 1] if f else flat[0:1]
        here = (lane >= f * z.face) & (lane < (f + 1) * z.face)
        line = jnp.where(here, moved + f * z.face, line)
        signs = jnp.where(here, SIGNS[f], signs)
    column = jnp.transpose(jnp.broadcast_to(line, (8, z.padded)))[:, 0:1]
    spread = []
    for low, high, first, last in blocks_of(z):
        hit = (iota((last - first, high - low), 1) + low) == column[first:last]
        spread.append(hit.astype(F32).astype(BF16))
    for low, high, first, last in blocks_of(z):
        hit = (iota((high - low, last - first), 0) + low) == line[:, first:last]
        collect = jnp.where(hit, signs[:, first:last], 0.0).astype(BF16)
        half[low:high, :] = dot(collect, ops[0, 0, first:last, :], precision=None).astype(BF16)
    values = primal[0, 0]
    parts = []
    for _ in range(3):
        parts.append(values.astype(BF16))
        values = values - parts[-1].astype(F32)
    pieces = jnp.concatenate(parts, axis=0)
    n = z.cases
    for (low, high, first, last), there in zip(blocks_of(z), spread):
        three = dot(pieces[:, first:last], there, precision=None)
        primal_packed[:, low:high] = three[0:n] + (three[n : 2 * n] + three[2 * n :])
    primal_packed.push()
    for (low, high, first, last), there in zip(blocks_of(z), spread):
        arranged[:, low:high] = dot(half[:, first:last], there, precision=None).astype(BF16)


def invert(z, padded, masks, loads, local_tile, aug, small):
    diagonal = sum(dot(padded[f] * masks[f : f + 1], padded[f], (1, 1)) for f in range(4))
    row, col = iota((8, 128), 0), iota((8, 128), 1)
    aug[...] = jnp.where((col == row + 8) & (row < z.modes), 1.0, 0.0).astype(F32)
    aug[:, 0:8] = diagonal
    matrix = aug[...]
    for p in range(z.modes):
        scaled = matrix[p : p + 1, :] / matrix[p : p + 1, p : p + 1]
        taken = matrix[:, p : p + 1] - (row[:, 0:1] == p).astype(F32)
        matrix = matrix - taken * scaled
    inverse = matrix[:, 8:16]
    small[...] = jnp.zeros(small.shape, F32)
    for j in range(z.modes):
        small[j : j + 1, :] = loads[0, j]
    local_tile[...] = jnp.zeros(local_tile.shape, F32)
    local_tile[:, FIRST_LANE : FIRST_LANE + z.cases] = dot(inverse, small[...])
    local_tile[:, INVERSE_LANE : INVERSE_LANE + 8] = inverse


def couple(z, padded, masks, local_tile, got0, got1, got2, got3, sent, live_rows, lift_rows, tile):
    near = across_faces(z, (got0, got1, got2, got3))
    inverse = local_tile[:, INVERSE_LANE : INVERSE_LANE + 8]
    tile[...] = local_tile[...]
    for f in range(4):
        live = padded[f] * masks[f : f + 1]
        lift_rows[f] = jnp.concatenate([live * SIGNS[f], near[f] * masks[f : f + 1] * -SIGNS[f]], axis=0)
        tile[:, 8 * f : 8 * f + 8] = dot(inverse, dot(live, near[f], (1, 1)))
    sent[...] = jnp.broadcast_to(tile[...][None], sent.shape)
    sent.push()
    live_rows[...] = masks[...]


def lifted(z, amplitudes, lift_rows, f):
    pair = jnp.concatenate([amplitudes[0:8], amplitudes[8 * f + 8 : 8 * f + 16]], axis=0)
    return dot(pair, lift_rows[f], (0, 0))


def apply(z, faces, arranged, packed):
    packed[...] = jnp.zeros(packed.shape, F32)
    for f in range(4):
        wide = jnp.concatenate([faces[f], jnp.zeros((z.cases, z.width - z.lanes), F32)], axis=1)
        shift = f * z.face - z.starts[f]
        packed[:, z.starts[f] : z.starts[f] + z.width] += pltpu.roll(wide, shift, 1) if shift else wide
    return dot(packed[:, 0 : z.order].astype(BF16), arranged[...], precision=None)


def unpacked(z, values, packed):
    packed[:, 0 : z.order] = values
    found = []
    for f in range(4):
        part = packed[:, z.starts[f] : z.starts[f] + z.width]
        shift = f * z.face - z.starts[f]
        part = (pltpu.roll(part, z.width - shift, 1) if shift else part)[:, 0 : z.lanes]
        found.append(jnp.where(iota(part.shape, 1) < z.face, part, 0.0))
    return found


def send_coarse(z, faces, rows, scalars, sent, tile):
    tile[...] = jnp.zeros_like(tile)
    mine = jnp.zeros((8, z.cases), F32)
    for f in range(4):
        both = dot(rows[f], faces[f], (1, 1))
        mine = mine + both[0:8]
        tile[:, (1 + f) * z.cases : (2 + f) * z.cases] = both[8:16]
    tile[:, 0 : z.cases] = mine
    send_tile(tile[...], scalars, sent)


def send_tile(values, scalars, sent):
    row, col = iota((8, 128), 0), iota((8, 128), 1)
    for i, scalar in enumerate(scalars):
        values = jnp.where((row == 0) & (col == SCALAR_LANE + i), scalar, values)
    sent[...] = jnp.broadcast_to(values[None], sent.shape)
    sent.push()


def scalar_of(total, i):
    row, col = iota((8, 128), 0), iota((8, 128), 1)
    return jnp.sum(jnp.where((row == 0) & (col == SCALAR_LANE + i), total, 0.0), keepdims=True)


def received_window(z, received):
    ix, _ = place()
    start = window_start(z, ix) * z.ny
    return received[pl.ds(start, z.wide * z.ny)].reshape(z.rows, 128)


def coarse_amplitudes(z, received, solve_rows):
    values = received_window(z, received)
    start = values
    for f in range(4):
        across = pltpu.roll(values, 128 - (1 + (f ^ 1)) * z.cases, 1)
        step = 8 * z.steps[f]
        empty = jnp.zeros((abs(step), 128), F32)
        if step > 0:
            moved = jnp.concatenate([across[step:], empty], axis=0)
        else:
            moved = jnp.concatenate([empty, across[: z.rows + step]], axis=0)
        start = start - moved
    return dot(solve_rows[...], start)[:, 0 : z.cases]


def total(values):
    return jnp.sum(values, keepdims=True)


def face_weights(z):
    ix, iy = place()
    edges = (ix == 0, ix == z.nx - 1, iy == 0, iy == z.ny - 1)
    return [jnp.where(edge, 1.0, 0.5).astype(F32) for edge in edges]


def begin(
    z, lift_rows, primal, received, arranged,
    solve_rows, rows, multipliers, faces, sent, to0, to1, to2, to3,
    matrix, tile, packed,
):
    ix, iy = place()
    near_spots = spots(z, ix, iy)
    values = received_window(z, received)
    lane = iota((z.rows, 128), 1)
    row = iota((z.rows, 128), 0)
    tiled = []
    for f in range(4):
        part = jnp.where(lane // 8 == f, values, 0.0)
        for shift in (64, 32, 16, 8):
            part = part + pltpu.roll(part, shift, 1)
        tiled.append(part)
    for block in range(-(-z.rows // 128)):
        target = (lane + 128 * block) // 8 - row // 8
        part = jnp.zeros((z.rows, 128), F32)
        for f in range(4):
            part = part + jnp.where(target == z.steps[f], tiled[f], 0.0)
        matrix[:, 128 * block : 128 * block + 128] = part
    once = jnp.concatenate([matrix[pl.ds(pl.multiple_of(s * 8, 8), 8), 0 : z.rows] for s in near_spots], axis=0)
    twice = dot(once, matrix[:, 0 : z.rows])
    cols = z.rows
    unit = jnp.concatenate([
        (iota((8, cols), 1) == iota((8, cols), 0) + s * 8).astype(F32) for s in near_spots
    ], axis=0)
    solve = unit + once + twice
    solve_rows[...] = solve
    amplitudes = dot(solve, values)[:, FIRST_LANE : FIRST_LANE + z.cases]
    start = window_start(z, ix) * z.ny
    inverses = [received[pl.ds(start + spot, 1)][0][:, INVERSE_LANE : INVERSE_LANE + 8] for spot in near_spots]
    fields = []
    for f in range(4):
        both = lift_rows[f]
        own, near = both[0:8] * SIGNS[f], both[8:16] * -SIGNS[f]
        rows[f] = jnp.concatenate([dot(inverses[0], own), dot(inverses[1 + f], near)], axis=0)
        fields.append(lifted(z, amplitudes, lift_rows, f))
        multipliers[f] = fields[f]
    for item in (solve_rows, rows, multipliers):
        item.push()
    image = unpacked(z, primal[...] - apply(z, fields, arranged, packed), packed)
    for f in range(4):
        faces[f] = image[f]
    faces.push()
    send_faces(z, image, (to0, to1, to2, to3))
    send_coarse(z, image, rows, [], sent, tile)


def jumped(z, masks, faces, got):
    near = across_faces(z, got)
    return [masks[f : f + 1] * SIGNS[f] * (faces[f] - near[f]) for f in range(4)]


def first_direction(
    z, solve_rows, lift_rows, faces, masks, rows, got0, got1, got2, got3, received, arranged,
    residual, direction, image, sent, to0, to1, to2, to3,
    tile, packed,
):
    amplitudes = coarse_amplitudes(z, received, solve_rows)
    field = jumped(z, masks, faces, (got0, got1, got2, got3))
    weights = face_weights(z)
    moved = [field[f] - lifted(z, amplitudes, lift_rows, f) for f in range(4)]
    for f in range(4):
        residual[f] = field[f]
        direction[f] = moved[f]
    residual.push()
    direction.push()
    found = unpacked(z, apply(z, moved, arranged, packed), packed)
    for f in range(4):
        image[f] = found[f]
    image.push()
    gamma = sum(weights[f] * total(field[f] * moved[f]) for f in range(4))
    curvature = sum(SIGNS[f] * total(moved[f] * found[f]) for f in range(4))
    send_faces(z, found, (to0, to1, to2, to3))
    send_coarse(z, found, rows, [gamma, curvature], sent, tile)


def second_direction(
    z, solve_rows, lift_rows, faces, masks, residual, direction, multipliers,
    got0, got1, got2, got3, received, arranged,
    next_multipliers, next_residual, projected, image, fresh, sums, sent, to0, to1, to2, to3,
    packed,
):
    amplitudes = coarse_amplitudes(z, received, solve_rows)
    summed = jnp.sum(received[...], axis=0)
    sums[...] = summed
    alpha = scalar_of(summed, 0) / scalar_of(summed, 1)
    field = jumped(z, masks, faces, (got0, got1, got2, got3))
    weights = face_weights(z)
    left, moved = [], []
    for f in range(4):
        image[f] = field[f]
        next_multipliers[f] = multipliers[f] + alpha * direction[f]
        left.append(residual[f] - alpha * field[f])
        moved.append(direction[f] - alpha * (field[f] - lifted(z, amplitudes, lift_rows, f)))
        next_residual[f] = left[f]
        projected[f] = moved[f]
    for item in (sums, image, next_multipliers, next_residual, projected):
        item.push()
    found = unpacked(z, apply(z, moved, arranged, packed), packed)
    for f in range(4):
        fresh[f] = found[f]
    fresh.push()
    send_faces(z, found, (to0, to1, to2, to3))
    gamma = sum(weights[f] * total(left[f] * moved[f]) for f in range(4))
    straight = sum(SIGNS[f] * total(moved[f] * found[f]) for f in range(4))
    crossed = sum(
        weights[f] * total(moved[f] * field[f]) + SIGNS[f] * total(direction[f] * found[f]) for f in range(4)
    )
    send_tile(jnp.zeros((8, 128), F32), [gamma, straight, crossed], sent)


def finish(
    z, sums, faces, masks, residual, image, multipliers, projected, direction,
    got0, got1, got2, got3, received,
    out_multipliers, out_residual,
):
    summed = jnp.sum(received[...], axis=0)
    field = jumped(z, masks, faces, (got0, got1, got2, got3))
    gamma, curvature = scalar_of(sums[...], 0), scalar_of(sums[...], 1)
    fresh, straight, crossed = (scalar_of(summed, i) for i in range(3))
    beta = fresh / gamma
    alpha = fresh / (straight + beta * crossed + beta * beta * curvature)
    for f in range(4):
        step = projected[f] + beta * direction[f]
        out_multipliers[0, 0, f] = (multipliers[f] + alpha * step)[:, 0 : z.face]
        out_residual[0, 0, f] = (residual[f] - alpha * (field[f] + beta * image[f]))[:, 0 : z.face]


class Coming:
    def __init__(self, source, held, semaphore):
        self.held = held
        self.copy = pltpu.make_async_copy(source, held, semaphore)
        self.copy.start()

    def ready(self):
        if self.copy is not None:
            self.copy.wait()
            self.copy = None
        return self.held

    def __getitem__(self, index):
        return self.ready()[index]


class Going:
    def __init__(self, held, target, semaphore):
        self.held = held
        self.copy = pltpu.make_async_copy(held, target, semaphore)
        self.shape, self.dtype = held.shape, held.dtype
        self.started = False

    def __getitem__(self, index):
        return self.held[index]

    def __setitem__(self, index, values):
        self.held[index] = values

    def push(self):
        if not self.started:
            self.copy.start()
            self.started = True


def call(z, kernel, outs, args, scratch=(), flops=0, near=0, kept=0):
    shapes = [jax.ShapeDtypeStruct(shape, dtype) for shape, dtype in outs]
    moved = sum(a.size * a.dtype.itemsize for a in args) + sum(s.size * s.dtype.itemsize for s in shapes)
    far, sent = len(args) - near, len(outs) - kept

    def run(*refs):
        refs = list(refs)
        take = lambda n: [refs.pop(0) for _ in range(n)]
        sources, others, targets, direct = take(far), take(near), take(sent), take(kept)
        held, made, work = take(far), take(sent), take(len(scratch))
        coming = [Coming(a, b, refs[0].at[i]) for i, (a, b) in enumerate(zip(sources, held))]
        going = [Going(a, b, refs[0].at[far + i]) for i, (a, b) in enumerate(zip(made, targets))]
        kernel(z, *coming, *others, *going, *direct, *work)
        for item in going:
            item.push()
        for item in coming:
            item.ready()
        for item in going:
            item.copy.wait()

    near_spec = lambda a: pl.BlockSpec(memory_space=SMEM if a.ndim == 3 and a.size == 4 else VMEM)
    far_spec = pl.BlockSpec(memory_space=pltpu.HBM)
    buffers = [VMEM(a.shape, a.dtype) for a in list(args[:far]) + shapes[:sent]]
    semaphores = [pltpu.SemaphoreType.DMA((far + sent,))] if far + sent else []
    return pl.pallas_call(
        run,
        out_shape=[pltpu.HBM(a.shape, a.dtype) for a in shapes[:sent]] + shapes[sent:],
        in_specs=[far_spec] * far + [near_spec(a) for a in args[far:]],
        out_specs=[far_spec] * sent + [near_spec(a) for a in shapes[sent:]],
        scratch_shapes=buffers + [VMEM(shape, dtype) for shape, dtype in scratch] + semaphores,
        compiler_params=pltpu.CompilerParams(vmem_limit_bytes=24 * 2**20),
        cost_estimate=pl.CostEstimate(flops=flops, bytes_accessed=moved, transcendentals=0),
        name=kernel.__name__,
    )(*[pltpu.with_memory_space_constraint(a, pltpu.HBM) for a in args[:far]], *args[far:])


def gather(values):
    return lax.all_to_all(values, AXES, 0, 0, tiled=True)


def body(ops, traces, primal, loads, maps, counts):
    z = Sizes(lax.axis_size("gx"), lax.axis_size("gy"), traces, loads)
    field = ((4, z.cases, z.lanes), F32)
    mode_rows = ((4, 8, z.lanes), F32)
    pair_rows = ((4, 16, z.lanes), F32)
    live_rows = ((8, z.lanes), F32)
    tile = ((8, 128), F32)
    sent = ((z.count, 8, 128), F32)
    to_faces = [((z.cases, z.lanes), F32)] * 4
    columns = -(-z.rows // 128) * 128
    product_flops = 2 * z.cases * z.order**2

    padded, masks, *trace_faces = call(
        z, prepare, [mode_rows, live_rows] + [((8, z.lanes), F32)] * 4,
        [jnp.transpose(traces, (0, 1, 3, 2, 4)), counts], near=2, kept=6,
    )
    got = exchange(trace_faces)
    (local_tile,) = call(
        z, invert, [tile], [padded, masks, jnp.transpose(loads, (0, 2, 1, 3))],
        [tile, ((8, z.cases), F32)], product_flops, near=3, kept=1,
    )
    blocks, masks, lift_rows = call(
        z, couple, [sent, live_rows, pair_rows], [padded, masks, local_tile, *got], [tile], near=7,
    )
    blocks = gather(blocks)
    packed = ((z.cases, z.padded), F32)
    primal_packed, arranged = call(
        z, arrange, [((z.cases, z.order), F32), ((z.order, z.order), BF16)], [ops, primal, maps],
        [((8, z.padded), jnp.int32), ((z.order, z.order), BF16)], 4 * z.order**2 * z.width, near=1, kept=1,
    )
    solve_rows, rows, multipliers, faces, coarse, *sent_faces = call(
        z, begin, [((40, z.rows), F32), pair_rows, field, field, sent] + to_faces,
        [lift_rows, primal_packed, blocks, arranged],
        [((z.rows, columns), F32), tile, packed], product_flops, near=2,
    )
    coarse, got = gather(coarse), exchange(sent_faces)
    residual, direction, faces, coarse, *sent_faces = call(
        z, first_direction, [field, field, field, sent] + to_faces,
        [solve_rows, lift_rows, faces, masks, rows, *got, coarse, arranged],
        [tile, packed], product_flops, near=2,
    )
    coarse, got = gather(coarse), exchange(sent_faces)
    multipliers, residual, projected, image, faces, sums, coarse, *sent_faces = call(
        z, second_direction, [field, field, field, field, field, tile, sent] + to_faces,
        [solve_rows, lift_rows, faces, masks, residual, direction, multipliers, *got, coarse, arranged],
        [packed], product_flops, near=2,
    )
    coarse, got = gather(coarse), exchange(sent_faces)
    whole = ((1, 1, 4, z.cases, z.face), F32)
    multipliers, residual = call(
        z, finish, [whole, whole],
        [sums, faces, masks, residual, image, multipliers, projected, direction, *got, coarse], near=1,
    )
    return multipliers, residual


def solution(mesh):
    in_specs = (
        P("gx", "gy", None, None),
        P("gx", "gy", None, None, None),
        P("gx", "gy", None, None),
        P("gx", "gy", None, None),
        P("gx", "gy", None, None),
        P("gx", "gy", None),
    )
    out_specs = (P("gx", "gy", None, None, None), P("gx", "gy", None, None, None))
    return jax.shard_map(body, mesh=mesh, in_specs=in_specs, out_specs=out_specs, check_vma=False)
```

```python
import functools

import jax
import jax.numpy as jnp
from jax import lax
from jax.experimental import pallas as pl
from jax.experimental.pallas import tpu as pltpu
from jax.sharding import PartitionSpec as P

SIGNS = (-1.0, 1.0, -1.0, 1.0)
HIGHEST = lax.Precision.HIGHEST
AXES = ("gx", "gy")
F32 = jnp.float32
BF16 = jnp.bfloat16
VMEM = pltpu.VMEM
SMEM = pltpu.SMEM
FIRST_LANE = 32
INVERSE_LANE = 48
SCALAR_LANE = 96
BLOCK = 256


class Sizes:
    def __init__(self, nx, ny, traces, loads):
        self.nx, self.ny = nx, ny
        self.count = nx * ny
        self.modes, self.face = traces.shape[-2:]
        self.cases = loads.shape[-1]
        self.order = 4 * self.face
        self.lanes = -(-self.face // 128) * 128
        self.starts = [f * self.face // 128 * 128 for f in range(4)]
        ends = [-(-(f + 1) * self.face // 128) * 128 for f in range(4)]
        self.width = max(e - s for s, e in zip(self.starts, ends))
        self.padded = max(s + self.width for s in self.starts)
        self.wide = min(nx, 9)
        self.rows = self.wide * ny * 8
        self.steps = (-ny, ny, -1, 1)


def dot(a, b, contract=(1, 0), precision=HIGHEST):
    dims = (((contract[0],), (contract[1],)), ((), ()))
    return lax.dot_general(a, b, dims, precision=precision, preferred_element_type=F32)


def iota(shape, dim):
    return lax.broadcasted_iota(jnp.int32, shape, dim)


def place():
    return lax.axis_index("gx"), lax.axis_index("gy")


def window_start(z, ix):
    return jnp.clip(ix - 4, 0, z.nx - z.wide) if z.wide < z.nx else 0


def spots(z, ix, iy):
    own = (ix - window_start(z, ix)) * z.ny + iy
    return [own] + [jnp.clip(own + step, 0, z.wide * z.ny - 1) for step in z.steps]


def send_faces(z, faces, sent):
    for i, at in enumerate(place()):
        even = at % 2 == 0
        low, high = faces[2 * i], faces[2 * i + 1]
        sent[2 * i][...] = jnp.where(even, high, low)
        sent[2 * i + 1][...] = jnp.where(even, low, high)
        sent[2 * i].push()
        sent[2 * i + 1].push()


def across_faces(z, got):
    found = []
    for i, at in enumerate(place()):
        even = at % 2 == 0
        first, second = got[2 * i][...], got[2 * i + 1][...]
        found += [jnp.where(even, second, first), jnp.where(even, first, second)]
    return found


def exchange(sent):
    got = [None] * 4
    for i in (1, 3, 0, 2):
        axis = AXES[i // 2]
        pairs = []
        for low in range(i % 2, lax.axis_size(axis) - 1, 2):
            pairs += [(low, low + 1), (low + 1, low)]
        got[i] = lax.ppermute(sent[i], axis, pairs)
    return got


def prepare(z, traces, counts, padded, masks, *sent):
    padded[...] = jnp.zeros(padded.shape, F32)
    for f in range(4):
        for j in range(z.modes):
            padded[f, j : j + 1, 0 : z.face] = traces[0, 0, j, f : f + 1]
    for i, at in enumerate(place()):
        even = at % 2 == 0
        low, high = padded[2 * i], padded[2 * i + 1]
        sent[2 * i][...] = jnp.where(even, high, low)
        sent[2 * i + 1][...] = jnp.where(even, low, high)
    row, lane = iota(masks.shape, 0), iota(masks.shape, 1)
    live = jnp.zeros(masks.shape, F32)
    for f in range(4):
        live = jnp.where((row == f) & (lane < counts[0, 0, f]), 1.0, live)
    masks[...] = live


def blocks_of(z):
    found = []
    for low in range(0, z.order, BLOCK):
        high = min(low + BLOCK, z.order)
        first, last = low // z.face, (high - 1) // z.face
        found.append((low, high, first * z.face // 128 * 128, min(-(-(last + 1) * z.face // 128) * 128, z.order)))
    return found


def arrange(z, ops, primal, maps, primal_packed, arranged, flat, half):
    flat[...] = jnp.zeros_like(flat)
    flat[0:4, 0 : z.face] = maps[0, 0]
    lane = iota((1, z.padded), 1)
    line = jnp.full((1, z.padded), -1, jnp.int32)
    signs = jnp.zeros((1, z.padded), F32)
    for f in range(4):
        moved = pltpu.roll(flat[...], f * z.face, 1)[f : f + 1] if f else flat[0:1]
        here = (lane >= f * z.face) & (lane < (f + 1) * z.face)
        line = jnp.where(here, moved + f * z.face, line)
        signs = jnp.where(here, SIGNS[f], signs)
    column = jnp.transpose(jnp.broadcast_to(line, (8, z.padded)))[:, 0:1]
    spread = []
    for low, high, first, last in blocks_of(z):
        hit = (iota((last - first, high - low), 1) + low) == column[first:last]
        spread.append(hit.astype(F32).astype(BF16))
    for low, high, first, last in blocks_of(z):
        hit = (iota((high - low, last - first), 0) + low) == line[:, first:last]
        collect = jnp.where(hit, signs[:, first:last], 0.0).astype(BF16)
        half[low:high, :] = dot(collect, ops[0, 0, first:last, :], precision=None).astype(BF16)
    values = primal[0, 0]
    parts = []
    for _ in range(3):
        parts.append(values.astype(BF16))
        values = values - parts[-1].astype(F32)
    pieces = jnp.concatenate(parts, axis=0)
    n = z.cases
    for (low, high, first, last), there in zip(blocks_of(z), spread):
        three = dot(pieces[:, first:last], there, precision=None)
        primal_packed[:, low:high] = three[0:n] + (three[n : 2 * n] + three[2 * n :])
    primal_packed.push()
    for (low, high, first, last), there in zip(blocks_of(z), spread):
        arranged[:, low:high] = dot(half[:, first:last], there, precision=None).astype(BF16)


def invert(z, padded, masks, loads, local_tile, aug, small):
    diagonal = sum(dot(padded[f] * masks[f : f + 1], padded[f], (1, 1)) for f in range(4))
    row, col = iota((8, 128), 0), iota((8, 128), 1)
    aug[...] = jnp.where((col == row + 8) & (row < z.modes), 1.0, 0.0).astype(F32)
    aug[:, 0:8] = diagonal
    matrix = aug[...]
    for p in range(z.modes):
        scaled = matrix[p : p + 1, :] / matrix[p : p + 1, p : p + 1]
        taken = matrix[:, p : p + 1] - (row[:, 0:1] == p).astype(F32)
        matrix = matrix - taken * scaled
    inverse = matrix[:, 8:16]
    small[...] = jnp.zeros(small.shape, F32)
    for j in range(z.modes):
        small[j : j + 1, :] = loads[0, j]
    local_tile[...] = jnp.zeros(local_tile.shape, F32)
    local_tile[:, FIRST_LANE : FIRST_LANE + z.cases] = dot(inverse, small[...])
    local_tile[:, INVERSE_LANE : INVERSE_LANE + 8] = inverse


def couple(z, padded, masks, local_tile, got0, got1, got2, got3, sent, live_rows, lift_rows, tile):
    near = across_faces(z, (got0, got1, got2, got3))
    inverse = local_tile[:, INVERSE_LANE : INVERSE_LANE + 8]
    tile[...] = local_tile[...]
    for f in range(4):
        live = padded[f] * masks[f : f + 1]
        lift_rows[f] = jnp.concatenate([live * SIGNS[f], near[f] * masks[f : f + 1] * -SIGNS[f]], axis=0)
        tile[:, 8 * f : 8 * f + 8] = dot(inverse, dot(live, near[f], (1, 1)))
    sent[...] = tile[...]
    sent.push()
    live_rows[...] = masks[...]


def lifted(z, amplitudes, lift_rows, f):
    pair = jnp.concatenate([amplitudes[0:8], amplitudes[8 * f + 8 : 8 * f + 16]], axis=0)
    return dot(pair, lift_rows[f], (0, 0))


def apply(z, faces, arranged, packed):
    packed[...] = jnp.zeros(packed.shape, F32)
    for f in range(4):
        wide = jnp.concatenate([faces[f], jnp.zeros((z.cases, z.width - z.lanes), F32)], axis=1)
        shift = f * z.face - z.starts[f]
        packed[:, z.starts[f] : z.starts[f] + z.width] += pltpu.roll(wide, shift, 1) if shift else wide
    return dot(packed[:, 0 : z.order].astype(BF16), arranged[...], precision=None)


def unpacked(z, values, packed):
    packed[:, 0 : z.order] = values
    found = []
    for f in range(4):
        part = packed[:, z.starts[f] : z.starts[f] + z.width]
        shift = f * z.face - z.starts[f]
        part = (pltpu.roll(part, z.width - shift, 1) if shift else part)[:, 0 : z.lanes]
        found.append(jnp.where(iota(part.shape, 1) < z.face, part, 0.0))
    return found


def send_coarse(z, faces, rows, scalars, sent, tile):
    tile[...] = jnp.zeros_like(tile)
    mine = jnp.zeros((8, z.cases), F32)
    for f in range(4):
        both = dot(rows[f], faces[f], (1, 1))
        mine = mine + both[0:8]
        tile[:, (1 + f) * z.cases : (2 + f) * z.cases] = both[8:16]
    tile[:, 0 : z.cases] = mine
    send_tile(tile[...], scalars, sent)


def send_tile(values, scalars, sent):
    row, col = iota((8, 128), 0), iota((8, 128), 1)
    for i, scalar in enumerate(scalars):
        values = jnp.where((row == 0) & (col == SCALAR_LANE + i), scalar, values)
    sent[...] = values
    sent.push()


def scalar_of(total, i):
    row, col = iota((8, 128), 0), iota((8, 128), 1)
    return jnp.sum(jnp.where((row == 0) & (col == SCALAR_LANE + i), total, 0.0), keepdims=True)


def received_window(z, received):
    ix, _ = place()
    start = window_start(z, ix) * z.ny
    return received[pl.ds(start, z.wide * z.ny)].reshape(z.rows, 128)


def coarse_amplitudes(z, received, solve_rows):
    values = received_window(z, received)
    start = values
    for f in range(4):
        across = pltpu.roll(values, 128 - (1 + (f ^ 1)) * z.cases, 1)
        step = 8 * z.steps[f]
        empty = jnp.zeros((abs(step), 128), F32)
        if step > 0:
            moved = jnp.concatenate([across[step:], empty], axis=0)
        else:
            moved = jnp.concatenate([empty, across[: z.rows + step]], axis=0)
        start = start - moved
    return dot(solve_rows[...], start)[:, 0 : z.cases]


def total(values):
    return jnp.sum(values, keepdims=True)


def face_weights(z):
    ix, iy = place()
    edges = (ix == 0, ix == z.nx - 1, iy == 0, iy == z.ny - 1)
    return [jnp.where(edge, 1.0, 0.5).astype(F32) for edge in edges]


def begin(
    z, received, lift_rows, primal, arranged,
    solve_rows, rows, multipliers, faces, sent, to0, to1, to2, to3,
    matrix, tile, packed,
):
    ix, iy = place()
    near_spots = spots(z, ix, iy)
    values = received_window(z, received)
    lane = iota((z.rows, 128), 1)
    row = iota((z.rows, 128), 0)
    tiled = []
    for f in range(4):
        part = jnp.where(lane // 8 == f, values, 0.0)
        for shift in (64, 32, 16, 8):
            part = part + pltpu.roll(part, shift, 1)
        tiled.append(part)
    for block in range(-(-z.rows // 128)):
        target = (lane + 128 * block) // 8 - row // 8
        part = jnp.zeros((z.rows, 128), F32)
        for f in range(4):
            part = part + jnp.where(target == z.steps[f], tiled[f], 0.0)
        matrix[:, 128 * block : 128 * block + 128] = part
    once = jnp.concatenate([matrix[pl.ds(pl.multiple_of(s * 8, 8), 8), 0 : z.rows] for s in near_spots], axis=0)
    twice = dot(once, matrix[:, 0 : z.rows])
    cols = z.rows
    unit = jnp.concatenate([
        (iota((8, cols), 1) == iota((8, cols), 0) + s * 8).astype(F32) for s in near_spots
    ], axis=0)
    solve = unit + once + twice
    solve_rows[...] = solve
    amplitudes = dot(solve, values)[:, FIRST_LANE : FIRST_LANE + z.cases]
    start = window_start(z, ix) * z.ny
    inverses = [received[pl.ds(start + spot, 1)][0][:, INVERSE_LANE : INVERSE_LANE + 8] for spot in near_spots]
    fields = []
    for f in range(4):
        both = lift_rows[f]
        own, near = both[0:8] * SIGNS[f], both[8:16] * -SIGNS[f]
        rows[f] = jnp.concatenate([dot(inverses[0], own), dot(inverses[1 + f], near)], axis=0)
        fields.append(lifted(z, amplitudes, lift_rows, f))
        multipliers[f] = fields[f]
    for item in (solve_rows, rows, multipliers):
        item.push()
    image = unpacked(z, primal[...] - apply(z, fields, arranged, packed), packed)
    for f in range(4):
        faces[f] = image[f]
    faces.push()
    send_faces(z, image, (to0, to1, to2, to3))
    send_coarse(z, image, rows, [], sent, tile)


def jumped(z, masks, faces, got):
    near = across_faces(z, got)
    return [masks[f : f + 1] * SIGNS[f] * (faces[f] - near[f]) for f in range(4)]


def first_direction(
    z, received, solve_rows, lift_rows, faces, masks, rows, got0, got1, got2, got3, arranged,
    residual, direction, image, sent, to0, to1, to2, to3,
    tile, packed,
):
    amplitudes = coarse_amplitudes(z, received, solve_rows)
    field = jumped(z, masks, faces, (got0, got1, got2, got3))
    weights = face_weights(z)
    moved = [field[f] - lifted(z, amplitudes, lift_rows, f) for f in range(4)]
    for f in range(4):
        residual[f] = field[f]
        direction[f] = moved[f]
    residual.push()
    direction.push()
    found = unpacked(z, apply(z, moved, arranged, packed), packed)
    for f in range(4):
        image[f] = found[f]
    image.push()
    gamma = sum(weights[f] * total(field[f] * moved[f]) for f in range(4))
    curvature = sum(SIGNS[f] * total(moved[f] * found[f]) for f in range(4))
    send_faces(z, found, (to0, to1, to2, to3))
    send_coarse(z, found, rows, [gamma, curvature], sent, tile)


def second_direction(
    z, received, solve_rows, lift_rows, faces, masks, residual, direction, multipliers,
    got0, got1, got2, got3, arranged,
    next_multipliers, next_residual, projected, image, fresh, sums, sent, to0, to1, to2, to3,
    packed,
):
    amplitudes = coarse_amplitudes(z, received, solve_rows)
    summed = jnp.sum(received[...], axis=0)
    sums[...] = summed
    alpha = scalar_of(summed, 0) / scalar_of(summed, 1)
    field = jumped(z, masks, faces, (got0, got1, got2, got3))
    weights = face_weights(z)
    left, moved = [], []
    for f in range(4):
        image[f] = field[f]
        next_multipliers[f] = multipliers[f] + alpha * direction[f]
        left.append(residual[f] - alpha * field[f])
        moved.append(direction[f] - alpha * (field[f] - lifted(z, amplitudes, lift_rows, f)))
        next_residual[f] = left[f]
        projected[f] = moved[f]
    for item in (sums, image, next_multipliers, next_residual, projected):
        item.push()
    found = unpacked(z, apply(z, moved, arranged, packed), packed)
    for f in range(4):
        fresh[f] = found[f]
    fresh.push()
    send_faces(z, found, (to0, to1, to2, to3))
    gamma = sum(weights[f] * total(left[f] * moved[f]) for f in range(4))
    straight = sum(SIGNS[f] * total(moved[f] * found[f]) for f in range(4))
    crossed = sum(
        weights[f] * total(moved[f] * field[f]) + SIGNS[f] * total(direction[f] * found[f]) for f in range(4)
    )
    send_tile(jnp.zeros((8, 128), F32), [gamma, straight, crossed], sent)


def finish(
    z, received, sums, faces, masks, residual, image, multipliers, projected, direction,
    got0, got1, got2, got3,
    out_multipliers, out_residual,
):
    summed = jnp.sum(received[...], axis=0)
    field = jumped(z, masks, faces, (got0, got1, got2, got3))
    gamma, curvature = scalar_of(sums[...], 0), scalar_of(sums[...], 1)
    fresh, straight, crossed = (scalar_of(summed, i) for i in range(3))
    beta = fresh / gamma
    alpha = fresh / (straight + beta * crossed + beta * beta * curvature)
    for f in range(4):
        step = projected[f] + beta * direction[f]
        out_multipliers[0, 0, f] = (multipliers[f] + alpha * step)[:, 0 : z.face]
        out_residual[0, 0, f] = (residual[f] - alpha * (field[f] + beta * image[f]))[:, 0 : z.face]


class Coming:
    def __init__(self, source, held, semaphore):
        self.held = held
        self.copy = pltpu.make_async_copy(source, held, semaphore)
        self.copy.start()

    def ready(self):
        if self.copy is not None:
            self.copy.wait()
            self.copy = None
        return self.held

    def __getitem__(self, index):
        return self.ready()[index]


class Going:
    def __init__(self, held, target, semaphore):
        self.held = held
        self.copy = pltpu.make_async_copy(held, target, semaphore)
        self.shape, self.dtype = held.shape, held.dtype
        self.started = False

    def __getitem__(self, index):
        return self.held[index]

    def __setitem__(self, index, values):
        self.held[index] = values

    def push(self):
        if not self.started:
            self.copy.start()
            self.started = True


def call(z, kernel, outs, args, scratch=(), flops=0, near=0, kept=0):
    shapes = [jax.ShapeDtypeStruct(shape, dtype) for shape, dtype in outs]
    moved = sum(a.size * a.dtype.itemsize for a in args) + sum(s.size * s.dtype.itemsize for s in shapes)
    far, sent = len(args) - near, len(outs) - kept

    def run(*refs):
        refs = list(refs)
        take = lambda n: [refs.pop(0) for _ in range(n)]
        sources, others, targets, direct = take(far), take(near), take(sent), take(kept)
        held, made, work = take(far), take(sent), take(len(scratch))
        coming = [Coming(a, b, refs[0].at[i]) for i, (a, b) in enumerate(zip(sources, held))]
        going = [Going(a, b, refs[0].at[far + i]) for i, (a, b) in enumerate(zip(made, targets))]
        kernel(z, *coming, *others, *going, *direct, *work)
        for item in going:
            item.push()
        for item in coming:
            item.ready()
        for item in going:
            item.copy.wait()

    near_spec = lambda a: pl.BlockSpec(memory_space=SMEM if a.ndim == 3 and a.size == 4 else VMEM)
    far_spec = pl.BlockSpec(memory_space=pltpu.HBM)
    buffers = [VMEM(a.shape, a.dtype) for a in list(args[:far]) + shapes[:sent]]
    semaphores = [pltpu.SemaphoreType.DMA((far + sent,))] if far + sent else []
    return pl.pallas_call(
        run,
        out_shape=[pltpu.HBM(a.shape, a.dtype) for a in shapes[:sent]] + shapes[sent:],
        in_specs=[far_spec] * far + [near_spec(a) for a in args[far:]],
        out_specs=[far_spec] * sent + [near_spec(a) for a in shapes[sent:]],
        scratch_shapes=buffers + [VMEM(shape, dtype) for shape, dtype in scratch] + semaphores,
        compiler_params=pltpu.CompilerParams(vmem_limit_bytes=24 * 2**20),
        cost_estimate=pl.CostEstimate(flops=flops, bytes_accessed=moved, transcendentals=0),
        name=kernel.__name__,
    )(*[pltpu.with_memory_space_constraint(a, pltpu.HBM) for a in args[:far]], *args[far:])


def gather(values):
    return lax.all_gather(values, AXES)


def body(ops, traces, primal, loads, maps, counts):
    z = Sizes(lax.axis_size("gx"), lax.axis_size("gy"), traces, loads)
    field = ((4, z.cases, z.lanes), F32)
    mode_rows = ((4, 8, z.lanes), F32)
    pair_rows = ((4, 16, z.lanes), F32)
    live_rows = ((8, z.lanes), F32)
    tile = ((8, 128), F32)
    sent = ((8, 128), F32)
    to_faces = [((z.cases, z.lanes), F32)] * 4
    columns = -(-z.rows // 128) * 128
    product_flops = 2 * z.cases * z.order**2

    padded, masks, *trace_faces = call(
        z, prepare, [mode_rows, live_rows] + [((8, z.lanes), F32)] * 4,
        [jnp.transpose(traces, (0, 1, 3, 2, 4)), counts], near=2, kept=6,
    )
    got = exchange(trace_faces)
    (local_tile,) = call(
        z, invert, [tile], [padded, masks, jnp.transpose(loads, (0, 2, 1, 3))],
        [tile, ((8, z.cases), F32)], product_flops, near=3, kept=1,
    )
    blocks, masks, lift_rows = call(
        z, couple, [sent, live_rows, pair_rows], [padded, masks, local_tile, *got], [tile], near=7,
    )
    blocks = gather(blocks)
    packed = ((z.cases, z.padded), F32)
    primal_packed, arranged = call(
        z, arrange, [((z.cases, z.order), F32), ((z.order, z.order), BF16)], [ops, primal, maps],
        [((8, z.padded), jnp.int32), ((z.order, z.order), BF16)], 4 * z.order**2 * z.width, near=1, kept=1,
    )
    solve_rows, rows, multipliers, faces, coarse, *sent_faces = call(
        z, begin, [((40, z.rows), F32), pair_rows, field, field, sent] + to_faces,
        [blocks, lift_rows, primal_packed, arranged],
        [((z.rows, columns), F32), tile, packed], product_flops, near=1,
    )
    coarse, got = gather(coarse), exchange(sent_faces)
    residual, direction, faces, coarse, *sent_faces = call(
        z, first_direction, [field, field, field, sent] + to_faces,
        [coarse, solve_rows, lift_rows, faces, masks, rows, *got, arranged],
        [tile, packed], product_flops, near=5,
    )
    coarse, got = gather(coarse), exchange(sent_faces)
    multipliers, residual, projected, image, faces, sums, coarse, *sent_faces = call(
        z, second_direction, [field, field, field, field, field, tile, sent] + to_faces,
        [coarse, solve_rows, lift_rows, faces, masks, residual, direction, multipliers, *got, arranged],
        [packed], product_flops, near=5,
    )
    coarse, got = gather(coarse), exchange(sent_faces)
    whole = ((1, 1, 4, z.cases, z.face), F32)
    multipliers, residual = call(
        z, finish, [whole, whole],
        [coarse, sums, faces, masks, residual, image, multipliers, projected, direction, *got], near=4,
    )
    return multipliers, residual


def solution(mesh):
    in_specs = (
        P("gx", "gy", None, None),
        P("gx", "gy", None, None, None),
        P("gx", "gy", None, None),
        P("gx", "gy", None, None),
        P("gx", "gy", None, None),
        P("gx", "gy", None),
    )
    out_specs = (P("gx", "gy", None, None, None), P("gx", "gy", None, None, None))
    return jax.shard_map(body, mesh=mesh, in_specs=in_specs, out_specs=out_specs, check_vma=False)
```

```python
import functools

import jax
import jax.numpy as jnp
from jax import lax
from jax.experimental import pallas as pl
from jax.experimental.pallas import tpu as pltpu
from jax.sharding import PartitionSpec as P

SIGNS = (-1.0, 1.0, -1.0, 1.0)
HIGHEST = lax.Precision.HIGHEST
AXES = ("gx", "gy")
F32 = jnp.float32
BF16 = jnp.bfloat16
VMEM = pltpu.VMEM
SMEM = pltpu.SMEM
FIRST_LANE = 32
INVERSE_LANE = 48
SCALAR_LANE = 96
BLOCK = 256
SWAPS = (1, 3, 0, 2)


class Sizes:
    def __init__(self, nx, ny, traces, loads):
        self.nx, self.ny = nx, ny
        self.count = nx * ny
        self.modes, self.face = traces.shape[-2:]
        self.cases = loads.shape[-1]
        self.order = 4 * self.face
        self.lanes = -(-self.face // 128) * 128
        self.starts = [f * self.face // 128 * 128 for f in range(4)]
        ends = [-(-(f + 1) * self.face // 128) * 128 for f in range(4)]
        self.width = max(e - s for s, e in zip(self.starts, ends))
        self.padded = max(s + self.width for s in self.starts)
        self.wide = min(nx, 9)
        self.rows = self.wide * ny * 8
        self.steps = (-ny, ny, -1, 1)


def dot(a, b, contract=(1, 0), precision=HIGHEST):
    dims = (((contract[0],), (contract[1],)), ((), ()))
    return lax.dot_general(a, b, dims, precision=precision, preferred_element_type=F32)


def iota(shape, dim):
    return lax.broadcasted_iota(jnp.int32, shape, dim)


def place():
    return lax.axis_index("gx"), lax.axis_index("gy")


def window_start(z, ix):
    return jnp.clip(ix - 4, 0, z.nx - z.wide) if z.wide < z.nx else 0


def spots(z, ix, iy):
    own = (ix - window_start(z, ix)) * z.ny + iy
    return [own] + [jnp.clip(own + step, 0, z.wide * z.ny - 1) for step in z.steps]


def send_faces(z, faces, sent):
    for i, at in enumerate(place()):
        even = at % 2 == 0
        low, high = faces[2 * i], faces[2 * i + 1]
        sent[2 * i][...] = jnp.where(even, high, low)
        sent[2 * i + 1][...] = jnp.where(even, low, high)
        sent[2 * i].push()
        sent[2 * i + 1].push()


def across_faces(z, got):
    found = []
    for i, at in enumerate(place()):
        even = at % 2 == 0
        first, second = got[2 * i][...], got[2 * i + 1][...]
        found += [jnp.where(even, second, first), jnp.where(even, first, second)]
    return found


def exchange(sent):
    got = []
    for i in SWAPS:
        axis = AXES[i // 2]
        pairs = []
        for low in range(i % 2, lax.axis_size(axis) - 1, 2):
            pairs += [(low, low + 1), (low + 1, low)]
        got.append(lax.ppermute(sent[i], axis, pairs))
    return got


def prepare(z, traces, counts, padded, masks, *sent):
    padded[...] = jnp.zeros(padded.shape, F32)
    for f in range(4):
        for j in range(z.modes):
            padded[f, j : j + 1, 0 : z.face] = traces[0, 0, j, f : f + 1]
    for i, at in enumerate(place()):
        even = at % 2 == 0
        low, high = padded[2 * i], padded[2 * i + 1]
        sent[2 * i][...] = jnp.where(even, high, low)
        sent[2 * i + 1][...] = jnp.where(even, low, high)
    row, lane = iota(masks.shape, 0), iota(masks.shape, 1)
    live = jnp.zeros(masks.shape, F32)
    for f in range(4):
        live = jnp.where((row == f) & (lane < counts[0, 0, f]), 1.0, live)
    masks[...] = live


def blocks_of(z):
    found = []
    for low in range(0, z.order, BLOCK):
        high = min(low + BLOCK, z.order)
        first, last = low // z.face, (high - 1) // z.face
        found.append((low, high, first * z.face // 128 * 128, min(-(-(last + 1) * z.face // 128) * 128, z.order)))
    return found


def arrange(z, maps, ops, primal, primal_packed, arranged, flat, half):
    flat[...] = jnp.zeros_like(flat)
    flat[0:4, 0 : z.face] = maps[0, 0]
    lane = iota((1, z.padded), 1)
    line = jnp.full((1, z.padded), -1, jnp.int32)
    signs = jnp.zeros((1, z.padded), F32)
    for f in range(4):
        moved = pltpu.roll(flat[...], f * z.face, 1)[f : f + 1] if f else flat[0:1]
        here = (lane >= f * z.face) & (lane < (f + 1) * z.face)
        line = jnp.where(here, moved + f * z.face, line)
        signs = jnp.where(here, SIGNS[f], signs)
    column = jnp.transpose(jnp.broadcast_to(line, (8, z.padded)))[:, 0:1]
    spread = []
    for low, high, first, last in blocks_of(z):
        hit = (iota((last - first, high - low), 1) + low) == column[first:last]
        spread.append(hit.astype(F32).astype(BF16))
    for low, high, first, last in blocks_of(z):
        hit = (iota((high - low, last - first), 0) + low) == line[:, first:last]
        collect = jnp.where(hit, signs[:, first:last], 0.0).astype(BF16)
        half[low:high, :] = dot(collect, ops[0, 0, first:last, :], precision=None).astype(BF16)
    values = primal[0, 0]
    parts = []
    for _ in range(3):
        parts.append(values.astype(BF16))
        values = values - parts[-1].astype(F32)
    pieces = jnp.concatenate(parts, axis=0)
    n = z.cases
    for (low, high, first, last), there in zip(blocks_of(z), spread):
        three = dot(pieces[:, first:last], there, precision=None)
        primal_packed[:, low:high] = three[0:n] + (three[n : 2 * n] + three[2 * n :])
    primal_packed.push()
    for (low, high, first, last), there in zip(blocks_of(z), spread):
        arranged[:, low:high] = dot(half[:, first:last], there, precision=None).astype(BF16)


def invert(z, loads, padded, masks, local_tile, aug, small):
    diagonal = sum(dot(padded[f] * masks[f : f + 1], padded[f], (1, 1)) for f in range(4))
    row, col = iota((8, 128), 0), iota((8, 128), 1)
    aug[...] = jnp.where((col == row + 8) & (row < z.modes), 1.0, 0.0).astype(F32)
    aug[:, 0:8] = diagonal
    matrix = aug[...]
    for p in range(z.modes):
        scaled = matrix[p : p + 1, :] / matrix[p : p + 1, p : p + 1]
        taken = matrix[:, p : p + 1] - (row[:, 0:1] == p).astype(F32)
        matrix = matrix - taken * scaled
    inverse = matrix[:, 8:16]
    small[...] = jnp.zeros(small.shape, F32)
    for j in range(z.modes):
        small[j : j + 1, :] = loads[0, j]
    local_tile[...] = jnp.zeros(local_tile.shape, F32)
    local_tile[:, FIRST_LANE : FIRST_LANE + z.cases] = dot(inverse, small[...])
    local_tile[:, INVERSE_LANE : INVERSE_LANE + 8] = inverse


def couple(z, padded, masks, local_tile, got1, got3, got0, got2, sent, live_rows, lift_rows, tile):
    near = across_faces(z, (got0, got1, got2, got3))
    inverse = local_tile[:, INVERSE_LANE : INVERSE_LANE + 8]
    tile[...] = local_tile[...]
    for f in range(4):
        live = padded[f] * masks[f : f + 1]
        lift_rows[f] = jnp.concatenate([live * SIGNS[f], near[f] * masks[f : f + 1] * -SIGNS[f]], axis=0)
        tile[:, 8 * f : 8 * f + 8] = dot(inverse, dot(live, near[f], (1, 1)))
    sent[...] = jnp.broadcast_to(tile[...][None], sent.shape)
    sent.push()
    live_rows[...] = masks[...]


def lifted(z, amplitudes, lift_rows, f):
    pair = jnp.concatenate([amplitudes[0:8], amplitudes[8 * f + 8 : 8 * f + 16]], axis=0)
    return dot(pair, lift_rows[f], (0, 0))


def apply(z, faces, arranged, packed):
    packed[...] = jnp.zeros(packed.shape, F32)
    for f in range(4):
        wide = jnp.concatenate([faces[f], jnp.zeros((z.cases, z.width - z.lanes), F32)], axis=1)
        shift = f * z.face - z.starts[f]
        packed[:, z.starts[f] : z.starts[f] + z.width] += pltpu.roll(wide, shift, 1) if shift else wide
    return dot(packed[:, 0 : z.order].astype(BF16), arranged[...], precision=None)


def unpacked(z, values, packed):
    packed[:, 0 : z.order] = values
    found = []
    for f in range(4):
        part = packed[:, z.starts[f] : z.starts[f] + z.width]
        shift = f * z.face - z.starts[f]
        part = (pltpu.roll(part, z.width - shift, 1) if shift else part)[:, 0 : z.lanes]
        found.append(jnp.where(iota(part.shape, 1) < z.face, part, 0.0))
    return found


def send_coarse(z, faces, rows, scalars, sent, tile):
    tile[...] = jnp.zeros_like(tile)
    mine = jnp.zeros((8, z.cases), F32)
    for f in range(4):
        both = dot(rows[f], faces[f], (1, 1))
        mine = mine + both[0:8]
        tile[:, (1 + f) * z.cases : (2 + f) * z.cases] = both[8:16]
    tile[:, 0 : z.cases] = mine
    send_tile(tile[...], scalars, sent)


def send_tile(values, scalars, sent):
    row, col = iota((8, 128), 0), iota((8, 128), 1)
    for i, scalar in enumerate(scalars):
        values = jnp.where((row == 0) & (col == SCALAR_LANE + i), scalar, values)
    sent[...] = jnp.broadcast_to(values[None], sent.shape)
    sent.push()


def scalar_of(total, i):
    row, col = iota((8, 128), 0), iota((8, 128), 1)
    return jnp.sum(jnp.where((row == 0) & (col == SCALAR_LANE + i), total, 0.0), keepdims=True)


def received_window(z, received):
    ix, _ = place()
    start = window_start(z, ix) * z.ny
    return received[pl.ds(start, z.wide * z.ny)].reshape(z.rows, 128)


def coarse_amplitudes(z, received, solve_rows):
    values = received_window(z, received)
    start = values
    for f in range(4):
        across = pltpu.roll(values, 128 - (1 + (f ^ 1)) * z.cases, 1)
        step = 8 * z.steps[f]
        empty = jnp.zeros((abs(step), 128), F32)
        if step > 0:
            moved = jnp.concatenate([across[step:], empty], axis=0)
        else:
            moved = jnp.concatenate([empty, across[: z.rows + step]], axis=0)
        start = start - moved
    return dot(solve_rows[...], start)[:, 0 : z.cases]


def total(values):
    return jnp.sum(values, keepdims=True)


def face_weights(z):
    ix, iy = place()
    edges = (ix == 0, ix == z.nx - 1, iy == 0, iy == z.ny - 1)
    return [jnp.where(edge, 1.0, 0.5).astype(F32) for edge in edges]


def begin(
    z, lift_rows, primal, received, arranged,
    solve_rows, rows, multipliers, faces, sent, to0, to1, to2, to3,
    matrix, tile, packed,
):
    ix, iy = place()
    near_spots = spots(z, ix, iy)
    values = received_window(z, received)
    lane = iota((z.rows, 128), 1)
    row = iota((z.rows, 128), 0)
    tiled = []
    for f in range(4):
        part = jnp.where(lane // 8 == f, values, 0.0)
        for shift in (64, 32, 16, 8):
            part = part + pltpu.roll(part, shift, 1)
        tiled.append(part)
    for block in range(-(-z.rows // 128)):
        target = (lane + 128 * block) // 8 - row // 8
        part = jnp.zeros((z.rows, 128), F32)
        for f in range(4):
            part = part + jnp.where(target == z.steps[f], tiled[f], 0.0)
        matrix[:, 128 * block : 128 * block + 128] = part
    once = jnp.concatenate([matrix[pl.ds(pl.multiple_of(s * 8, 8), 8), 0 : z.rows] for s in near_spots], axis=0)
    twice = dot(once, matrix[:, 0 : z.rows])
    cols = z.rows
    unit = jnp.concatenate([
        (iota((8, cols), 1) == iota((8, cols), 0) + s * 8).astype(F32) for s in near_spots
    ], axis=0)
    solve = unit + once + twice
    solve_rows[...] = solve
    amplitudes = dot(solve, values)[:, FIRST_LANE : FIRST_LANE + z.cases]
    start = window_start(z, ix) * z.ny
    inverses = [received[pl.ds(start + spot, 1)][0][:, INVERSE_LANE : INVERSE_LANE + 8] for spot in near_spots]
    fields = []
    for f in range(4):
        both = lift_rows[f]
        own, near = both[0:8] * SIGNS[f], both[8:16] * -SIGNS[f]
        rows[f] = jnp.concatenate([dot(inverses[0], own), dot(inverses[1 + f], near)], axis=0)
        fields.append(lifted(z, amplitudes, lift_rows, f))
        multipliers[f] = fields[f]
    for item in (solve_rows, rows, multipliers):
        item.push()
    image = unpacked(z, primal[...] - apply(z, fields, arranged, packed), packed)
    for f in range(4):
        faces[f] = image[f]
    faces.push()
    send_faces(z, image, (to0, to1, to2, to3))
    send_coarse(z, image, rows, [], sent, tile)


def jumped(z, masks, faces, got):
    near = across_faces(z, got)
    return [masks[f : f + 1] * SIGNS[f] * (faces[f] - near[f]) for f in range(4)]


def first_direction(
    z, solve_rows, lift_rows, faces, masks, rows, got1, got3, got0, got2, received, arranged,
    residual, direction, image, sent, to0, to1, to2, to3,
    tile, packed,
):
    amplitudes = coarse_amplitudes(z, received, solve_rows)
    field = jumped(z, masks, faces, (got0, got1, got2, got3))
    weights = face_weights(z)
    moved = [field[f] - lifted(z, amplitudes, lift_rows, f) for f in range(4)]
    for f in range(4):
        residual[f] = field[f]
        direction[f] = moved[f]
    residual.push()
    direction.push()
    found = unpacked(z, apply(z, moved, arranged, packed), packed)
    for f in range(4):
        image[f] = found[f]
    image.push()
    gamma = sum(weights[f] * total(field[f] * moved[f]) for f in range(4))
    curvature = sum(SIGNS[f] * total(moved[f] * found[f]) for f in range(4))
    send_faces(z, found, (to0, to1, to2, to3))
    send_coarse(z, found, rows, [gamma, curvature], sent, tile)


def second_direction(
    z, solve_rows, lift_rows, faces, masks, residual, direction, multipliers,
    got1, got3, got0, got2, received, arranged,
    next_multipliers, next_residual, projected, image, fresh, sums, sent, to0, to1, to2, to3,
    packed,
):
    amplitudes = coarse_amplitudes(z, received, solve_rows)
    summed = jnp.sum(received[...], axis=0)
    sums[...] = summed
    alpha = scalar_of(summed, 0) / scalar_of(summed, 1)
    field = jumped(z, masks, faces, (got0, got1, got2, got3))
    weights = face_weights(z)
    left, moved = [], []
    for f in range(4):
        image[f] = field[f]
        next_multipliers[f] = multipliers[f] + alpha * direction[f]
        left.append(residual[f] - alpha * field[f])
        moved.append(direction[f] - alpha * (field[f] - lifted(z, amplitudes, lift_rows, f)))
        next_residual[f] = left[f]
        projected[f] = moved[f]
    for item in (sums, image, next_multipliers, next_residual, projected):
        item.push()
    found = unpacked(z, apply(z, moved, arranged, packed), packed)
    for f in range(4):
        fresh[f] = found[f]
    fresh.push()
    send_faces(z, found, (to0, to1, to2, to3))
    gamma = sum(weights[f] * total(left[f] * moved[f]) for f in range(4))
    straight = sum(SIGNS[f] * total(moved[f] * found[f]) for f in range(4))
    crossed = sum(
        weights[f] * total(moved[f] * field[f]) + SIGNS[f] * total(direction[f] * found[f]) for f in range(4)
    )
    send_tile(jnp.zeros((8, 128), F32), [gamma, straight, crossed], sent)


def finish(
    z, sums, faces, masks, residual, image, multipliers, projected, direction,
    got1, got3, got0, got2, received,
    out_multipliers, out_residual,
):
    summed = jnp.sum(received[...], axis=0)
    field = jumped(z, masks, faces, (got0, got1, got2, got3))
    gamma, curvature = scalar_of(sums[...], 0), scalar_of(sums[...], 1)
    fresh, straight, crossed = (scalar_of(summed, i) for i in range(3))
    beta = fresh / gamma
    alpha = fresh / (straight + beta * crossed + beta * beta * curvature)
    for f in range(4):
        step = projected[f] + beta * direction[f]
        out_multipliers[0, 0, f] = (multipliers[f] + alpha * step)[:, 0 : z.face]
        out_residual[0, 0, f] = (residual[f] - alpha * (field[f] + beta * image[f]))[:, 0 : z.face]


class Coming:
    def __init__(self, source, held, semaphore):
        self.held = held
        self.copy = pltpu.make_async_copy(source, held, semaphore)
        self.copy.start()

    def ready(self):
        if self.copy is not None:
            self.copy.wait()
            self.copy = None
        return self.held

    def __getitem__(self, index):
        return self.ready()[index]


class Going:
    def __init__(self, held, target, semaphore):
        self.held = held
        self.copy = pltpu.make_async_copy(held, target, semaphore)
        self.shape, self.dtype = held.shape, held.dtype
        self.started = False

    def __getitem__(self, index):
        return self.held[index]

    def __setitem__(self, index, values):
        self.held[index] = values

    def push(self):
        if not self.started:
            self.copy.start()
            self.started = True


def call(z, kernel, outs, args, scratch=(), flops=0, near=0, kept=0):
    shapes = [jax.ShapeDtypeStruct(shape, dtype) for shape, dtype in outs]
    moved = sum(a.size * a.dtype.itemsize for a in args) + sum(s.size * s.dtype.itemsize for s in shapes)
    far, sent = len(args) - near, len(outs) - kept

    def run(*refs):
        refs = list(refs)
        take = lambda n: [refs.pop(0) for _ in range(n)]
        sources, others, targets, direct = take(far), take(near), take(sent), take(kept)
        held, made, work = take(far), take(sent), take(len(scratch))
        coming = [Coming(a, b, refs[0].at[i]) for i, (a, b) in enumerate(zip(sources, held))]
        going = [Going(a, b, refs[0].at[far + i]) for i, (a, b) in enumerate(zip(made, targets))]
        kernel(z, *coming, *others, *going, *direct, *work)
        for item in going:
            item.push()
        for item in coming:
            item.ready()
        for item in going:
            item.copy.wait()

    near_spec = lambda a: pl.BlockSpec(memory_space=SMEM if a.ndim == 3 and a.size == 4 else VMEM)
    far_spec = pl.BlockSpec(memory_space=pltpu.HBM)
    buffers = [(SMEM if a.size == 4 else VMEM)(a.shape, a.dtype) for a in list(args[:far]) + shapes[:sent]]
    semaphores = [pltpu.SemaphoreType.DMA((far + sent,))] if far + sent else []
    return pl.pallas_call(
        run,
        out_shape=[pltpu.HBM(a.shape, a.dtype) for a in shapes[:sent]] + shapes[sent:],
        in_specs=[far_spec] * far + [near_spec(a) for a in args[far:]],
        out_specs=[far_spec] * sent + [near_spec(a) for a in shapes[sent:]],
        scratch_shapes=buffers + [VMEM(shape, dtype) for shape, dtype in scratch] + semaphores,
        compiler_params=pltpu.CompilerParams(vmem_limit_bytes=24 * 2**20),
        cost_estimate=pl.CostEstimate(flops=flops, bytes_accessed=moved, transcendentals=0),
        name=kernel.__name__,
    )(*[pltpu.with_memory_space_constraint(a, pltpu.HBM) for a in args[:far]], *args[far:])


def gather(values):
    return lax.all_to_all(values, AXES, 0, 0, tiled=True)


def body(ops, traces, primal, loads, maps, counts):
    z = Sizes(lax.axis_size("gx"), lax.axis_size("gy"), traces, loads)
    field = ((4, z.cases, z.lanes), F32)
    mode_rows = ((4, 8, z.lanes), F32)
    pair_rows = ((4, 16, z.lanes), F32)
    live_rows = ((8, z.lanes), F32)
    tile = ((8, 128), F32)
    sent = ((z.count, 8, 128), F32)
    to_faces = [((z.cases, z.lanes), F32)] * 4
    columns = -(-z.rows // 128) * 128
    product_flops = 2 * z.cases * z.order**2

    padded, masks, *trace_faces = call(
        z, prepare, [mode_rows, live_rows] + [((8, z.lanes), F32)] * 4,
        [jnp.transpose(traces, (0, 1, 3, 2, 4)), counts], kept=6,
    )
    got = exchange(trace_faces)
    (local_tile,) = call(
        z, invert, [tile], [jnp.transpose(loads, (0, 2, 1, 3)), padded, masks],
        [tile, ((8, z.cases), F32)], product_flops, near=2, kept=1,
    )
    blocks, masks, lift_rows = call(
        z, couple, [sent, live_rows, pair_rows], [padded, masks, local_tile, *got], [tile], near=7,
    )
    blocks = gather(blocks)
    packed = ((z.cases, z.padded), F32)
    primal_packed, arranged = call(
        z, arrange, [((z.cases, z.order), F32), ((z.order, z.order), BF16)], [maps, ops, primal],
        [((8, z.padded), jnp.int32), ((z.order, z.order), BF16)], 4 * z.order**2 * z.width, kept=1,
    )
    solve_rows, rows, multipliers, faces, coarse, *sent_faces = call(
        z, begin, [((40, z.rows), F32), pair_rows, field, field, sent] + to_faces,
        [lift_rows, primal_packed, blocks, arranged],
        [((z.rows, columns), F32), tile, packed], product_flops, near=2,
    )
    coarse, got = gather(coarse), exchange(sent_faces)
    residual, direction, faces, coarse, *sent_faces = call(
        z, first_direction, [field, field, field, sent] + to_faces,
        [solve_rows, lift_rows, faces, masks, rows, *got, coarse, arranged],
        [tile, packed], product_flops, near=2,
    )
    coarse, got = gather(coarse), exchange(sent_faces)
    multipliers, residual, projected, image, faces, sums, coarse, *sent_faces = call(
        z, second_direction, [field, field, field, field, field, tile, sent] + to_faces,
        [solve_rows, lift_rows, faces, masks, residual, direction, multipliers, *got, coarse, arranged],
        [packed], product_flops, near=2,
    )
    coarse, got = gather(coarse), exchange(sent_faces)
    whole = ((1, 1, 4, z.cases, z.face), F32)
    multipliers, residual = call(
        z, finish, [whole, whole],
        [sums, faces, masks, residual, image, multipliers, projected, direction, *got, coarse], near=1,
    )
    return multipliers, residual


def solution(mesh):
    in_specs = (
        P("gx", "gy", None, None),
        P("gx", "gy", None, None, None),
        P("gx", "gy", None, None),
        P("gx", "gy", None, None),
        P("gx", "gy", None, None),
        P("gx", "gy", None),
    )
    out_specs = (P("gx", "gy", None, None, None), P("gx", "gy", None, None, None))
    return jax.shard_map(body, mesh=mesh, in_specs=in_specs, out_specs=out_specs, check_vma=False)
```

```python
import functools

import jax
import jax.numpy as jnp
from jax import lax
from jax.experimental import pallas as pl
from jax.experimental.pallas import tpu as pltpu
from jax.sharding import PartitionSpec as P

SIGNS = (-1.0, 1.0, -1.0, 1.0)
HIGHEST = lax.Precision.HIGHEST
AXES = ("gx", "gy")
F32 = jnp.float32
BF16 = jnp.bfloat16
VMEM = pltpu.VMEM
SMEM = pltpu.SMEM
FIRST_LANE = 32
INVERSE_LANE = 48
SCALAR_LANE = 96
BLOCK = 256
SWAPS = (1, 0, 3, 2)


class Sizes:
    def __init__(self, nx, ny, traces, loads):
        self.nx, self.ny = nx, ny
        self.count = nx * ny
        self.modes, self.face = traces.shape[-2:]
        self.cases = loads.shape[-1]
        self.order = 4 * self.face
        self.lanes = -(-self.face // 128) * 128
        self.starts = [f * self.face // 128 * 128 for f in range(4)]
        ends = [-(-(f + 1) * self.face // 128) * 128 for f in range(4)]
        self.width = max(e - s for s, e in zip(self.starts, ends))
        self.padded = max(s + self.width for s in self.starts)
        self.wide = min(nx, 9)
        self.rows = self.wide * ny * 8
        self.steps = (-ny, ny, -1, 1)


def dot(a, b, contract=(1, 0), precision=HIGHEST):
    dims = (((contract[0],), (contract[1],)), ((), ()))
    return lax.dot_general(a, b, dims, precision=precision, preferred_element_type=F32)


def iota(shape, dim):
    return lax.broadcasted_iota(jnp.int32, shape, dim)


def place():
    return lax.axis_index("gx"), lax.axis_index("gy")


def window_start(z, ix):
    return jnp.clip(ix - 4, 0, z.nx - z.wide) if z.wide < z.nx else 0


def spots(z, ix, iy):
    own = (ix - window_start(z, ix)) * z.ny + iy
    return [own] + [jnp.clip(own + step, 0, z.wide * z.ny - 1) for step in z.steps]


def send_faces(z, faces, sent):
    for i, at in enumerate(place()):
        even = at % 2 == 0
        low, high = faces[2 * i], faces[2 * i + 1]
        sent[2 * i][...] = jnp.where(even, high, low)
        sent[2 * i + 1][...] = jnp.where(even, low, high)
        sent[2 * i].push()
        sent[2 * i + 1].push()


def across_faces(z, got):
    found = []
    for i, at in enumerate(place()):
        even = at % 2 == 0
        first, second = got[2 * i][...], got[2 * i + 1][...]
        found += [jnp.where(even, second, first), jnp.where(even, first, second)]
    return found


def exchange(sent):
    got = []
    for i in SWAPS:
        axis = AXES[i // 2]
        pairs = []
        for low in range(i % 2, lax.axis_size(axis) - 1, 2):
            pairs += [(low, low + 1), (low + 1, low)]
        got.append(lax.ppermute(sent[i], axis, pairs))
    return got


def prepare(z, traces, counts, padded, masks, *sent):
    padded[...] = jnp.zeros(padded.shape, F32)
    for f in range(4):
        for j in range(z.modes):
            padded[f, j : j + 1, 0 : z.face] = traces[0, 0, j, f : f + 1]
    for i, at in enumerate(place()):
        even = at % 2 == 0
        low, high = padded[2 * i], padded[2 * i + 1]
        sent[2 * i][...] = jnp.where(even, high, low)
        sent[2 * i + 1][...] = jnp.where(even, low, high)
    row, lane = iota(masks.shape, 0), iota(masks.shape, 1)
    live = jnp.zeros(masks.shape, F32)
    for f in range(4):
        live = jnp.where((row == f) & (lane < counts[0, 0, f]), 1.0, live)
    masks[...] = live


def blocks_of(z):
    found = []
    for low in range(0, z.order, BLOCK):
        high = min(low + BLOCK, z.order)
        first, last = low // z.face, (high - 1) // z.face
        found.append((low, high, first * z.face // 128 * 128, min(-(-(last + 1) * z.face // 128) * 128, z.order)))
    return found


def arrange(z, maps, ops, primal, primal_packed, arranged, flat, half):
    flat[...] = jnp.zeros_like(flat)
    flat[0:4, 0 : z.face] = maps[0, 0]
    lane = iota((1, z.padded), 1)
    line = jnp.full((1, z.padded), -1, jnp.int32)
    signs = jnp.zeros((1, z.padded), F32)
    for f in range(4):
        moved = pltpu.roll(flat[...], f * z.face, 1)[f : f + 1] if f else flat[0:1]
        here = (lane >= f * z.face) & (lane < (f + 1) * z.face)
        line = jnp.where(here, moved + f * z.face, line)
        signs = jnp.where(here, SIGNS[f], signs)
    column = jnp.transpose(jnp.broadcast_to(line, (8, z.padded)))[:, 0:1]
    spread = []
    for low, high, first, last in blocks_of(z):
        hit = (iota((last - first, high - low), 1) + low) == column[first:last]
        spread.append(hit.astype(F32).astype(BF16))
    for low, high, first, last in blocks_of(z):
        hit = (iota((high - low, last - first), 0) + low) == line[:, first:last]
        collect = jnp.where(hit, signs[:, first:last], 0.0).astype(BF16)
        half[low:high, :] = dot(collect, ops[0, 0, first:last, :], precision=None).astype(BF16)
    values = primal[0, 0]
    parts = []
    for _ in range(3):
        parts.append(values.astype(BF16))
        values = values - parts[-1].astype(F32)
    pieces = jnp.concatenate(parts, axis=0)
    n = z.cases
    for (low, high, first, last), there in zip(blocks_of(z), spread):
        three = dot(pieces[:, first:last], there, precision=None)
        primal_packed[:, low:high] = three[0:n] + (three[n : 2 * n] + three[2 * n :])
    primal_packed.push()
    for (low, high, first, last), there in zip(blocks_of(z), spread):
        arranged[:, low:high] = dot(half[:, first:last], there, precision=None).astype(BF16)


def invert(z, loads, padded, masks, local_tile, aug, small):
    diagonal = sum(dot(padded[f] * masks[f : f + 1], padded[f], (1, 1)) for f in range(4))
    row, col = iota((8, 128), 0), iota((8, 128), 1)
    aug[...] = jnp.where((col == row + 8) & (row < z.modes), 1.0, 0.0).astype(F32)
    aug[:, 0:8] = diagonal
    matrix = aug[...]
    for p in range(z.modes):
        scaled = matrix[p : p + 1, :] / matrix[p : p + 1, p : p + 1]
        taken = matrix[:, p : p + 1] - (row[:, 0:1] == p).astype(F32)
        matrix = matrix - taken * scaled
    inverse = matrix[:, 8:16]
    small[...] = jnp.zeros(small.shape, F32)
    for j in range(z.modes):
        small[j : j + 1, :] = loads[0, j]
    local_tile[...] = jnp.zeros(local_tile.shape, F32)
    local_tile[:, FIRST_LANE : FIRST_LANE + z.cases] = dot(inverse, small[...])
    local_tile[:, INVERSE_LANE : INVERSE_LANE + 8] = inverse


def couple(z, padded, masks, local_tile, got1, got0, got3, got2, sent, live_rows, lift_rows, tile):
    near = across_faces(z, (got0, got1, got2, got3))
    inverse = local_tile[:, INVERSE_LANE : INVERSE_LANE + 8]
    tile[...] = local_tile[...]
    for f in range(4):
        live = padded[f] * masks[f : f + 1]
        lift_rows[f] = jnp.concatenate([live * SIGNS[f], near[f] * masks[f : f + 1] * -SIGNS[f]], axis=0)
        tile[:, 8 * f : 8 * f + 8] = dot(inverse, dot(live, near[f], (1, 1)))
    sent[...] = jnp.broadcast_to(tile[...][None], sent.shape)
    sent.push()
    live_rows[...] = masks[...]


def lifted(z, amplitudes, lift_rows, f):
    pair = jnp.concatenate([amplitudes[0:8], amplitudes[8 * f + 8 : 8 * f + 16]], axis=0)
    return dot(pair, lift_rows[f], (0, 0))


def apply(z, faces, arranged, packed):
    packed[...] = jnp.zeros(packed.shape, F32)
    for f in range(4):
        wide = jnp.concatenate([faces[f], jnp.zeros((z.cases, z.width - z.lanes), F32)], axis=1)
        shift = f * z.face - z.starts[f]
        packed[:, z.starts[f] : z.starts[f] + z.width] += pltpu.roll(wide, shift, 1) if shift else wide
    return dot(packed[:, 0 : z.order].astype(BF16), arranged[...], precision=None)


def unpacked(z, values, packed):
    packed[:, 0 : z.order] = values
    found = []
    for f in range(4):
        part = packed[:, z.starts[f] : z.starts[f] + z.width]
        shift = f * z.face - z.starts[f]
        part = (pltpu.roll(part, z.width - shift, 1) if shift else part)[:, 0 : z.lanes]
        found.append(jnp.where(iota(part.shape, 1) < z.face, part, 0.0))
    return found


def send_coarse(z, faces, rows, scalars, sent, tile):
    tile[...] = jnp.zeros_like(tile)
    mine = jnp.zeros((8, z.cases), F32)
    for f in range(4):
        both = dot(rows[f], faces[f], (1, 1))
        mine = mine + both[0:8]
        tile[:, (1 + f) * z.cases : (2 + f) * z.cases] = both[8:16]
    tile[:, 0 : z.cases] = mine
    send_tile(tile[...], scalars, sent)


def send_tile(values, scalars, sent):
    row, col = iota((8, 128), 0), iota((8, 128), 1)
    for i, scalar in enumerate(scalars):
        values = jnp.where((row == 0) & (col == SCALAR_LANE + i), scalar, values)
    sent[...] = jnp.broadcast_to(values[None], sent.shape)
    sent.push()


def scalar_of(total, i):
    row, col = iota((8, 128), 0), iota((8, 128), 1)
    return jnp.sum(jnp.where((row == 0) & (col == SCALAR_LANE + i), total, 0.0), keepdims=True)


def received_window(z, received):
    ix, _ = place()
    start = window_start(z, ix) * z.ny
    return received[pl.ds(start, z.wide * z.ny)].reshape(z.rows, 128)


def coarse_amplitudes(z, received, solve_rows):
    values = received_window(z, received)
    start = values
    for f in range(4):
        across = pltpu.roll(values, 128 - (1 + (f ^ 1)) * z.cases, 1)
        step = 8 * z.steps[f]
        empty = jnp.zeros((abs(step), 128), F32)
        if step > 0:
            moved = jnp.concatenate([across[step:], empty], axis=0)
        else:
            moved = jnp.concatenate([empty, across[: z.rows + step]], axis=0)
        start = start - moved
    return dot(solve_rows[...], start)[:, 0 : z.cases]


def total(values):
    return jnp.sum(values, keepdims=True)


def face_weights(z):
    ix, iy = place()
    edges = (ix == 0, ix == z.nx - 1, iy == 0, iy == z.ny - 1)
    return [jnp.where(edge, 1.0, 0.5).astype(F32) for edge in edges]


def begin(
    z, lift_rows, primal, received, arranged,
    solve_rows, rows, multipliers, faces, sent, to0, to1, to2, to3,
    matrix, tile, packed,
):
    ix, iy = place()
    near_spots = spots(z, ix, iy)
    values = received_window(z, received)
    lane = iota((z.rows, 128), 1)
    row = iota((z.rows, 128), 0)
    tiled = []
    for f in range(4):
        part = jnp.where(lane // 8 == f, values, 0.0)
        for shift in (64, 32, 16, 8):
            part = part + pltpu.roll(part, shift, 1)
        tiled.append(part)
    for block in range(-(-z.rows // 128)):
        target = (lane + 128 * block) // 8 - row // 8
        part = jnp.zeros((z.rows, 128), F32)
        for f in range(4):
            part = part + jnp.where(target == z.steps[f], tiled[f], 0.0)
        matrix[:, 128 * block : 128 * block + 128] = part
    once = jnp.concatenate([matrix[pl.ds(pl.multiple_of(s * 8, 8), 8), 0 : z.rows] for s in near_spots], axis=0)
    twice = dot(once, matrix[:, 0 : z.rows])
    cols = z.rows
    unit = jnp.concatenate([
        (iota((8, cols), 1) == iota((8, cols), 0) + s * 8).astype(F32) for s in near_spots
    ], axis=0)
    solve = unit + once + twice
    solve_rows[...] = solve
    amplitudes = dot(solve, values)[:, FIRST_LANE : FIRST_LANE + z.cases]
    start = window_start(z, ix) * z.ny
    inverses = [received[pl.ds(start + spot, 1)][0][:, INVERSE_LANE : INVERSE_LANE + 8] for spot in near_spots]
    fields = []
    for f in range(4):
        both = lift_rows[f]
        own, near = both[0:8] * SIGNS[f], both[8:16] * -SIGNS[f]
        rows[f] = jnp.concatenate([dot(inverses[0], own), dot(inverses[1 + f], near)], axis=0)
        fields.append(lifted(z, amplitudes, lift_rows, f))
        multipliers[f] = fields[f]
    for item in (solve_rows, rows, multipliers):
        item.push()
    image = unpacked(z, primal[...] - apply(z, fields, arranged, packed), packed)
    for f in range(4):
        faces[f] = image[f]
    faces.push()
    send_faces(z, image, (to0, to1, to2, to3))
    send_coarse(z, image, rows, [], sent, tile)


def jumped(z, masks, faces, got):
    near = across_faces(z, got)
    return [masks[f : f + 1] * SIGNS[f] * (faces[f] - near[f]) for f in range(4)]


def first_direction(
    z, solve_rows, lift_rows, faces, masks, rows, got1, got0, got3, got2, received, arranged,
    residual, direction, image, sent, to0, to1, to2, to3,
    tile, packed,
):
    amplitudes = coarse_amplitudes(z, received, solve_rows)
    field = jumped(z, masks, faces, (got0, got1, got2, got3))
    weights = face_weights(z)
    moved = [field[f] - lifted(z, amplitudes, lift_rows, f) for f in range(4)]
    for f in range(4):
        residual[f] = field[f]
        direction[f] = moved[f]
    residual.push()
    direction.push()
    found = unpacked(z, apply(z, moved, arranged, packed), packed)
    for f in range(4):
        image[f] = found[f]
    image.push()
    gamma = sum(weights[f] * total(field[f] * moved[f]) for f in range(4))
    curvature = sum(SIGNS[f] * total(moved[f] * found[f]) for f in range(4))
    send_faces(z, found, (to0, to1, to2, to3))
    send_coarse(z, found, rows, [gamma, curvature], sent, tile)


def second_direction(
    z, solve_rows, lift_rows, faces, masks, residual, direction, multipliers,
    got1, got0, got3, got2, received, arranged,
    next_multipliers, next_residual, projected, image, fresh, sums, sent, to0, to1, to2, to3,
    packed,
):
    amplitudes = coarse_amplitudes(z, received, solve_rows)
    summed = jnp.sum(received[...], axis=0)
    sums[...] = summed
    alpha = scalar_of(summed, 0) / scalar_of(summed, 1)
    field = jumped(z, masks, faces, (got0, got1, got2, got3))
    weights = face_weights(z)
    left, moved = [], []
    for f in range(4):
        image[f] = field[f]
        next_multipliers[f] = multipliers[f] + alpha * direction[f]
        left.append(residual[f] - alpha * field[f])
        moved.append(direction[f] - alpha * (field[f] - lifted(z, amplitudes, lift_rows, f)))
        next_residual[f] = left[f]
        projected[f] = moved[f]
    for item in (sums, image, next_multipliers, next_residual, projected):
        item.push()
    found = unpacked(z, apply(z, moved, arranged, packed), packed)
    for f in range(4):
        fresh[f] = found[f]
    fresh.push()
    send_faces(z, found, (to0, to1, to2, to3))
    gamma = sum(weights[f] * total(left[f] * moved[f]) for f in range(4))
    straight = sum(SIGNS[f] * total(moved[f] * found[f]) for f in range(4))
    crossed = sum(
        weights[f] * total(moved[f] * field[f]) + SIGNS[f] * total(direction[f] * found[f]) for f in range(4)
    )
    send_tile(jnp.zeros((8, 128), F32), [gamma, straight, crossed], sent)


def finish(
    z, sums, faces, masks, residual, image, multipliers, projected, direction,
    got1, got0, got3, got2, received,
    out_multipliers, out_residual,
):
    summed = jnp.sum(received[...], axis=0)
    field = jumped(z, masks, faces, (got0, got1, got2, got3))
    gamma, curvature = scalar_of(sums[...], 0), scalar_of(sums[...], 1)
    fresh, straight, crossed = (scalar_of(summed, i) for i in range(3))
    beta = fresh / gamma
    alpha = fresh / (straight + beta * crossed + beta * beta * curvature)
    for f in range(4):
        step = projected[f] + beta * direction[f]
        out_multipliers[0, 0, f] = (multipliers[f] + alpha * step)[:, 0 : z.face]
        out_residual[0, 0, f] = (residual[f] - alpha * (field[f] + beta * image[f]))[:, 0 : z.face]


class Coming:
    def __init__(self, source, held, semaphore):
        self.held = held
        self.copy = pltpu.make_async_copy(source, held, semaphore)
        self.copy.start()

    def ready(self):
        if self.copy is not None:
            self.copy.wait()
            self.copy = None
        return self.held

    def __getitem__(self, index):
        return self.ready()[index]


class Going:
    def __init__(self, held, target, semaphore):
        self.held = held
        self.copy = pltpu.make_async_copy(held, target, semaphore)
        self.shape, self.dtype = held.shape, held.dtype
        self.started = False

    def __getitem__(self, index):
        return self.held[index]

    def __setitem__(self, index, values):
        self.held[index] = values

    def push(self):
        if not self.started:
            self.copy.start()
            self.started = True


def call(z, kernel, outs, args, scratch=(), flops=0, near=0, kept=0):
    shapes = [jax.ShapeDtypeStruct(shape, dtype) for shape, dtype in outs]
    moved = sum(a.size * a.dtype.itemsize for a in args) + sum(s.size * s.dtype.itemsize for s in shapes)
    far, sent = len(args) - near, len(outs) - kept

    def run(*refs):
        refs = list(refs)
        take = lambda n: [refs.pop(0) for _ in range(n)]
        sources, others, targets, direct = take(far), take(near), take(sent), take(kept)
        held, made, work = take(far), take(sent), take(len(scratch))
        coming = [Coming(a, b, refs[0].at[i]) for i, (a, b) in enumerate(zip(sources, held))]
        going = [Going(a, b, refs[0].at[far + i]) for i, (a, b) in enumerate(zip(made, targets))]
        kernel(z, *coming, *others, *going, *direct, *work)
        for item in going:
            item.push()
        for item in coming:
            item.ready()
        for item in going:
            item.copy.wait()

    near_spec = lambda a: pl.BlockSpec(memory_space=SMEM if a.ndim == 3 and a.size == 4 else VMEM)
    far_spec = pl.BlockSpec(memory_space=pltpu.HBM)
    buffers = [(SMEM if a.size == 4 else VMEM)(a.shape, a.dtype) for a in list(args[:far]) + shapes[:sent]]
    semaphores = [pltpu.SemaphoreType.DMA((far + sent,))] if far + sent else []
    return pl.pallas_call(
        run,
        out_shape=[pltpu.HBM(a.shape, a.dtype) for a in shapes[:sent]] + shapes[sent:],
        in_specs=[far_spec] * far + [near_spec(a) for a in args[far:]],
        out_specs=[far_spec] * sent + [near_spec(a) for a in shapes[sent:]],
        scratch_shapes=buffers + [VMEM(shape, dtype) for shape, dtype in scratch] + semaphores,
        compiler_params=pltpu.CompilerParams(vmem_limit_bytes=24 * 2**20),
        cost_estimate=pl.CostEstimate(flops=flops, bytes_accessed=moved, transcendentals=0),
        name=kernel.__name__,
    )(*[pltpu.with_memory_space_constraint(a, pltpu.HBM) for a in args[:far]], *args[far:])


def gather(values):
    return lax.all_to_all(values, AXES, 0, 0, tiled=True)


def body(ops, traces, primal, loads, maps, counts):
    z = Sizes(lax.axis_size("gx"), lax.axis_size("gy"), traces, loads)
    field = ((4, z.cases, z.lanes), F32)
    mode_rows = ((4, 8, z.lanes), F32)
    pair_rows = ((4, 16, z.lanes), F32)
    live_rows = ((8, z.lanes), F32)
    tile = ((8, 128), F32)
    sent = ((z.count, 8, 128), F32)
    to_faces = [((z.cases, z.lanes), F32)] * 4
    columns = -(-z.rows // 128) * 128
    product_flops = 2 * z.cases * z.order**2

    padded, masks, *trace_faces = call(
        z, prepare, [mode_rows, live_rows] + [((8, z.lanes), F32)] * 4,
        [jnp.transpose(traces, (0, 1, 3, 2, 4)), counts], kept=6,
    )
    got = exchange(trace_faces)
    (local_tile,) = call(
        z, invert, [tile], [jnp.transpose(loads, (0, 2, 1, 3)), padded, masks],
        [tile, ((8, z.cases), F32)], product_flops, near=2, kept=1,
    )
    blocks, masks, lift_rows = call(
        z, couple, [sent, live_rows, pair_rows], [padded, masks, local_tile, *got], [tile], near=7,
    )
    blocks = gather(blocks)
    packed = ((z.cases, z.padded), F32)
    primal_packed, arranged = call(
        z, arrange, [((z.cases, z.order), F32), ((z.order, z.order), BF16)], [maps, ops, primal],
        [((8, z.padded), jnp.int32), ((z.order, z.order), BF16)], 4 * z.order**2 * z.width, kept=1,
    )
    solve_rows, rows, multipliers, faces, coarse, *sent_faces = call(
        z, begin, [((40, z.rows), F32), pair_rows, field, field, sent] + to_faces,
        [lift_rows, primal_packed, blocks, arranged],
        [((z.rows, columns), F32), tile, packed], product_flops, near=2,
    )
    coarse, got = gather(coarse), exchange(sent_faces)
    residual, direction, faces, coarse, *sent_faces = call(
        z, first_direction, [field, field, field, sent] + to_faces,
        [solve_rows, lift_rows, faces, masks, rows, *got, coarse, arranged],
        [tile, packed], product_flops, near=6,
    )
    coarse, got = gather(coarse), exchange(sent_faces)
    multipliers, residual, projected, image, faces, sums, coarse, *sent_faces = call(
        z, second_direction, [field, field, field, field, field, tile, sent] + to_faces,
        [solve_rows, lift_rows, faces, masks, residual, direction, multipliers, *got, coarse, arranged],
        [packed], product_flops, near=6,
    )
    coarse, got = gather(coarse), exchange(sent_faces)
    whole = ((1, 1, 4, z.cases, z.face), F32)
    multipliers, residual = call(
        z, finish, [whole, whole],
        [sums, faces, masks, residual, image, multipliers, projected, direction, *got, coarse], near=5,
    )
    return multipliers, residual


def solution(mesh):
    in_specs = (
        P("gx", "gy", None, None),
        P("gx", "gy", None, None, None),
        P("gx", "gy", None, None),
        P("gx", "gy", None, None),
        P("gx", "gy", None, None),
        P("gx", "gy", None),
    )
    out_specs = (P("gx", "gy", None, None, None), P("gx", "gy", None, None, None))
    return jax.shard_map(body, mesh=mesh, in_specs=in_specs, out_specs=out_specs, check_vma=False)
```

```python
import functools

import jax
import jax.numpy as jnp
from jax import lax
from jax.experimental import pallas as pl
from jax.experimental.pallas import tpu as pltpu
from jax.sharding import PartitionSpec as P

SIGNS = (-1.0, 1.0, -1.0, 1.0)
HIGHEST = lax.Precision.HIGHEST
AXES = ("gx", "gy")
F32 = jnp.float32
BF16 = jnp.bfloat16
VMEM = pltpu.VMEM
SMEM = pltpu.SMEM
FIRST_LANE = 32
INVERSE_LANE = 48
SCALAR_LANE = 96
BLOCK = 256
SWAPS = (1, 3, 0, 2)


class Sizes:
    def __init__(self, nx, ny, traces, loads):
        self.nx, self.ny = nx, ny
        self.count = nx * ny
        self.modes, self.face = traces.shape[-2:]
        self.cases = loads.shape[-1]
        self.order = 4 * self.face
        self.lanes = -(-self.face // 128) * 128
        self.starts = [f * self.face // 128 * 128 for f in range(4)]
        ends = [-(-(f + 1) * self.face // 128) * 128 for f in range(4)]
        self.width = max(e - s for s, e in zip(self.starts, ends))
        self.padded = max(s + self.width for s in self.starts)
        self.wide = min(nx, 9)
        self.rows = self.wide * ny * 8
        self.steps = (-ny, ny, -1, 1)


def dot(a, b, contract=(1, 0), precision=HIGHEST):
    dims = (((contract[0],), (contract[1],)), ((), ()))
    return lax.dot_general(a, b, dims, precision=precision, preferred_element_type=F32)


def iota(shape, dim):
    return lax.broadcasted_iota(jnp.int32, shape, dim)


def place():
    return lax.axis_index("gx"), lax.axis_index("gy")


def window_start(z, ix):
    return jnp.clip(ix - 4, 0, z.nx - z.wide) if z.wide < z.nx else 0


def spots(z, ix, iy):
    own = (ix - window_start(z, ix)) * z.ny + iy
    return [own] + [jnp.clip(own + step, 0, z.wide * z.ny - 1) for step in z.steps]


def send_faces(z, faces, sent):
    for i, at in enumerate(place()):
        even = at % 2 == 0
        low, high = faces[2 * i], faces[2 * i + 1]
        sent[2 * i][...] = jnp.where(even, high, low)
        sent[2 * i + 1][...] = jnp.where(even, low, high)
        sent[2 * i].push()
        sent[2 * i + 1].push()


def across_faces(z, got):
    found = []
    for i, at in enumerate(place()):
        even = at % 2 == 0
        first, second = got[2 * i][...], got[2 * i + 1][...]
        found += [jnp.where(even, second, first), jnp.where(even, first, second)]
    return found


def exchange(sent):
    got = []
    for i in SWAPS:
        axis = AXES[i // 2]
        pairs = []
        for low in range(i % 2, lax.axis_size(axis) - 1, 2):
            pairs += [(low, low + 1), (low + 1, low)]
        got.append(lax.ppermute(sent[i], axis, pairs))
    return got


def prepare(z, traces, counts, padded, masks, *sent):
    padded[...] = jnp.zeros(padded.shape, F32)
    for f in range(4):
        for j in range(z.modes):
            padded[f, j : j + 1, 0 : z.face] = traces[0, 0, j, f : f + 1]
    for i, at in enumerate(place()):
        even = at % 2 == 0
        low, high = padded[2 * i], padded[2 * i + 1]
        sent[2 * i][...] = jnp.where(even, high, low)
        sent[2 * i + 1][...] = jnp.where(even, low, high)
    row, lane = iota(masks.shape, 0), iota(masks.shape, 1)
    live = jnp.zeros(masks.shape, F32)
    for f in range(4):
        live = jnp.where((row == f) & (lane < counts[0, 0, f]), 1.0, live)
    masks[...] = live


def blocks_of(z):
    found = []
    for low in range(0, z.order, BLOCK):
        high = min(low + BLOCK, z.order)
        first, last = low // z.face, (high - 1) // z.face
        found.append((low, high, first * z.face // 128 * 128, min(-(-(last + 1) * z.face // 128) * 128, z.order)))
    return found


def arrange(z, maps, ops, primal, primal_packed, arranged, flat, half):
    flat[...] = jnp.zeros_like(flat)
    flat[0:4, 0 : z.face] = maps[0, 0]
    lane = iota((1, z.padded), 1)
    line = jnp.full((1, z.padded), -1, jnp.int32)
    signs = jnp.zeros((1, z.padded), F32)
    for f in range(4):
        moved = pltpu.roll(flat[...], f * z.face, 1)[f : f + 1] if f else flat[0:1]
        here = (lane >= f * z.face) & (lane < (f + 1) * z.face)
        line = jnp.where(here, moved + f * z.face, line)
        signs = jnp.where(here, SIGNS[f], signs)
    column = jnp.transpose(jnp.broadcast_to(line, (8, z.padded)))[:, 0:1]
    spread = []
    for low, high, first, last in blocks_of(z):
        hit = (iota((last - first, high - low), 1) + low) == column[first:last]
        spread.append(hit.astype(F32).astype(BF16))
    for low, high, first, last in blocks_of(z):
        hit = (iota((high - low, last - first), 0) + low) == line[:, first:last]
        collect = jnp.where(hit, signs[:, first:last], 0.0).astype(BF16)
        half[low:high, :] = dot(collect, ops[0, 0, first:last, :], precision=None).astype(BF16)
    values = primal[0, 0]
    parts = []
    for _ in range(3):
        parts.append(values.astype(BF16))
        values = values - parts[-1].astype(F32)
    pieces = jnp.concatenate(parts, axis=0)
    n = z.cases
    for (low, high, first, last), there in zip(blocks_of(z), spread):
        three = dot(pieces[:, first:last], there, precision=None)
        primal_packed[:, low:high] = three[0:n] + (three[n : 2 * n] + three[2 * n :])
    primal_packed.push()
    for (low, high, first, last), there in zip(blocks_of(z), spread):
        arranged[:, low:high] = dot(half[:, first:last], there, precision=None).astype(BF16)


def invert(z, loads, padded, masks, local_tile, aug, small):
    diagonal = sum(dot(padded[f] * masks[f : f + 1], padded[f], (1, 1)) for f in range(4))
    row, col = iota((8, 128), 0), iota((8, 128), 1)
    aug[...] = jnp.where((col == row + 8) & (row < z.modes), 1.0, 0.0).astype(F32)
    aug[:, 0:8] = diagonal
    matrix = aug[...]
    for p in range(z.modes):
        scaled = matrix[p : p + 1, :] / matrix[p : p + 1, p : p + 1]
        taken = matrix[:, p : p + 1] - (row[:, 0:1] == p).astype(F32)
        matrix = matrix - taken * scaled
    inverse = matrix[:, 8:16]
    small[...] = jnp.zeros(small.shape, F32)
    for j in range(z.modes):
        small[j : j + 1, :] = loads[0, j]
    local_tile[...] = jnp.zeros(local_tile.shape, F32)
    local_tile[:, FIRST_LANE : FIRST_LANE + z.cases] = dot(inverse, small[...])
    local_tile[:, INVERSE_LANE : INVERSE_LANE + 8] = inverse


def couple(z, padded, masks, local_tile, got1, got3, got0, got2, sent, live_rows, lift_rows, tile):
    near = across_faces(z, (got0, got1, got2, got3))
    inverse = local_tile[:, INVERSE_LANE : INVERSE_LANE + 8]
    tile[...] = local_tile[...]
    for f in range(4):
        live = padded[f] * masks[f : f + 1]
        lift_rows[f] = jnp.concatenate([live * SIGNS[f], near[f] * masks[f : f + 1] * -SIGNS[f]], axis=0)
        tile[:, 8 * f : 8 * f + 8] = dot(inverse, dot(live, near[f], (1, 1)))
    sent[...] = jnp.broadcast_to(tile[...][None], sent.shape)
    sent.push()
    live_rows[...] = masks[...]


def lifted(z, amplitudes, lift_rows, f):
    pair = jnp.concatenate([amplitudes[0:8], amplitudes[8 * f + 8 : 8 * f + 16]], axis=0)
    return dot(pair, lift_rows[f], (0, 0))


def apply(z, faces, arranged, packed):
    packed[...] = jnp.zeros(packed.shape, F32)
    for f in range(4):
        wide = jnp.concatenate([faces[f], jnp.zeros((z.cases, z.width - z.lanes), F32)], axis=1)
        shift = f * z.face - z.starts[f]
        packed[:, z.starts[f] : z.starts[f] + z.width] += pltpu.roll(wide, shift, 1) if shift else wide
    return dot(packed[:, 0 : z.order].astype(BF16), arranged[...], precision=None)


def unpacked(z, values, packed):
    packed[:, 0 : z.order] = values
    found = []
    for f in range(4):
        part = packed[:, z.starts[f] : z.starts[f] + z.width]
        shift = f * z.face - z.starts[f]
        part = (pltpu.roll(part, z.width - shift, 1) if shift else part)[:, 0 : z.lanes]
        found.append(jnp.where(iota(part.shape, 1) < z.face, part, 0.0))
    return found


def send_coarse(z, faces, rows, scalars, sent, tile):
    tile[...] = jnp.zeros_like(tile)
    mine = jnp.zeros((8, z.cases), F32)
    for f in range(4):
        both = dot(rows[f], faces[f], (1, 1))
        mine = mine + both[0:8]
        tile[:, (1 + f) * z.cases : (2 + f) * z.cases] = both[8:16]
    tile[:, 0 : z.cases] = mine
    send_tile(tile[...], scalars, sent)


def send_tile(values, scalars, sent):
    row, col = iota((8, 128), 0), iota((8, 128), 1)
    for i, scalar in enumerate(scalars):
        values = jnp.where((row == 0) & (col == SCALAR_LANE + i), scalar, values)
    sent[...] = jnp.broadcast_to(values[None], sent.shape)
    sent.push()


def scalar_of(total, i):
    row, col = iota((8, 128), 0), iota((8, 128), 1)
    return jnp.sum(jnp.where((row == 0) & (col == SCALAR_LANE + i), total, 0.0), keepdims=True)


def received_window(z, received):
    ix, _ = place()
    start = window_start(z, ix) * z.ny
    return received[pl.ds(start, z.wide * z.ny)].reshape(z.rows, 128)


def coarse_amplitudes(z, received, solve_rows):
    values = received_window(z, received)
    start = values
    for f in range(4):
        across = pltpu.roll(values, 128 - (1 + (f ^ 1)) * z.cases, 1)
        step = 8 * z.steps[f]
        empty = jnp.zeros((abs(step), 128), F32)
        if step > 0:
            moved = jnp.concatenate([across[step:], empty], axis=0)
        else:
            moved = jnp.concatenate([empty, across[: z.rows + step]], axis=0)
        start = start - moved
    return dot(solve_rows[...], start)[:, 0 : z.cases]


def total(values):
    return jnp.sum(values, keepdims=True)


def face_weights(z):
    ix, iy = place()
    edges = (ix == 0, ix == z.nx - 1, iy == 0, iy == z.ny - 1)
    return [jnp.where(edge, 1.0, 0.5).astype(F32) for edge in edges]


def begin(
    z, lift_rows, primal, received, arranged,
    solve_rows, rows, multipliers, faces, sent, to0, to1, to2, to3,
    matrix, tile, packed,
):
    ix, iy = place()
    near_spots = spots(z, ix, iy)
    values = received_window(z, received)
    lane = iota((z.rows, 128), 1)
    row = iota((z.rows, 128), 0)
    tiled = []
    for f in range(4):
        part = jnp.where(lane // 8 == f, values, 0.0)
        for shift in (64, 32, 16, 8):
            part = part + pltpu.roll(part, shift, 1)
        tiled.append(part)
    for block in range(-(-z.rows // 128)):
        target = (lane + 128 * block) // 8 - row // 8
        part = jnp.zeros((z.rows, 128), F32)
        for f in range(4):
            part = part + jnp.where(target == z.steps[f], tiled[f], 0.0)
        matrix[:, 128 * block : 128 * block + 128] = part
    once = jnp.concatenate([matrix[pl.ds(pl.multiple_of(s * 8, 8), 8), 0 : z.rows] for s in near_spots], axis=0)
    twice = dot(once, matrix[:, 0 : z.rows])
    cols = z.rows
    unit = jnp.concatenate([
        (iota((8, cols), 1) == iota((8, cols), 0) + s * 8).astype(F32) for s in near_spots
    ], axis=0)
    solve = unit + once + twice
    solve_rows[...] = solve
    amplitudes = dot(solve, values)[:, FIRST_LANE : FIRST_LANE + z.cases]
    start = window_start(z, ix) * z.ny
    inverses = [received[pl.ds(start + spot, 1)][0][:, INVERSE_LANE : INVERSE_LANE + 8] for spot in near_spots]
    fields = []
    for f in range(4):
        both = lift_rows[f]
        own, near = both[0:8] * SIGNS[f], both[8:16] * -SIGNS[f]
        rows[f] = jnp.concatenate([dot(inverses[0], own), dot(inverses[1 + f], near)], axis=0)
        fields.append(lifted(z, amplitudes, lift_rows, f))
        multipliers[f] = fields[f]
    for item in (solve_rows, rows, multipliers):
        item.push()
    image = unpacked(z, primal[...] - apply(z, fields, arranged, packed), packed)
    for f in range(4):
        faces[f] = image[f]
    faces.push()
    send_faces(z, image, (to0, to1, to2, to3))
    send_coarse(z, image, rows, [], sent, tile)


def jumped(z, masks, faces, got):
    near = across_faces(z, got)
    return [masks[f : f + 1] * SIGNS[f] * (faces[f] - near[f]) for f in range(4)]


def first_direction(
    z, solve_rows, lift_rows, faces, masks, rows, got1, got3, got0, got2, received, arranged,
    residual, direction, image, sent, to0, to1, to2, to3,
    tile, packed,
):
    amplitudes = coarse_amplitudes(z, received, solve_rows)
    field = jumped(z, masks, faces, (got0, got1, got2, got3))
    weights = face_weights(z)
    moved = [field[f] - lifted(z, amplitudes, lift_rows, f) for f in range(4)]
    for f in range(4):
        residual[f] = field[f]
        direction[f] = moved[f]
    residual.push()
    direction.push()
    found = unpacked(z, apply(z, moved, arranged, packed), packed)
    for f in range(4):
        image[f] = found[f]
    image.push()
    gamma = sum(weights[f] * total(field[f] * moved[f]) for f in range(4))
    curvature = sum(SIGNS[f] * total(moved[f] * found[f]) for f in range(4))
    send_faces(z, found, (to0, to1, to2, to3))
    send_coarse(z, found, rows, [gamma, curvature], sent, tile)


def second_direction(
    z, solve_rows, lift_rows, faces, masks, residual, direction, multipliers,
    got1, got3, got0, got2, received, arranged,
    next_multipliers, next_residual, projected, image, fresh, sums, sent, to0, to1, to2, to3,
    packed,
):
    amplitudes = coarse_amplitudes(z, received, solve_rows)
    summed = jnp.sum(received[...], axis=0)
    sums[...] = summed
    alpha = scalar_of(summed, 0) / scalar_of(summed, 1)
    field = jumped(z, masks, faces, (got0, got1, got2, got3))
    weights = face_weights(z)
    left, moved = [], []
    for f in range(4):
        image[f] = field[f]
        next_multipliers[f] = multipliers[f] + alpha * direction[f]
        left.append(residual[f] - alpha * field[f])
        moved.append(direction[f] - alpha * (field[f] - lifted(z, amplitudes, lift_rows, f)))
        next_residual[f] = left[f]
        projected[f] = moved[f]
    for item in (sums, image, next_multipliers, next_residual, projected):
        item.push()
    found = unpacked(z, apply(z, moved, arranged, packed), packed)
    for f in range(4):
        fresh[f] = found[f]
    fresh.push()
    send_faces(z, found, (to0, to1, to2, to3))
    gamma = sum(weights[f] * total(left[f] * moved[f]) for f in range(4))
    straight = sum(SIGNS[f] * total(moved[f] * found[f]) for f in range(4))
    crossed = sum(
        weights[f] * total(moved[f] * field[f]) + SIGNS[f] * total(direction[f] * found[f]) for f in range(4)
    )
    send_tile(jnp.zeros((8, 128), F32), [gamma, straight, crossed], sent)


def finish(
    z, sums, faces, masks, residual, image, multipliers, projected, direction,
    got1, got3, got0, got2, received,
    out_multipliers, out_residual,
):
    summed = jnp.sum(received[...], axis=0)
    field = jumped(z, masks, faces, (got0, got1, got2, got3))
    gamma, curvature = scalar_of(sums[...], 0), scalar_of(sums[...], 1)
    fresh, straight, crossed = (scalar_of(summed, i) for i in range(3))
    beta = fresh / gamma
    alpha = fresh / (straight + beta * crossed + beta * beta * curvature)
    for f in range(4):
        step = projected[f] + beta * direction[f]
        out_multipliers[0, 0, f] = (multipliers[f] + alpha * step)[:, 0 : z.face]
        out_residual[0, 0, f] = (residual[f] - alpha * (field[f] + beta * image[f]))[:, 0 : z.face]


class Coming:
    def __init__(self, source, held, semaphore):
        self.held = held
        self.copy = pltpu.make_async_copy(source, held, semaphore)
        self.copy.start()

    def ready(self):
        if self.copy is not None:
            self.copy.wait()
            self.copy = None
        return self.held

    def __getitem__(self, index):
        return self.ready()[index]


class Going:
    def __init__(self, held, target, semaphore):
        self.held = held
        self.copy = pltpu.make_async_copy(held, target, semaphore)
        self.shape, self.dtype = held.shape, held.dtype
        self.started = False

    def __getitem__(self, index):
        return self.held[index]

    def __setitem__(self, index, values):
        self.held[index] = values

    def push(self):
        if not self.started:
            self.copy.start()
            self.started = True


def call(z, kernel, outs, args, scratch=(), flops=0, near=0, kept=0):
    shapes = [jax.ShapeDtypeStruct(shape, dtype) for shape, dtype in outs]
    moved = sum(a.size * a.dtype.itemsize for a in args) + sum(s.size * s.dtype.itemsize for s in shapes)
    far, sent = len(args) - near, len(outs) - kept

    def run(*refs):
        refs = list(refs)
        take = lambda n: [refs.pop(0) for _ in range(n)]
        sources, others, targets, direct = take(far), take(near), take(sent), take(kept)
        held, made, work = take(far), take(sent), take(len(scratch))
        coming = [Coming(a, b, refs[0].at[i]) for i, (a, b) in enumerate(zip(sources, held))]
        going = [Going(a, b, refs[0].at[far + i]) for i, (a, b) in enumerate(zip(made, targets))]
        kernel(z, *coming, *others, *going, *direct, *work)
        for item in going:
            item.push()
        for item in coming:
            item.ready()
        for item in going:
            item.copy.wait()

    near_spec = lambda a: pl.BlockSpec(memory_space=SMEM if a.ndim == 3 and a.size == 4 else VMEM)
    far_spec = pl.BlockSpec(memory_space=pltpu.HBM)
    buffers = [(SMEM if a.size == 4 else VMEM)(a.shape, a.dtype) for a in list(args[:far]) + shapes[:sent]]
    semaphores = [pltpu.SemaphoreType.DMA((far + sent,))] if far + sent else []
    return pl.pallas_call(
        run,
        out_shape=[pltpu.HBM(a.shape, a.dtype) for a in shapes[:sent]] + shapes[sent:],
        in_specs=[far_spec] * far + [near_spec(a) for a in args[far:]],
        out_specs=[far_spec] * sent + [near_spec(a) for a in shapes[sent:]],
        scratch_shapes=buffers + [VMEM(shape, dtype) for shape, dtype in scratch] + semaphores,
        compiler_params=pltpu.CompilerParams(vmem_limit_bytes=24 * 2**20),
        cost_estimate=pl.CostEstimate(flops=flops, bytes_accessed=moved, transcendentals=0),
        name=kernel.__name__,
    )(*[pltpu.with_memory_space_constraint(a, pltpu.HBM) for a in args[:far]], *args[far:])


def gather(values):
    return lax.all_to_all(values, AXES, 0, 0, tiled=True)


def body(ops, traces, primal, loads, maps, counts):
    z = Sizes(lax.axis_size("gx"), lax.axis_size("gy"), traces, loads)
    field = ((4, z.cases, z.lanes), F32)
    mode_rows = ((4, 8, z.lanes), F32)
    pair_rows = ((4, 16, z.lanes), F32)
    live_rows = ((8, z.lanes), F32)
    tile = ((8, 128), F32)
    sent = ((z.count, 8, 128), F32)
    to_faces = [((z.cases, z.lanes), F32)] * 4
    columns = -(-z.rows // 128) * 128
    product_flops = 2 * z.cases * z.order**2

    padded, masks, *trace_faces = call(
        z, prepare, [mode_rows, live_rows] + [((8, z.lanes), F32)] * 4,
        [jnp.transpose(traces, (0, 1, 3, 2, 4)), counts], kept=6,
    )
    got = exchange(trace_faces)
    (local_tile,) = call(
        z, invert, [tile], [jnp.transpose(loads, (0, 2, 1, 3)), padded, masks],
        [tile, ((8, z.cases), F32)], product_flops, near=2, kept=1,
    )
    blocks, masks, lift_rows = call(
        z, couple, [sent, live_rows, pair_rows], [padded, masks, local_tile, *got], [tile], near=7,
    )
    blocks = gather(blocks)
    packed = ((z.cases, z.padded), F32)
    primal_packed, arranged = call(
        z, arrange, [((z.cases, z.order), F32), ((z.order, z.order), BF16)], [maps, ops, primal],
        [((8, z.padded), jnp.int32), ((z.order, z.order), BF16)], 4 * z.order**2 * z.width, kept=1,
    )
    solve_rows, rows, multipliers, faces, coarse, *sent_faces = call(
        z, begin, [((40, z.rows), F32), pair_rows, field, field, sent] + to_faces,
        [lift_rows, primal_packed, blocks, arranged],
        [((z.rows, columns), F32), tile, packed], product_flops, near=2,
    )
    coarse, got = gather(coarse), exchange(sent_faces)
    residual, direction, faces, coarse, *sent_faces = call(
        z, first_direction, [field, field, field, sent] + to_faces,
        [solve_rows, lift_rows, faces, masks, rows, *got, coarse, arranged],
        [tile, packed], product_flops, near=6,
    )
    coarse, got = gather(coarse), exchange(sent_faces)
    multipliers, residual, projected, image, faces, sums, coarse, *sent_faces = call(
        z, second_direction, [field, field, field, field, field, tile, sent] + to_faces,
        [solve_rows, lift_rows, faces, masks, residual, direction, multipliers, *got, coarse, arranged],
        [packed], product_flops, near=6,
    )
    coarse, got = gather(coarse), exchange(sent_faces)
    whole = ((1, 1, 4, z.cases, z.face), F32)
    multipliers, residual = call(
        z, finish, [whole, whole],
        [sums, faces, masks, residual, image, multipliers, projected, direction, *got, coarse], near=5,
    )
    return multipliers, residual


def solution(mesh):
    in_specs = (
        P("gx", "gy", None, None),
        P("gx", "gy", None, None, None),
        P("gx", "gy", None, None),
        P("gx", "gy", None, None),
        P("gx", "gy", None, None),
        P("gx", "gy", None),
    )
    out_specs = (P("gx", "gy", None, None, None), P("gx", "gy", None, None, None))
    return jax.shard_map(body, mesh=mesh, in_specs=in_specs, out_specs=out_specs, check_vma=False)
```

```python
import functools

import jax
import jax.numpy as jnp
from jax import lax
from jax.experimental import pallas as pl
from jax.experimental.pallas import tpu as pltpu
from jax.sharding import PartitionSpec as P

SIGNS = (-1.0, 1.0, -1.0, 1.0)
HIGHEST = lax.Precision.HIGHEST
AXES = ("gx", "gy")
F32 = jnp.float32
BF16 = jnp.bfloat16
VMEM = pltpu.VMEM
SMEM = pltpu.SMEM
FIRST_LANE = 32
INVERSE_LANE = 48
SCALAR_LANE = 96
BLOCK = 256
SWAPS = (1, 3, 0, 2)


class Sizes:
    def __init__(self, nx, ny, traces, loads):
        self.nx, self.ny = nx, ny
        self.count = nx * ny
        self.modes, self.face = traces.shape[-2:]
        self.cases = loads.shape[-1]
        self.order = 4 * self.face
        self.lanes = -(-self.face // 128) * 128
        self.starts = [f * self.face // 128 * 128 for f in range(4)]
        ends = [-(-(f + 1) * self.face // 128) * 128 for f in range(4)]
        self.width = max(e - s for s, e in zip(self.starts, ends))
        self.padded = max(s + self.width for s in self.starts)
        self.wide = min(nx, 9)
        self.rows = self.wide * ny * 8
        self.steps = (-ny, ny, -1, 1)


def dot(a, b, contract=(1, 0), precision=HIGHEST):
    dims = (((contract[0],), (contract[1],)), ((), ()))
    return lax.dot_general(a, b, dims, precision=precision, preferred_element_type=F32)


def iota(shape, dim):
    return lax.broadcasted_iota(jnp.int32, shape, dim)


def place():
    return lax.axis_index("gx"), lax.axis_index("gy")


def window_start(z, ix):
    return jnp.clip(ix - 4, 0, z.nx - z.wide) if z.wide < z.nx else 0


def spots(z, ix, iy):
    own = (ix - window_start(z, ix)) * z.ny + iy
    return [own] + [jnp.clip(own + step, 0, z.wide * z.ny - 1) for step in z.steps]


def send_faces(z, faces, sent):
    for i, at in enumerate(place()):
        even = at % 2 == 0
        low, high = faces[2 * i], faces[2 * i + 1]
        sent[2 * i][...] = jnp.where(even, high, low)
        sent[2 * i + 1][...] = jnp.where(even, low, high)
        sent[2 * i].push()
        sent[2 * i + 1].push()


def across_faces(z, got):
    found = []
    for i, at in enumerate(place()):
        even = at % 2 == 0
        first, second = got[2 * i][...], got[2 * i + 1][...]
        found += [jnp.where(even, second, first), jnp.where(even, first, second)]
    return found


def exchange(sent):
    got = []
    for i in SWAPS:
        axis = AXES[i // 2]
        pairs = []
        for low in range(i % 2, lax.axis_size(axis) - 1, 2):
            pairs += [(low, low + 1), (low + 1, low)]
        got.append(lax.ppermute(sent[i], axis, pairs))
    return got


def prepare(z, traces, counts, padded, masks, *sent):
    padded[...] = jnp.zeros(padded.shape, F32)
    for f in range(4):
        for j in range(z.modes):
            padded[f, j : j + 1, 0 : z.face] = traces[0, 0, j, f : f + 1]
    for i, at in enumerate(place()):
        even = at % 2 == 0
        low, high = padded[2 * i], padded[2 * i + 1]
        sent[2 * i][...] = jnp.where(even, high, low)
        sent[2 * i + 1][...] = jnp.where(even, low, high)
    row, lane = iota(masks.shape, 0), iota(masks.shape, 1)
    live = jnp.zeros(masks.shape, F32)
    for f in range(4):
        live = jnp.where((row == f) & (lane < counts[0, 0, f]), 1.0, live)
    masks[...] = live


def blocks_of(z):
    found = []
    for low in range(0, z.order, BLOCK):
        high = min(low + BLOCK, z.order)
        first, last = low // z.face, (high - 1) // z.face
        found.append((low, high, first * z.face // 128 * 128, min(-(-(last + 1) * z.face // 128) * 128, z.order)))
    return found


def arrange(z, maps, ops, primal, primal_packed, arranged, flat, half):
    flat[...] = jnp.zeros_like(flat)
    flat[0:4, 0 : z.face] = maps[0, 0]
    lane = iota((1, z.padded), 1)
    line = jnp.full((1, z.padded), -1, jnp.int32)
    signs = jnp.zeros((1, z.padded), F32)
    for f in range(4):
        moved = pltpu.roll(flat[...], f * z.face, 1)[f : f + 1] if f else flat[0:1]
        here = (lane >= f * z.face) & (lane < (f + 1) * z.face)
        line = jnp.where(here, moved + f * z.face, line)
        signs = jnp.where(here, SIGNS[f], signs)
    column = jnp.transpose(jnp.broadcast_to(line, (8, z.padded)))[:, 0:1]
    spread = []
    for low, high, first, last in blocks_of(z):
        hit = (iota((last - first, high - low), 1) + low) == column[first:last]
        spread.append(hit.astype(F32).astype(BF16))
    for low, high, first, last in blocks_of(z):
        hit = (iota((high - low, last - first), 0) + low) == line[:, first:last]
        collect = jnp.where(hit, signs[:, first:last], 0.0).astype(BF16)
        half[low:high, :] = dot(collect, ops[0, 0, first:last, :], precision=None).astype(BF16)
    values = primal[0, 0]
    parts = []
    for _ in range(3):
        parts.append(values.astype(BF16))
        values = values - parts[-1].astype(F32)
    pieces = jnp.concatenate(parts, axis=0)
    n = z.cases
    for (low, high, first, last), there in zip(blocks_of(z), spread):
        three = dot(pieces[:, first:last], there, precision=None)
        primal_packed[:, low:high] = three[0:n] + (three[n : 2 * n] + three[2 * n :])
    primal_packed.push()
    for (low, high, first, last), there in zip(blocks_of(z), spread):
        arranged[:, low:high] = dot(half[:, first:last], there, precision=None).astype(BF16)


def invert(z, loads, padded, masks, local_tile, aug, small):
    diagonal = sum(dot(padded[f] * masks[f : f + 1], padded[f], (1, 1)) for f in range(4))
    row, col = iota((8, 128), 0), iota((8, 128), 1)
    aug[...] = jnp.where((col == row + 8) & (row < z.modes), 1.0, 0.0).astype(F32)
    aug[:, 0:8] = diagonal
    matrix = aug[...]
    for p in range(z.modes):
        scaled = matrix[p : p + 1, :] / matrix[p : p + 1, p : p + 1]
        taken = matrix[:, p : p + 1] - (row[:, 0:1] == p).astype(F32)
        matrix = matrix - taken * scaled
    inverse = matrix[:, 8:16]
    small[...] = jnp.zeros(small.shape, F32)
    for j in range(z.modes):
        small[j : j + 1, :] = loads[0, j]
    local_tile[...] = jnp.zeros(local_tile.shape, F32)
    local_tile[:, FIRST_LANE : FIRST_LANE + z.cases] = dot(inverse, small[...])
    local_tile[:, INVERSE_LANE : INVERSE_LANE + 8] = inverse


def couple(z, padded, masks, local_tile, got1, got3, got0, got2, sent, live_rows, lift_rows, tile):
    near = across_faces(z, (got0, got1, got2, got3))
    inverse = local_tile[:, INVERSE_LANE : INVERSE_LANE + 8]
    tile[...] = local_tile[...]
    for f in range(4):
        live = padded[f] * masks[f : f + 1]
        lift_rows[f] = jnp.concatenate([live * SIGNS[f], near[f] * masks[f : f + 1] * -SIGNS[f]], axis=0)
        tile[:, 8 * f : 8 * f + 8] = dot(inverse, dot(live, near[f], (1, 1)))
    sent[...] = jnp.broadcast_to(tile[...][None], sent.shape)
    sent.push()
    live_rows[...] = masks[...]


def lifted(z, amplitudes, lift_rows, f):
    pair = jnp.concatenate([amplitudes[0:8], amplitudes[8 * f + 8 : 8 * f + 16]], axis=0)
    return dot(pair, lift_rows[f], (0, 0))


def apply(z, faces, arranged, packed):
    packed[...] = jnp.zeros(packed.shape, F32)
    for f in range(4):
        wide = jnp.concatenate([faces[f], jnp.zeros((z.cases, z.width - z.lanes), F32)], axis=1)
        shift = f * z.face - z.starts[f]
        packed[:, z.starts[f] : z.starts[f] + z.width] += pltpu.roll(wide, shift, 1) if shift else wide
    return dot(packed[:, 0 : z.order].astype(BF16), arranged[...], precision=None)


def unpacked(z, values, packed):
    packed[:, 0 : z.order] = values
    found = []
    for f in range(4):
        part = packed[:, z.starts[f] : z.starts[f] + z.width]
        shift = f * z.face - z.starts[f]
        part = (pltpu.roll(part, z.width - shift, 1) if shift else part)[:, 0 : z.lanes]
        found.append(jnp.where(iota(part.shape, 1) < z.face, part, 0.0))
    return found


def send_coarse(z, faces, rows, scalars, sent, tile):
    tile[...] = jnp.zeros_like(tile)
    mine = jnp.zeros((8, z.cases), F32)
    for f in range(4):
        both = dot(rows[f], faces[f], (1, 1))
        mine = mine + both[0:8]
        tile[:, (1 + f) * z.cases : (2 + f) * z.cases] = both[8:16]
    tile[:, 0 : z.cases] = mine
    send_tile(tile[...], scalars, sent)


def send_tile(values, scalars, sent):
    row, col = iota((8, 128), 0), iota((8, 128), 1)
    for i, scalar in enumerate(scalars):
        values = jnp.where((row == 0) & (col == SCALAR_LANE + i), scalar, values)
    sent[...] = jnp.broadcast_to(values[None], sent.shape)
    sent.push()


def scalar_of(total, i):
    row, col = iota((8, 128), 0), iota((8, 128), 1)
    return jnp.sum(jnp.where((row == 0) & (col == SCALAR_LANE + i), total, 0.0), keepdims=True)


def received_window(z, received):
    ix, _ = place()
    start = window_start(z, ix) * z.ny
    return received[pl.ds(start, z.wide * z.ny)].reshape(z.rows, 128)


def coarse_amplitudes(z, received, solve_rows):
    values = received_window(z, received)
    start = values
    for f in range(4):
        across = pltpu.roll(values, 128 - (1 + (f ^ 1)) * z.cases, 1)
        step = 8 * z.steps[f]
        empty = jnp.zeros((abs(step), 128), F32)
        if step > 0:
            moved = jnp.concatenate([across[step:], empty], axis=0)
        else:
            moved = jnp.concatenate([empty, across[: z.rows + step]], axis=0)
        start = start - moved
    return dot(solve_rows[...], start)[:, 0 : z.cases]


def total(values):
    return jnp.sum(values, keepdims=True)


def face_weights(z):
    ix, iy = place()
    edges = (ix == 0, ix == z.nx - 1, iy == 0, iy == z.ny - 1)
    return [jnp.where(edge, 1.0, 0.5).astype(F32) for edge in edges]


def begin(
    z, primal, lift_rows, received, arranged,
    rows, multipliers, sent, to0, to1, to2, to3, solve_rows, faces,
    matrix, tile, packed,
):
    ix, iy = place()
    near_spots = spots(z, ix, iy)
    values = received_window(z, received)
    lane = iota((z.rows, 128), 1)
    row = iota((z.rows, 128), 0)
    tiled = []
    for f in range(4):
        part = jnp.where(lane // 8 == f, values, 0.0)
        for shift in (64, 32, 16, 8):
            part = part + pltpu.roll(part, shift, 1)
        tiled.append(part)
    for block in range(-(-z.rows // 128)):
        target = (lane + 128 * block) // 8 - row // 8
        part = jnp.zeros((z.rows, 128), F32)
        for f in range(4):
            part = part + jnp.where(target == z.steps[f], tiled[f], 0.0)
        matrix[:, 128 * block : 128 * block + 128] = part
    once = jnp.concatenate([matrix[pl.ds(pl.multiple_of(s * 8, 8), 8), 0 : z.rows] for s in near_spots], axis=0)
    twice = dot(once, matrix[:, 0 : z.rows])
    cols = z.rows
    unit = jnp.concatenate([
        (iota((8, cols), 1) == iota((8, cols), 0) + s * 8).astype(F32) for s in near_spots
    ], axis=0)
    solve = unit + once + twice
    solve_rows[...] = solve
    amplitudes = dot(solve, values)[:, FIRST_LANE : FIRST_LANE + z.cases]
    start = window_start(z, ix) * z.ny
    inverses = [received[pl.ds(start + spot, 1)][0][:, INVERSE_LANE : INVERSE_LANE + 8] for spot in near_spots]
    fields = []
    own = dot(inverses[0], jnp.concatenate([lift_rows[f][0:8] * SIGNS[f] for f in range(4)], axis=1))
    for f in range(4):
        near = dot(inverses[1 + f], lift_rows[f][8:16] * -SIGNS[f])
        rows[f] = jnp.concatenate([own[:, f * z.lanes : (f + 1) * z.lanes], near], axis=0)
        fields.append(lifted(z, amplitudes, lift_rows, f))
        multipliers[f] = fields[f]
    for item in (rows, multipliers):
        item.push()
    image = unpacked(z, primal[...] - apply(z, fields, arranged, packed), packed)
    for f in range(4):
        faces[f] = image[f]
    send_faces(z, image, (to0, to1, to2, to3))
    send_coarse(z, image, rows, [], sent, tile)


def jumped(z, masks, faces, got):
    near = across_faces(z, got)
    return [masks[f : f + 1] * SIGNS[f] * (faces[f] - near[f]) for f in range(4)]


def first_direction(
    z, rows, solve_rows, lift_rows, faces, masks, got1, got3, got0, got2, received, arranged,
    residual, direction, sent, to0, to1, to2, to3, image,
    tile, packed,
):
    amplitudes = coarse_amplitudes(z, received, solve_rows)
    field = jumped(z, masks, faces, (got0, got1, got2, got3))
    weights = face_weights(z)
    moved = [field[f] - lifted(z, amplitudes, lift_rows, f) for f in range(4)]
    for f in range(4):
        residual[f] = field[f]
        direction[f] = moved[f]
    residual.push()
    direction.push()
    found = unpacked(z, apply(z, moved, arranged, packed), packed)
    for f in range(4):
        image[f] = found[f]
    gamma = sum(weights[f] * total(field[f] * moved[f]) for f in range(4))
    curvature = sum(SIGNS[f] * total(moved[f] * found[f]) for f in range(4))
    send_faces(z, found, (to0, to1, to2, to3))
    send_coarse(z, found, rows, [gamma, curvature], sent, tile)


def second_direction(
    z, residual, direction, multipliers, solve_rows, lift_rows, faces, masks,
    got1, got3, got0, got2, received, arranged,
    next_multipliers, next_residual, projected, image, sums, sent, to0, to1, to2, to3, fresh,
    packed,
):
    amplitudes = coarse_amplitudes(z, received, solve_rows)
    summed = jnp.sum(received[...], axis=0)
    sums[...] = summed
    alpha = scalar_of(summed, 0) / scalar_of(summed, 1)
    field = jumped(z, masks, faces, (got0, got1, got2, got3))
    weights = face_weights(z)
    left, moved = [], []
    for f in range(4):
        image[f] = field[f]
        next_multipliers[f] = multipliers[f] + alpha * direction[f]
        left.append(residual[f] - alpha * field[f])
        moved.append(direction[f] - alpha * (field[f] - lifted(z, amplitudes, lift_rows, f)))
        next_residual[f] = left[f]
        projected[f] = moved[f]
    for item in (sums, image, next_multipliers, next_residual, projected):
        item.push()
    found = unpacked(z, apply(z, moved, arranged, packed), packed)
    for f in range(4):
        fresh[f] = found[f]
    send_faces(z, found, (to0, to1, to2, to3))
    gamma = sum(weights[f] * total(left[f] * moved[f]) for f in range(4))
    straight = sum(SIGNS[f] * total(moved[f] * found[f]) for f in range(4))
    crossed = sum(
        weights[f] * total(moved[f] * field[f]) + SIGNS[f] * total(direction[f] * found[f]) for f in range(4)
    )
    send_tile(jnp.zeros((8, 128), F32), [gamma, straight, crossed], sent)


def finish(
    z, sums, residual, image, multipliers, projected, direction, faces, masks,
    got1, got3, got0, got2, received,
    out_multipliers, out_residual,
):
    summed = jnp.sum(received[...], axis=0)
    field = jumped(z, masks, faces, (got0, got1, got2, got3))
    gamma, curvature = scalar_of(sums[...], 0), scalar_of(sums[...], 1)
    fresh, straight, crossed = (scalar_of(summed, i) for i in range(3))
    beta = fresh / gamma
    alpha = fresh / (straight + beta * crossed + beta * beta * curvature)
    for f in range(4):
        step = projected[f] + beta * direction[f]
        out_multipliers[0, 0, f] = (multipliers[f] + alpha * step)[:, 0 : z.face]
        out_residual[0, 0, f] = (residual[f] - alpha * (field[f] + beta * image[f]))[:, 0 : z.face]


class Coming:
    def __init__(self, source, held, semaphore):
        self.held = held
        self.copy = pltpu.make_async_copy(source, held, semaphore)
        self.copy.start()

    def ready(self):
        if self.copy is not None:
            self.copy.wait()
            self.copy = None
        return self.held

    def __getitem__(self, index):
        return self.ready()[index]


class Going:
    def __init__(self, held, target, semaphore):
        self.held = held
        self.copy = pltpu.make_async_copy(held, target, semaphore)
        self.shape, self.dtype = held.shape, held.dtype
        self.started = False

    def __getitem__(self, index):
        return self.held[index]

    def __setitem__(self, index, values):
        self.held[index] = values

    def push(self):
        if not self.started:
            self.copy.start()
            self.started = True


def call(z, kernel, outs, args, scratch=(), flops=0, near=0, kept=0):
    shapes = [jax.ShapeDtypeStruct(shape, dtype) for shape, dtype in outs]
    moved = sum(a.size * a.dtype.itemsize for a in args) + sum(s.size * s.dtype.itemsize for s in shapes)
    far, sent = len(args) - near, len(outs) - kept

    def run(*refs):
        refs = list(refs)
        take = lambda n: [refs.pop(0) for _ in range(n)]
        sources, others, targets, direct = take(far), take(near), take(sent), take(kept)
        held, made, work = take(far), take(sent), take(len(scratch))
        coming = [Coming(a, b, refs[0].at[i]) for i, (a, b) in enumerate(zip(sources, held))]
        going = [Going(a, b, refs[0].at[far + i]) for i, (a, b) in enumerate(zip(made, targets))]
        kernel(z, *coming, *others, *going, *direct, *work)
        for item in going:
            item.push()
        for item in coming:
            item.ready()
        for item in going:
            item.copy.wait()

    near_spec = lambda a: pl.BlockSpec(memory_space=SMEM if a.ndim == 3 and a.size == 4 else VMEM)
    far_spec = pl.BlockSpec(memory_space=pltpu.HBM)
    buffers = [(SMEM if a.size == 4 else VMEM)(a.shape, a.dtype) for a in list(args[:far]) + shapes[:sent]]
    semaphores = [pltpu.SemaphoreType.DMA((far + sent,))] if far + sent else []
    return pl.pallas_call(
        run,
        out_shape=[pltpu.HBM(a.shape, a.dtype) for a in shapes[:sent]] + shapes[sent:],
        in_specs=[far_spec] * far + [near_spec(a) for a in args[far:]],
        out_specs=[far_spec] * sent + [near_spec(a) for a in shapes[sent:]],
        scratch_shapes=buffers + [VMEM(shape, dtype) for shape, dtype in scratch] + semaphores,
        compiler_params=pltpu.CompilerParams(vmem_limit_bytes=24 * 2**20),
        cost_estimate=pl.CostEstimate(flops=flops, bytes_accessed=moved, transcendentals=0),
        name=kernel.__name__,
    )(*[pltpu.with_memory_space_constraint(a, pltpu.HBM) for a in args[:far]], *args[far:])


def gather(values):
    return lax.all_to_all(values, AXES, 0, 0, tiled=True)


def body(ops, traces, primal, loads, maps, counts):
    z = Sizes(lax.axis_size("gx"), lax.axis_size("gy"), traces, loads)
    field = ((4, z.cases, z.lanes), F32)
    mode_rows = ((4, 8, z.lanes), F32)
    pair_rows = ((4, 16, z.lanes), F32)
    live_rows = ((8, z.lanes), F32)
    tile = ((8, 128), F32)
    sent = ((z.count, 8, 128), F32)
    to_faces = [((z.cases, z.lanes), F32)] * 4
    columns = -(-z.rows // 128) * 128
    product_flops = 2 * z.cases * z.order**2

    padded, masks, *trace_faces = call(
        z, prepare, [mode_rows, live_rows] + [((8, z.lanes), F32)] * 4,
        [jnp.transpose(traces, (0, 1, 3, 2, 4)), counts], kept=6,
    )
    got = exchange(trace_faces)
    (local_tile,) = call(
        z, invert, [tile], [jnp.transpose(loads, (0, 2, 1, 3)), padded, masks],
        [tile, ((8, z.cases), F32)], product_flops, near=2, kept=1,
    )
    blocks, masks, lift_rows = call(
        z, couple, [sent, live_rows, pair_rows], [padded, masks, local_tile, *got], [tile], near=7, kept=2,
    )
    blocks = gather(blocks)
    packed = ((z.cases, z.padded), F32)
    primal_packed, arranged = call(
        z, arrange, [((z.cases, z.order), F32), ((z.order, z.order), BF16)], [maps, ops, primal],
        [((8, z.padded), jnp.int32), ((z.order, z.order), BF16)], 4 * z.order**2 * z.width, kept=1,
    )
    rows, multipliers, coarse, *sent_faces, solve_rows, faces = call(
        z, begin, [pair_rows, field, sent] + to_faces + [((40, z.rows), F32), field],
        [primal_packed, lift_rows, blocks, arranged],
        [((z.rows, columns), F32), tile, packed], product_flops, near=3, kept=2,
    )
    coarse, got = gather(coarse), exchange(sent_faces)
    residual, direction, coarse, *sent_faces, faces = call(
        z, first_direction, [field, field, sent] + to_faces + [field],
        [rows, solve_rows, lift_rows, faces, masks, *got, coarse, arranged],
        [tile, packed], product_flops, near=10, kept=1,
    )
    coarse, got = gather(coarse), exchange(sent_faces)
    multipliers, residual, projected, image, sums, coarse, *sent_faces, faces = call(
        z, second_direction, [field, field, field, field, tile, sent] + to_faces + [field],
        [residual, direction, multipliers, solve_rows, lift_rows, faces, masks, *got, coarse, arranged],
        [packed], product_flops, near=10, kept=1,
    )
    coarse, got = gather(coarse), exchange(sent_faces)
    whole = ((1, 1, 4, z.cases, z.face), F32)
    multipliers, residual = call(
        z, finish, [whole, whole],
        [sums, residual, image, multipliers, projected, direction, faces, masks, *got, coarse], near=7,
    )
    return multipliers, residual


def solution(mesh):
    in_specs = (
        P("gx", "gy", None, None),
        P("gx", "gy", None, None, None),
        P("gx", "gy", None, None),
        P("gx", "gy", None, None),
        P("gx", "gy", None, None),
        P("gx", "gy", None),
    )
    out_specs = (P("gx", "gy", None, None, None), P("gx", "gy", None, None, None))
    return jax.shard_map(body, mesh=mesh, in_specs=in_specs, out_specs=out_specs, check_vma=False)
```

```python
import functools

import jax
import jax.numpy as jnp
from jax import lax
from jax.experimental import pallas as pl
from jax.experimental.pallas import tpu as pltpu
from jax.sharding import PartitionSpec as P

SIGNS = (-1.0, 1.0, -1.0, 1.0)
HIGHEST = lax.Precision.HIGHEST
AXES = ("gx", "gy")
F32 = jnp.float32
BF16 = jnp.bfloat16
VMEM = pltpu.VMEM
SMEM = pltpu.SMEM
FIRST_LANE = 32
INVERSE_LANE = 48
SCALAR_LANE = 96
BLOCK = 256
SWAPS = (3, 0, 1, 2)


class Sizes:
    def __init__(self, nx, ny, traces, loads):
        self.nx, self.ny = nx, ny
        self.count = nx * ny
        self.modes, self.face = traces.shape[-2:]
        self.cases = loads.shape[-1]
        self.order = 4 * self.face
        self.lanes = -(-self.face // 128) * 128
        self.starts = [f * self.face // 128 * 128 for f in range(4)]
        ends = [-(-(f + 1) * self.face // 128) * 128 for f in range(4)]
        self.width = max(e - s for s, e in zip(self.starts, ends))
        self.padded = max(s + self.width for s in self.starts)
        self.wide = min(nx, 9)
        self.rows = self.wide * ny * 8
        self.steps = (-ny, ny, -1, 1)


def dot(a, b, contract=(1, 0), precision=HIGHEST):
    dims = (((contract[0],), (contract[1],)), ((), ()))
    return lax.dot_general(a, b, dims, precision=precision, preferred_element_type=F32)


def iota(shape, dim):
    return lax.broadcasted_iota(jnp.int32, shape, dim)


def place():
    return lax.axis_index("gx"), lax.axis_index("gy")


def window_start(z, ix):
    return jnp.clip(ix - 4, 0, z.nx - z.wide) if z.wide < z.nx else 0


def spots(z, ix, iy):
    own = (ix - window_start(z, ix)) * z.ny + iy
    return [own] + [jnp.clip(own + step, 0, z.wide * z.ny - 1) for step in z.steps]


def send_faces(z, faces, sent):
    for i, at in enumerate(place()):
        even = at % 2 == 0
        low, high = faces[2 * i], faces[2 * i + 1]
        sent[2 * i][...] = jnp.where(even, high, low)
        sent[2 * i + 1][...] = jnp.where(even, low, high)
        sent[2 * i].push()
        sent[2 * i + 1].push()


def across_faces(z, got):
    found = []
    for i, at in enumerate(place()):
        even = at % 2 == 0
        first, second = got[2 * i][...], got[2 * i + 1][...]
        found += [jnp.where(even, second, first), jnp.where(even, first, second)]
    return found


def exchange(sent):
    got = []
    for i in SWAPS:
        axis = AXES[i // 2]
        pairs = []
        for low in range(i % 2, lax.axis_size(axis) - 1, 2):
            pairs += [(low, low + 1), (low + 1, low)]
        got.append(lax.ppermute(sent[i], axis, pairs))
    return got


def prepare(z, traces, counts, padded, masks, *sent):
    padded[...] = jnp.zeros(padded.shape, F32)
    for f in range(4):
        for j in range(z.modes):
            padded[f, j : j + 1, 0 : z.face] = traces[0, 0, j, f : f + 1]
    for i, at in enumerate(place()):
        even = at % 2 == 0
        low, high = padded[2 * i], padded[2 * i + 1]
        sent[2 * i][...] = jnp.where(even, high, low)
        sent[2 * i + 1][...] = jnp.where(even, low, high)
    row, lane = iota(masks.shape, 0), iota(masks.shape, 1)
    live = jnp.zeros(masks.shape, F32)
    for f in range(4):
        live = jnp.where((row == f) & (lane < counts[0, 0, f]), 1.0, live)
    masks[...] = live


def blocks_of(z):
    found = []
    for low in range(0, z.order, BLOCK):
        high = min(low + BLOCK, z.order)
        first, last = low // z.face, (high - 1) // z.face
        found.append((low, high, first * z.face // 128 * 128, min(-(-(last + 1) * z.face // 128) * 128, z.order)))
    return found


def arrange(z, maps, ops, primal, primal_packed, arranged, flat, half):
    flat[...] = jnp.zeros_like(flat)
    flat[0:4, 0 : z.face] = maps[0, 0]
    lane = iota((1, z.padded), 1)
    line = jnp.full((1, z.padded), -1, jnp.int32)
    signs = jnp.zeros((1, z.padded), F32)
    for f in range(4):
        moved = pltpu.roll(flat[...], f * z.face, 1)[f : f + 1] if f else flat[0:1]
        here = (lane >= f * z.face) & (lane < (f + 1) * z.face)
        line = jnp.where(here, moved + f * z.face, line)
        signs = jnp.where(here, SIGNS[f], signs)
    column = jnp.transpose(jnp.broadcast_to(line, (8, z.padded)))[:, 0:1]
    spread = []
    for low, high, first, last in blocks_of(z):
        hit = (iota((last - first, high - low), 1) + low) == column[first:last]
        spread.append(hit.astype(F32).astype(BF16))
    for low, high, first, last in blocks_of(z):
        hit = (iota((high - low, last - first), 0) + low) == line[:, first:last]
        collect = jnp.where(hit, signs[:, first:last], 0.0).astype(BF16)
        half[low:high, :] = dot(collect, ops[0, 0, first:last, :], precision=None).astype(BF16)
    values = primal[0, 0]
    parts = []
    for _ in range(3):
        parts.append(values.astype(BF16))
        values = values - parts[-1].astype(F32)
    pieces = jnp.concatenate(parts, axis=0)
    n = z.cases
    for (low, high, first, last), there in zip(blocks_of(z), spread):
        three = dot(pieces[:, first:last], there, precision=None)
        primal_packed[:, low:high] = three[0:n] + (three[n : 2 * n] + three[2 * n :])
    primal_packed.push()
    for (low, high, first, last), there in zip(blocks_of(z), spread):
        arranged[:, low:high] = dot(half[:, first:last], there, precision=None).astype(BF16)


def invert(z, loads, padded, masks, local_tile, aug, small):
    diagonal = sum(dot(padded[f] * masks[f : f + 1], padded[f], (1, 1)) for f in range(4))
    row, col = iota((8, 128), 0), iota((8, 128), 1)
    aug[...] = jnp.where((col == row + 8) & (row < z.modes), 1.0, 0.0).astype(F32)
    aug[:, 0:8] = diagonal
    matrix = aug[...]
    for p in range(z.modes):
        scaled = matrix[p : p + 1, :] / matrix[p : p + 1, p : p + 1]
        taken = matrix[:, p : p + 1] - (row[:, 0:1] == p).astype(F32)
        matrix = matrix - taken * scaled
    inverse = matrix[:, 8:16]
    small[...] = jnp.zeros(small.shape, F32)
    for j in range(z.modes):
        small[j : j + 1, :] = loads[0, j]
    local_tile[...] = jnp.zeros(local_tile.shape, F32)
    local_tile[:, FIRST_LANE : FIRST_LANE + z.cases] = dot(inverse, small[...])
    local_tile[:, INVERSE_LANE : INVERSE_LANE + 8] = inverse


def couple(z, padded, masks, local_tile, got3, got0, got1, got2, sent, live_rows, lift_rows, tile):
    near = across_faces(z, (got0, got1, got2, got3))
    inverse = local_tile[:, INVERSE_LANE : INVERSE_LANE + 8]
    tile[...] = local_tile[...]
    for f in range(4):
        live = padded[f] * masks[f : f + 1]
        lift_rows[f] = jnp.concatenate([live * SIGNS[f], near[f] * masks[f : f + 1] * -SIGNS[f]], axis=0)
        tile[:, 8 * f : 8 * f + 8] = dot(inverse, dot(live, near[f], (1, 1)))
    sent[...] = jnp.broadcast_to(tile[...][None], sent.shape)
    sent.push()
    live_rows[...] = masks[...]


def lifted(z, amplitudes, lift_rows, f):
    pair = jnp.concatenate([amplitudes[0:8], amplitudes[8 * f + 8 : 8 * f + 16]], axis=0)
    return dot(pair, lift_rows[f], (0, 0))


def apply(z, faces, arranged, packed):
    packed[...] = jnp.zeros(packed.shape, F32)
    for f in range(4):
        wide = jnp.concatenate([faces[f], jnp.zeros((z.cases, z.width - z.lanes), F32)], axis=1)
        shift = f * z.face - z.starts[f]
        packed[:, z.starts[f] : z.starts[f] + z.width] += pltpu.roll(wide, shift, 1) if shift else wide
    return dot(packed[:, 0 : z.order].astype(BF16), arranged[...], precision=None)


def unpacked(z, values, packed):
    packed[:, 0 : z.order] = values
    found = []
    for f in range(4):
        part = packed[:, z.starts[f] : z.starts[f] + z.width]
        shift = f * z.face - z.starts[f]
        part = (pltpu.roll(part, z.width - shift, 1) if shift else part)[:, 0 : z.lanes]
        found.append(jnp.where(iota(part.shape, 1) < z.face, part, 0.0))
    return found


def send_coarse(z, faces, rows, scalars, sent, tile):
    tile[...] = jnp.zeros_like(tile)
    mine = jnp.zeros((8, z.cases), F32)
    for f in range(4):
        both = dot(rows[f], faces[f], (1, 1))
        mine = mine + both[0:8]
        tile[:, (1 + f) * z.cases : (2 + f) * z.cases] = both[8:16]
    tile[:, 0 : z.cases] = mine
    send_tile(tile[...], scalars, sent)


def send_tile(values, scalars, sent):
    row, col = iota((8, 128), 0), iota((8, 128), 1)
    for i, scalar in enumerate(scalars):
        values = jnp.where((row == 0) & (col == SCALAR_LANE + i), scalar, values)
    sent[...] = jnp.broadcast_to(values[None], sent.shape)
    sent.push()


def scalar_of(total, i):
    row, col = iota((8, 128), 0), iota((8, 128), 1)
    return jnp.sum(jnp.where((row == 0) & (col == SCALAR_LANE + i), total, 0.0), keepdims=True)


def received_window(z, received):
    ix, _ = place()
    start = window_start(z, ix) * z.ny
    return received[pl.ds(start, z.wide * z.ny)].reshape(z.rows, 128)


def coarse_amplitudes(z, received, solve_rows):
    values = received_window(z, received)
    start = values
    for f in range(4):
        across = pltpu.roll(values, 128 - (1 + (f ^ 1)) * z.cases, 1)
        step = 8 * z.steps[f]
        empty = jnp.zeros((abs(step), 128), F32)
        if step > 0:
            moved = jnp.concatenate([across[step:], empty], axis=0)
        else:
            moved = jnp.concatenate([empty, across[: z.rows + step]], axis=0)
        start = start - moved
    return dot(solve_rows[...], start)[:, 0 : z.cases]


def total(values):
    return jnp.sum(values, keepdims=True)


def face_weights(z):
    ix, iy = place()
    edges = (ix == 0, ix == z.nx - 1, iy == 0, iy == z.ny - 1)
    return [jnp.where(edge, 1.0, 0.5).astype(F32) for edge in edges]


def begin(
    z, lift_rows, primal, received, arranged,
    solve_rows, rows, multipliers, faces, sent, to0, to1, to2, to3,
    matrix, tile, packed,
):
    ix, iy = place()
    near_spots = spots(z, ix, iy)
    values = received_window(z, received)
    lane = iota((z.rows, 128), 1)
    row = iota((z.rows, 128), 0)
    tiled = []
    for f in range(4):
        part = jnp.where(lane // 8 == f, values, 0.0)
        for shift in (64, 32, 16, 8):
            part = part + pltpu.roll(part, shift, 1)
        tiled.append(part)
    for block in range(-(-z.rows // 128)):
        target = (lane + 128 * block) // 8 - row // 8
        part = jnp.zeros((z.rows, 128), F32)
        for f in range(4):
            part = part + jnp.where(target == z.steps[f], tiled[f], 0.0)
        matrix[:, 128 * block : 128 * block + 128] = part
    once = jnp.concatenate([matrix[pl.ds(pl.multiple_of(s * 8, 8), 8), 0 : z.rows] for s in near_spots], axis=0)
    twice = dot(once, matrix[:, 0 : z.rows])
    cols = z.rows
    unit = jnp.concatenate([
        (iota((8, cols), 1) == iota((8, cols), 0) + s * 8).astype(F32) for s in near_spots
    ], axis=0)
    solve = unit + once + twice
    solve_rows[...] = solve
    amplitudes = dot(solve, values)[:, FIRST_LANE : FIRST_LANE + z.cases]
    start = window_start(z, ix) * z.ny
    inverses = [received[pl.ds(start + spot, 1)][0][:, INVERSE_LANE : INVERSE_LANE + 8] for spot in near_spots]
    fields = []
    own = dot(inverses[0], jnp.concatenate([lift_rows[f][0:8] * SIGNS[f] for f in range(4)], axis=1))
    for f in range(4):
        near = dot(inverses[1 + f], lift_rows[f][8:16] * -SIGNS[f])
        rows[f] = jnp.concatenate([own[:, f * z.lanes : (f + 1) * z.lanes], near], axis=0)
        fields.append(lifted(z, amplitudes, lift_rows, f))
        multipliers[f] = fields[f]
    for item in (solve_rows, rows, multipliers):
        item.push()
    image = unpacked(z, primal[...] - apply(z, fields, arranged, packed), packed)
    for f in range(4):
        faces[f] = image[f]
    faces.push()
    send_faces(z, image, (to0, to1, to2, to3))
    send_coarse(z, image, rows, [], sent, tile)


def jumped(z, masks, faces, got):
    near = across_faces(z, got)
    return [masks[f : f + 1] * SIGNS[f] * (faces[f] - near[f]) for f in range(4)]


def first_direction(
    z, solve_rows, lift_rows, faces, masks, rows, got3, got0, got1, got2, received, arranged,
    residual, direction, image, sent, to0, to1, to2, to3,
    tile, packed,
):
    amplitudes = coarse_amplitudes(z, received, solve_rows)
    field = jumped(z, masks, faces, (got0, got1, got2, got3))
    weights = face_weights(z)
    moved = [field[f] - lifted(z, amplitudes, lift_rows, f) for f in range(4)]
    for f in range(4):
        residual[f] = field[f]
        direction[f] = moved[f]
    residual.push()
    direction.push()
    found = unpacked(z, apply(z, moved, arranged, packed), packed)
    for f in range(4):
        image[f] = found[f]
    image.push()
    gamma = sum(weights[f] * total(field[f] * moved[f]) for f in range(4))
    curvature = sum(SIGNS[f] * total(moved[f] * found[f]) for f in range(4))
    send_faces(z, found, (to0, to1, to2, to3))
    send_coarse(z, found, rows, [gamma, curvature], sent, tile)


def second_direction(
    z, solve_rows, lift_rows, faces, masks, residual, direction, multipliers,
    got3, got0, got1, got2, received, arranged,
    next_multipliers, next_residual, projected, image, fresh, sums, sent, to0, to1, to2, to3,
    packed,
):
    amplitudes = coarse_amplitudes(z, received, solve_rows)
    summed = jnp.sum(received[...], axis=0)
    sums[...] = summed
    alpha = scalar_of(summed, 0) / scalar_of(summed, 1)
    field = jumped(z, masks, faces, (got0, got1, got2, got3))
    weights = face_weights(z)
    left, moved = [], []
    for f in range(4):
        image[f] = field[f]
        next_multipliers[f] = multipliers[f] + alpha * direction[f]
        left.append(residual[f] - alpha * field[f])
        moved.append(direction[f] - alpha * (field[f] - lifted(z, amplitudes, lift_rows, f)))
        next_residual[f] = left[f]
        projected[f] = moved[f]
    for item in (sums, image, next_multipliers, next_residual, projected):
        item.push()
    found = unpacked(z, apply(z, moved, arranged, packed), packed)
    for f in range(4):
        fresh[f] = found[f]
    fresh.push()
    send_faces(z, found, (to0, to1, to2, to3))
    gamma = sum(weights[f] * total(left[f] * moved[f]) for f in range(4))
    straight = sum(SIGNS[f] * total(moved[f] * found[f]) for f in range(4))
    crossed = sum(
        weights[f] * total(moved[f] * field[f]) + SIGNS[f] * total(direction[f] * found[f]) for f in range(4)
    )
    send_tile(jnp.zeros((8, 128), F32), [gamma, straight, crossed], sent)


def finish(
    z, sums, faces, masks, residual, image, multipliers, projected, direction,
    got3, got0, got1, got2, received,
    out_multipliers, out_residual,
):
    summed = jnp.sum(received[...], axis=0)
    field = jumped(z, masks, faces, (got0, got1, got2, got3))
    gamma, curvature = scalar_of(sums[...], 0), scalar_of(sums[...], 1)
    fresh, straight, crossed = (scalar_of(summed, i) for i in range(3))
    beta = fresh / gamma
    alpha = fresh / (straight + beta * crossed + beta * beta * curvature)
    for f in range(4):
        step = projected[f] + beta * direction[f]
        out_multipliers[0, 0, f] = (multipliers[f] + alpha * step)[:, 0 : z.face]
        out_residual[0, 0, f] = (residual[f] - alpha * (field[f] + beta * image[f]))[:, 0 : z.face]


class Coming:
    def __init__(self, source, held, semaphore):
        self.held = held
        self.copy = pltpu.make_async_copy(source, held, semaphore)
        self.copy.start()

    def ready(self):
        if self.copy is not None:
            self.copy.wait()
            self.copy = None
        return self.held

    def __getitem__(self, index):
        return self.ready()[index]


class Going:
    def __init__(self, held, target, semaphore):
        self.held = held
        self.copy = pltpu.make_async_copy(held, target, semaphore)
        self.shape, self.dtype = held.shape, held.dtype
        self.started = False

    def __getitem__(self, index):
        return self.held[index]

    def __setitem__(self, index, values):
        self.held[index] = values

    def push(self):
        if not self.started:
            self.copy.start()
            self.started = True


def call(z, kernel, outs, args, scratch=(), flops=0, near=0, kept=0):
    shapes = [jax.ShapeDtypeStruct(shape, dtype) for shape, dtype in outs]
    moved = sum(a.size * a.dtype.itemsize for a in args) + sum(s.size * s.dtype.itemsize for s in shapes)
    far, sent = len(args) - near, len(outs) - kept

    def run(*refs):
        refs = list(refs)
        take = lambda n: [refs.pop(0) for _ in range(n)]
        sources, others, targets, direct = take(far), take(near), take(sent), take(kept)
        held, made, work = take(far), take(sent), take(len(scratch))
        coming = [Coming(a, b, refs[0].at[i]) for i, (a, b) in enumerate(zip(sources, held))]
        going = [Going(a, b, refs[0].at[far + i]) for i, (a, b) in enumerate(zip(made, targets))]
        kernel(z, *coming, *others, *going, *direct, *work)
        for item in going:
            item.push()
        for item in coming:
            item.ready()
        for item in going:
            item.copy.wait()

    near_spec = lambda a: pl.BlockSpec(memory_space=SMEM if a.ndim == 3 and a.size == 4 else VMEM)
    far_spec = pl.BlockSpec(memory_space=pltpu.HBM)
    buffers = [(SMEM if a.size == 4 else VMEM)(a.shape, a.dtype) for a in list(args[:far]) + shapes[:sent]]
    semaphores = [pltpu.SemaphoreType.DMA((far + sent,))] if far + sent else []
    return pl.pallas_call(
        run,
        out_shape=[pltpu.HBM(a.shape, a.dtype) for a in shapes[:sent]] + shapes[sent:],
        in_specs=[far_spec] * far + [near_spec(a) for a in args[far:]],
        out_specs=[far_spec] * sent + [near_spec(a) for a in shapes[sent:]],
        scratch_shapes=buffers + [VMEM(shape, dtype) for shape, dtype in scratch] + semaphores,
        compiler_params=pltpu.CompilerParams(vmem_limit_bytes=24 * 2**20),
        cost_estimate=pl.CostEstimate(flops=flops, bytes_accessed=moved, transcendentals=0),
        name=kernel.__name__,
    )(*[pltpu.with_memory_space_constraint(a, pltpu.HBM) for a in args[:far]], *args[far:])


def gather(values):
    return lax.all_to_all(values, AXES, 0, 0, tiled=True)


def body(ops, traces, primal, loads, maps, counts):
    z = Sizes(lax.axis_size("gx"), lax.axis_size("gy"), traces, loads)
    field = ((4, z.cases, z.lanes), F32)
    mode_rows = ((4, 8, z.lanes), F32)
    pair_rows = ((4, 16, z.lanes), F32)
    live_rows = ((8, z.lanes), F32)
    tile = ((8, 128), F32)
    sent = ((z.count, 8, 128), F32)
    to_faces = [((z.cases, z.lanes), F32)] * 4
    columns = -(-z.rows // 128) * 128
    product_flops = 2 * z.cases * z.order**2

    padded, masks, *trace_faces = call(
        z, prepare, [mode_rows, live_rows] + [((8, z.lanes), F32)] * 4,
        [jnp.transpose(traces, (0, 1, 3, 2, 4)), counts], kept=6,
    )
    got = exchange(trace_faces)
    (local_tile,) = call(
        z, invert, [tile], [jnp.transpose(loads, (0, 2, 1, 3)), padded, masks],
        [tile, ((8, z.cases), F32)], product_flops, near=2, kept=1,
    )
    blocks, masks, lift_rows = call(
        z, couple, [sent, live_rows, pair_rows], [padded, masks, local_tile, *got], [tile], near=7,
    )
    blocks = gather(blocks)
    packed = ((z.cases, z.padded), F32)
    primal_packed, arranged = call(
        z, arrange, [((z.cases, z.order), F32), ((z.order, z.order), BF16)], [maps, ops, primal],
        [((8, z.padded), jnp.int32), ((z.order, z.order), BF16)], 4 * z.order**2 * z.width, kept=1,
    )
    solve_rows, rows, multipliers, faces, coarse, *sent_faces = call(
        z, begin, [((40, z.rows), F32), pair_rows, field, field, sent] + to_faces,
        [lift_rows, primal_packed, blocks, arranged],
        [((z.rows, columns), F32), tile, packed], product_flops, near=2,
    )
    coarse, got = gather(coarse), exchange(sent_faces)
    residual, direction, faces, coarse, *sent_faces = call(
        z, first_direction, [field, field, field, sent] + to_faces,
        [solve_rows, lift_rows, faces, masks, rows, *got, coarse, arranged],
        [tile, packed], product_flops, near=6,
    )
    coarse, got = gather(coarse), exchange(sent_faces)
    multipliers, residual, projected, image, faces, sums, coarse, *sent_faces = call(
        z, second_direction, [field, field, field, field, field, tile, sent] + to_faces,
        [solve_rows, lift_rows, faces, masks, residual, direction, multipliers, *got, coarse, arranged],
        [packed], product_flops, near=6,
    )
    coarse, got = gather(coarse), exchange(sent_faces)
    whole = ((1, 1, 4, z.cases, z.face), F32)
    multipliers, residual = call(
        z, finish, [whole, whole],
        [sums, faces, masks, residual, image, multipliers, projected, direction, *got, coarse], near=5,
    )
    return multipliers, residual


def solution(mesh):
    in_specs = (
        P("gx", "gy", None, None),
        P("gx", "gy", None, None, None),
        P("gx", "gy", None, None),
        P("gx", "gy", None, None),
        P("gx", "gy", None, None),
        P("gx", "gy", None),
    )
    out_specs = (P("gx", "gy", None, None, None), P("gx", "gy", None, None, None))
    return jax.shard_map(body, mesh=mesh, in_specs=in_specs, out_specs=out_specs, check_vma=False)
```

```python
import functools

import jax
import jax.numpy as jnp
from jax import lax
from jax.experimental import pallas as pl
from jax.experimental.pallas import tpu as pltpu
from jax.sharding import PartitionSpec as P

SIGNS = (-1.0, 1.0, -1.0, 1.0)
HIGHEST = lax.Precision.HIGHEST
AXES = ("gx", "gy")
F32 = jnp.float32
BF16 = jnp.bfloat16
VMEM = pltpu.VMEM
SMEM = pltpu.SMEM
FIRST_LANE = 32
INVERSE_LANE = 48
SCALAR_LANE = 96
BLOCK = 256
SWAPS = (3, 1, 0, 2)


class Sizes:
    def __init__(self, nx, ny, traces, loads):
        self.nx, self.ny = nx, ny
        self.count = nx * ny
        self.modes, self.face = traces.shape[-2:]
        self.cases = loads.shape[-1]
        self.order = 4 * self.face
        self.lanes = -(-self.face // 128) * 128
        self.starts = [f * self.face // 128 * 128 for f in range(4)]
        ends = [-(-(f + 1) * self.face // 128) * 128 for f in range(4)]
        self.width = max(e - s for s, e in zip(self.starts, ends))
        self.padded = max(s + self.width for s in self.starts)
        self.wide = min(nx, 9)
        self.rows = self.wide * ny * 8
        self.steps = (-ny, ny, -1, 1)


def dot(a, b, contract=(1, 0), precision=HIGHEST):
    dims = (((contract[0],), (contract[1],)), ((), ()))
    return lax.dot_general(a, b, dims, precision=precision, preferred_element_type=F32)


def iota(shape, dim):
    return lax.broadcasted_iota(jnp.int32, shape, dim)


def place():
    return lax.axis_index("gx"), lax.axis_index("gy")


def window_start(z, ix):
    return jnp.clip(ix - 4, 0, z.nx - z.wide) if z.wide < z.nx else 0


def spots(z, ix, iy):
    own = (ix - window_start(z, ix)) * z.ny + iy
    return [own] + [jnp.clip(own + step, 0, z.wide * z.ny - 1) for step in z.steps]


def send_faces(z, faces, sent):
    for i, at in enumerate(place()):
        even = at % 2 == 0
        low, high = faces[2 * i], faces[2 * i + 1]
        sent[2 * i][...] = jnp.where(even, high, low)
        sent[2 * i + 1][...] = jnp.where(even, low, high)
        sent[2 * i].push()
        sent[2 * i + 1].push()


def across_faces(z, got):
    found = []
    for i, at in enumerate(place()):
        even = at % 2 == 0
        first, second = got[2 * i][...], got[2 * i + 1][...]
        found += [jnp.where(even, second, first), jnp.where(even, first, second)]
    return found


def exchange(sent):
    got = []
    for i in SWAPS:
        axis = AXES[i // 2]
        pairs = []
        for low in range(i % 2, lax.axis_size(axis) - 1, 2):
            pairs += [(low, low + 1), (low + 1, low)]
        got.append(lax.ppermute(sent[i], axis, pairs))
    return got


def prepare(z, traces, counts, padded, masks, *sent):
    padded[...] = jnp.zeros(padded.shape, F32)
    for f in range(4):
        for j in range(z.modes):
            padded[f, j : j + 1, 0 : z.face] = traces[0, 0, j, f : f + 1]
    for i, at in enumerate(place()):
        even = at % 2 == 0
        low, high = padded[2 * i], padded[2 * i + 1]
        sent[2 * i][...] = jnp.where(even, high, low)
        sent[2 * i + 1][...] = jnp.where(even, low, high)
    row, lane = iota(masks.shape, 0), iota(masks.shape, 1)
    live = jnp.zeros(masks.shape, F32)
    for f in range(4):
        live = jnp.where((row == f) & (lane < counts[0, 0, f]), 1.0, live)
    masks[...] = live


def blocks_of(z):
    found = []
    for low in range(0, z.order, BLOCK):
        high = min(low + BLOCK, z.order)
        first, last = low // z.face, (high - 1) // z.face
        found.append((low, high, first * z.face // 128 * 128, min(-(-(last + 1) * z.face // 128) * 128, z.order)))
    return found


def arrange(z, maps, ops, primal, primal_packed, arranged, flat, half):
    flat[...] = jnp.zeros_like(flat)
    flat[0:4, 0 : z.face] = maps[0, 0]
    lane = iota((1, z.padded), 1)
    line = jnp.full((1, z.padded), -1, jnp.int32)
    signs = jnp.zeros((1, z.padded), F32)
    for f in range(4):
        moved = pltpu.roll(flat[...], f * z.face, 1)[f : f + 1] if f else flat[0:1]
        here = (lane >= f * z.face) & (lane < (f + 1) * z.face)
        line = jnp.where(here, moved + f * z.face, line)
        signs = jnp.where(here, SIGNS[f], signs)
    column = jnp.transpose(jnp.broadcast_to(line, (8, z.padded)))[:, 0:1]
    spread = []
    for low, high, first, last in blocks_of(z):
        hit = (iota((last - first, high - low), 1) + low) == column[first:last]
        spread.append(hit.astype(F32).astype(BF16))
    for low, high, first, last in blocks_of(z):
        hit = (iota((high - low, last - first), 0) + low) == line[:, first:last]
        collect = jnp.where(hit, signs[:, first:last], 0.0).astype(BF16)
        half[low:high, :] = dot(collect, ops[0, 0, first:last, :], precision=None).astype(BF16)
    values = primal[0, 0]
    parts = []
    for _ in range(3):
        parts.append(values.astype(BF16))
        values = values - parts[-1].astype(F32)
    pieces = jnp.concatenate(parts, axis=0)
    n = z.cases
    for (low, high, first, last), there in zip(blocks_of(z), spread):
        three = dot(pieces[:, first:last], there, precision=None)
        primal_packed[:, low:high] = three[0:n] + (three[n : 2 * n] + three[2 * n :])
    primal_packed.push()
    for (low, high, first, last), there in zip(blocks_of(z), spread):
        arranged[:, low:high] = dot(half[:, first:last], there, precision=None).astype(BF16)


def invert(z, loads, padded, masks, local_tile, aug, small):
    diagonal = sum(dot(padded[f] * masks[f : f + 1], padded[f], (1, 1)) for f in range(4))
    row, col = iota((8, 128), 0), iota((8, 128), 1)
    aug[...] = jnp.where((col == row + 8) & (row < z.modes), 1.0, 0.0).astype(F32)
    aug[:, 0:8] = diagonal
    matrix = aug[...]
    for p in range(z.modes):
        scaled = matrix[p : p + 1, :] / matrix[p : p + 1, p : p + 1]
        taken = matrix[:, p : p + 1] - (row[:, 0:1] == p).astype(F32)
        matrix = matrix - taken * scaled
    inverse = matrix[:, 8:16]
    small[...] = jnp.zeros(small.shape, F32)
    for j in range(z.modes):
        small[j : j + 1, :] = loads[0, j]
    local_tile[...] = jnp.zeros(local_tile.shape, F32)
    local_tile[:, FIRST_LANE : FIRST_LANE + z.cases] = dot(inverse, small[...])
    local_tile[:, INVERSE_LANE : INVERSE_LANE + 8] = inverse


def couple(z, padded, masks, local_tile, got3, got1, got0, got2, sent, live_rows, lift_rows, tile):
    near = across_faces(z, (got0, got1, got2, got3))
    inverse = local_tile[:, INVERSE_LANE : INVERSE_LANE + 8]
    tile[...] = local_tile[...]
    for f in range(4):
        live = padded[f] * masks[f : f + 1]
        lift_rows[f] = jnp.concatenate([live * SIGNS[f], near[f] * masks[f : f + 1] * -SIGNS[f]], axis=0)
        tile[:, 8 * f : 8 * f + 8] = dot(inverse, dot(live, near[f], (1, 1)))
    sent[...] = jnp.broadcast_to(tile[...][None], sent.shape)
    sent.push()
    live_rows[...] = masks[...]


def lifted(z, amplitudes, lift_rows, f):
    pair = jnp.concatenate([amplitudes[0:8], amplitudes[8 * f + 8 : 8 * f + 16]], axis=0)
    return dot(pair, lift_rows[f], (0, 0))


def apply(z, faces, arranged, packed):
    packed[...] = jnp.zeros(packed.shape, F32)
    for f in range(4):
        wide = jnp.concatenate([faces[f], jnp.zeros((z.cases, z.width - z.lanes), F32)], axis=1)
        shift = f * z.face - z.starts[f]
        packed[:, z.starts[f] : z.starts[f] + z.width] += pltpu.roll(wide, shift, 1) if shift else wide
    return dot(packed[:, 0 : z.order].astype(BF16), arranged[...], precision=None)


def unpacked(z, values, packed):
    packed[:, 0 : z.order] = values
    found = []
    for f in range(4):
        part = packed[:, z.starts[f] : z.starts[f] + z.width]
        shift = f * z.face - z.starts[f]
        part = (pltpu.roll(part, z.width - shift, 1) if shift else part)[:, 0 : z.lanes]
        found.append(jnp.where(iota(part.shape, 1) < z.face, part, 0.0))
    return found


def send_coarse(z, faces, rows, scalars, sent, tile):
    tile[...] = jnp.zeros_like(tile)
    mine = jnp.zeros((8, z.cases), F32)
    for f in range(4):
        both = dot(rows[f], faces[f], (1, 1))
        mine = mine + both[0:8]
        tile[:, (1 + f) * z.cases : (2 + f) * z.cases] = both[8:16]
    tile[:, 0 : z.cases] = mine
    send_tile(tile[...], scalars, sent)


def send_tile(values, scalars, sent):
    row, col = iota((8, 128), 0), iota((8, 128), 1)
    for i, scalar in enumerate(scalars):
        values = jnp.where((row == 0) & (col == SCALAR_LANE + i), scalar, values)
    sent[...] = jnp.broadcast_to(values[None], sent.shape)
    sent.push()


def scalar_of(total, i):
    row, col = iota((8, 128), 0), iota((8, 128), 1)
    return jnp.sum(jnp.where((row == 0) & (col == SCALAR_LANE + i), total, 0.0), keepdims=True)


def received_window(z, received):
    ix, _ = place()
    start = window_start(z, ix) * z.ny
    return received[pl.ds(start, z.wide * z.ny)].reshape(z.rows, 128)


def coarse_amplitudes(z, received, solve_rows):
    values = received_window(z, received)
    start = values
    for f in range(4):
        across = pltpu.roll(values, 128 - (1 + (f ^ 1)) * z.cases, 1)
        step = 8 * z.steps[f]
        empty = jnp.zeros((abs(step), 128), F32)
        if step > 0:
            moved = jnp.concatenate([across[step:], empty], axis=0)
        else:
            moved = jnp.concatenate([empty, across[: z.rows + step]], axis=0)
        start = start - moved
    return dot(solve_rows[...], start)[:, 0 : z.cases]


def total(values):
    return jnp.sum(values, keepdims=True)


def face_weights(z):
    ix, iy = place()
    edges = (ix == 0, ix == z.nx - 1, iy == 0, iy == z.ny - 1)
    return [jnp.where(edge, 1.0, 0.5).astype(F32) for edge in edges]


def begin(
    z, lift_rows, primal, received, arranged,
    solve_rows, rows, multipliers, faces, sent, to0, to1, to2, to3,
    matrix, tile, packed,
):
    ix, iy = place()
    near_spots = spots(z, ix, iy)
    values = received_window(z, received)
    lane = iota((z.rows, 128), 1)
    row = iota((z.rows, 128), 0)
    tiled = []
    for f in range(4):
        part = jnp.where(lane // 8 == f, values, 0.0)
        for shift in (64, 32, 16, 8):
            part = part + pltpu.roll(part, shift, 1)
        tiled.append(part)
    for block in range(-(-z.rows // 128)):
        target = (lane + 128 * block) // 8 - row // 8
        part = jnp.zeros((z.rows, 128), F32)
        for f in range(4):
            part = part + jnp.where(target == z.steps[f], tiled[f], 0.0)
        matrix[:, 128 * block : 128 * block + 128] = part
    once = jnp.concatenate([matrix[pl.ds(pl.multiple_of(s * 8, 8), 8), 0 : z.rows] for s in near_spots], axis=0)
    twice = dot(once, matrix[:, 0 : z.rows])
    cols = z.rows
    unit = jnp.concatenate([
        (iota((8, cols), 1) == iota((8, cols), 0) + s * 8).astype(F32) for s in near_spots
    ], axis=0)
    solve = unit + once + twice
    solve_rows[...] = solve
    amplitudes = dot(solve, values)[:, FIRST_LANE : FIRST_LANE + z.cases]
    start = window_start(z, ix) * z.ny
    inverses = [received[pl.ds(start + spot, 1)][0][:, INVERSE_LANE : INVERSE_LANE + 8] for spot in near_spots]
    fields = []
    own = dot(inverses[0], jnp.concatenate([lift_rows[f][0:8] * SIGNS[f] for f in range(4)], axis=1))
    for f in range(4):
        near = dot(inverses[1 + f], lift_rows[f][8:16] * -SIGNS[f])
        rows[f] = jnp.concatenate([own[:, f * z.lanes : (f + 1) * z.lanes], near], axis=0)
        fields.append(lifted(z, amplitudes, lift_rows, f))
        multipliers[f] = fields[f]
    for item in (solve_rows, rows, multipliers):
        item.push()
    image = unpacked(z, primal[...] - apply(z, fields, arranged, packed), packed)
    for f in range(4):
        faces[f] = image[f]
    faces.push()
    send_faces(z, image, (to0, to1, to2, to3))
    send_coarse(z, image, rows, [], sent, tile)


def jumped(z, masks, faces, got):
    near = across_faces(z, got)
    return [masks[f : f + 1] * SIGNS[f] * (faces[f] - near[f]) for f in range(4)]


def first_direction(
    z, solve_rows, lift_rows, faces, masks, rows, got3, got1, got0, got2, received, arranged,
    residual, direction, image, sent, to0, to1, to2, to3,
    tile, packed,
):
    amplitudes = coarse_amplitudes(z, received, solve_rows)
    field = jumped(z, masks, faces, (got0, got1, got2, got3))
    weights = face_weights(z)
    moved = [field[f] - lifted(z, amplitudes, lift_rows, f) for f in range(4)]
    for f in range(4):
        residual[f] = field[f]
        direction[f] = moved[f]
    residual.push()
    direction.push()
    found = unpacked(z, apply(z, moved, arranged, packed), packed)
    for f in range(4):
        image[f] = found[f]
    image.push()
    gamma = sum(weights[f] * total(field[f] * moved[f]) for f in range(4))
    curvature = sum(SIGNS[f] * total(moved[f] * found[f]) for f in range(4))
    send_faces(z, found, (to0, to1, to2, to3))
    send_coarse(z, found, rows, [gamma, curvature], sent, tile)


def second_direction(
    z, solve_rows, lift_rows, faces, masks, residual, direction, multipliers,
    got3, got1, got0, got2, received, arranged,
    next_multipliers, next_residual, projected, image, fresh, sums, sent, to0, to1, to2, to3,
    packed,
):
    amplitudes = coarse_amplitudes(z, received, solve_rows)
    summed = jnp.sum(received[...], axis=0)
    sums[...] = summed
    alpha = scalar_of(summed, 0) / scalar_of(summed, 1)
    field = jumped(z, masks, faces, (got0, got1, got2, got3))
    weights = face_weights(z)
    left, moved = [], []
    for f in range(4):
        image[f] = field[f]
        next_multipliers[f] = multipliers[f] + alpha * direction[f]
        left.append(residual[f] - alpha * field[f])
        moved.append(direction[f] - alpha * (field[f] - lifted(z, amplitudes, lift_rows, f)))
        next_residual[f] = left[f]
        projected[f] = moved[f]
    for item in (sums, image, next_multipliers, next_residual, projected):
        item.push()
    found = unpacked(z, apply(z, moved, arranged, packed), packed)
    for f in range(4):
        fresh[f] = found[f]
    fresh.push()
    send_faces(z, found, (to0, to1, to2, to3))
    gamma = sum(weights[f] * total(left[f] * moved[f]) for f in range(4))
    straight = sum(SIGNS[f] * total(moved[f] * found[f]) for f in range(4))
    crossed = sum(
        weights[f] * total(moved[f] * field[f]) + SIGNS[f] * total(direction[f] * found[f]) for f in range(4)
    )
    send_tile(jnp.zeros((8, 128), F32), [gamma, straight, crossed], sent)


def finish(
    z, sums, faces, masks, residual, image, multipliers, projected, direction,
    got3, got1, got0, got2, received,
    out_multipliers, out_residual,
):
    summed = jnp.sum(received[...], axis=0)
    field = jumped(z, masks, faces, (got0, got1, got2, got3))
    gamma, curvature = scalar_of(sums[...], 0), scalar_of(sums[...], 1)
    fresh, straight, crossed = (scalar_of(summed, i) for i in range(3))
    beta = fresh / gamma
    alpha = fresh / (straight + beta * crossed + beta * beta * curvature)
    for f in range(4):
        step = projected[f] + beta * direction[f]
        out_multipliers[0, 0, f] = (multipliers[f] + alpha * step)[:, 0 : z.face]
        out_residual[0, 0, f] = (residual[f] - alpha * (field[f] + beta * image[f]))[:, 0 : z.face]


class Coming:
    def __init__(self, source, held, semaphore):
        self.held = held
        self.copy = pltpu.make_async_copy(source, held, semaphore)
        self.copy.start()

    def ready(self):
        if self.copy is not None:
            self.copy.wait()
            self.copy = None
        return self.held

    def __getitem__(self, index):
        return self.ready()[index]


class Going:
    def __init__(self, held, target, semaphore):
        self.held = held
        self.copy = pltpu.make_async_copy(held, target, semaphore)
        self.shape, self.dtype = held.shape, held.dtype
        self.started = False

    def __getitem__(self, index):
        return self.held[index]

    def __setitem__(self, index, values):
        self.held[index] = values

    def push(self):
        if not self.started:
            self.copy.start()
            self.started = True


def call(z, kernel, outs, args, scratch=(), flops=0, near=0, kept=0):
    shapes = [jax.ShapeDtypeStruct(shape, dtype) for shape, dtype in outs]
    moved = sum(a.size * a.dtype.itemsize for a in args) + sum(s.size * s.dtype.itemsize for s in shapes)
    far, sent = len(args) - near, len(outs) - kept

    def run(*refs):
        refs = list(refs)
        take = lambda n: [refs.pop(0) for _ in range(n)]
        sources, others, targets, direct = take(far), take(near), take(sent), take(kept)
        held, made, work = take(far), take(sent), take(len(scratch))
        coming = [Coming(a, b, refs[0].at[i]) for i, (a, b) in enumerate(zip(sources, held))]
        going = [Going(a, b, refs[0].at[far + i]) for i, (a, b) in enumerate(zip(made, targets))]
        kernel(z, *coming, *others, *going, *direct, *work)
        for item in going:
            item.push()
        for item in coming:
            item.ready()
        for item in going:
            item.copy.wait()

    near_spec = lambda a: pl.BlockSpec(memory_space=SMEM if a.ndim == 3 and a.size == 4 else VMEM)
    far_spec = pl.BlockSpec(memory_space=pltpu.HBM)
    buffers = [(SMEM if a.size == 4 else VMEM)(a.shape, a.dtype) for a in list(args[:far]) + shapes[:sent]]
    semaphores = [pltpu.SemaphoreType.DMA((far + sent,))] if far + sent else []
    return pl.pallas_call(
        run,
        out_shape=[pltpu.HBM(a.shape, a.dtype) for a in shapes[:sent]] + shapes[sent:],
        in_specs=[far_spec] * far + [near_spec(a) for a in args[far:]],
        out_specs=[far_spec] * sent + [near_spec(a) for a in shapes[sent:]],
        scratch_shapes=buffers + [VMEM(shape, dtype) for shape, dtype in scratch] + semaphores,
        compiler_params=pltpu.CompilerParams(vmem_limit_bytes=24 * 2**20),
        cost_estimate=pl.CostEstimate(flops=flops, bytes_accessed=moved, transcendentals=0),
        name=kernel.__name__,
    )(*[pltpu.with_memory_space_constraint(a, pltpu.HBM) for a in args[:far]], *args[far:])


def gather(values):
    return lax.all_to_all(values, AXES, 0, 0, tiled=True)


def body(ops, traces, primal, loads, maps, counts):
    z = Sizes(lax.axis_size("gx"), lax.axis_size("gy"), traces, loads)
    field = ((4, z.cases, z.lanes), F32)
    mode_rows = ((4, 8, z.lanes), F32)
    pair_rows = ((4, 16, z.lanes), F32)
    live_rows = ((8, z.lanes), F32)
    tile = ((8, 128), F32)
    sent = ((z.count, 8, 128), F32)
    to_faces = [((z.cases, z.lanes), F32)] * 4
    columns = -(-z.rows // 128) * 128
    product_flops = 2 * z.cases * z.order**2

    padded, masks, *trace_faces = call(
        z, prepare, [mode_rows, live_rows] + [((8, z.lanes), F32)] * 4,
        [jnp.transpose(traces, (0, 1, 3, 2, 4)), counts], kept=6,
    )
    got = exchange(trace_faces)
    (local_tile,) = call(
        z, invert, [tile], [jnp.transpose(loads, (0, 2, 1, 3)), padded, masks],
        [tile, ((8, z.cases), F32)], product_flops, near=2, kept=1,
    )
    blocks, masks, lift_rows = call(
        z, couple, [sent, live_rows, pair_rows], [padded, masks, local_tile, *got], [tile], near=7,
    )
    blocks = gather(blocks)
    packed = ((z.cases, z.padded), F32)
    primal_packed, arranged = call(
        z, arrange, [((z.cases, z.order), F32), ((z.order, z.order), BF16)], [maps, ops, primal],
        [((8, z.padded), jnp.int32), ((z.order, z.order), BF16)], 4 * z.order**2 * z.width, kept=1,
    )
    solve_rows, rows, multipliers, faces, coarse, *sent_faces = call(
        z, begin, [((40, z.rows), F32), pair_rows, field, field, sent] + to_faces,
        [lift_rows, primal_packed, blocks, arranged],
        [((z.rows, columns), F32), tile, packed], product_flops, near=2,
    )
    coarse, got = gather(coarse), exchange(sent_faces)
    residual, direction, faces, coarse, *sent_faces = call(
        z, first_direction, [field, field, field, sent] + to_faces,
        [solve_rows, lift_rows, faces, masks, rows, *got, coarse, arranged],
        [tile, packed], product_flops, near=6,
    )
    coarse, got = gather(coarse), exchange(sent_faces)
    multipliers, residual, projected, image, faces, sums, coarse, *sent_faces = call(
        z, second_direction, [field, field, field, field, field, tile, sent] + to_faces,
        [solve_rows, lift_rows, faces, masks, residual, direction, multipliers, *got, coarse, arranged],
        [packed], product_flops, near=6,
    )
    coarse, got = gather(coarse), exchange(sent_faces)
    whole = ((1, 1, 4, z.cases, z.face), F32)
    multipliers, residual = call(
        z, finish, [whole, whole],
        [sums, faces, masks, residual, image, multipliers, projected, direction, *got, coarse], near=5,
    )
    return multipliers, residual


def solution(mesh):
    in_specs = (
        P("gx", "gy", None, None),
        P("gx", "gy", None, None, None),
        P("gx", "gy", None, None),
        P("gx", "gy", None, None),
        P("gx", "gy", None, None),
        P("gx", "gy", None),
    )
    out_specs = (P("gx", "gy", None, None, None), P("gx", "gy", None, None, None))
    return jax.shard_map(body, mesh=mesh, in_specs=in_specs, out_specs=out_specs, check_vma=False)
```

```python
import functools

import jax
import jax.numpy as jnp
from jax import lax
from jax.experimental import pallas as pl
from jax.experimental.pallas import tpu as pltpu
from jax.sharding import PartitionSpec as P

SIGNS = (-1.0, 1.0, -1.0, 1.0)
HIGHEST = lax.Precision.HIGHEST
AXES = ("gx", "gy")
F32 = jnp.float32
BF16 = jnp.bfloat16
VMEM = pltpu.VMEM
SMEM = pltpu.SMEM
FIRST_LANE = 32
INVERSE_LANE = 48
SCALAR_LANE = 96
BLOCK = 256
SWAPS = (1, 3, 0, 2)


class Sizes:
    def __init__(self, nx, ny, traces, loads):
        self.nx, self.ny = nx, ny
        self.count = nx * ny
        self.modes, self.face = traces.shape[-2:]
        self.cases = loads.shape[-1]
        self.order = 4 * self.face
        self.lanes = -(-self.face // 128) * 128
        self.starts = [f * self.face // 128 * 128 for f in range(4)]
        ends = [-(-(f + 1) * self.face // 128) * 128 for f in range(4)]
        self.width = max(e - s for s, e in zip(self.starts, ends))
        self.padded = max(s + self.width for s in self.starts)
        self.wide = min(nx, 9)
        self.rows = self.wide * ny * 8
        self.steps = (-ny, ny, -1, 1)


def dot(a, b, contract=(1, 0), precision=HIGHEST):
    dims = (((contract[0],), (contract[1],)), ((), ()))
    return lax.dot_general(a, b, dims, precision=precision, preferred_element_type=F32)


def iota(shape, dim):
    return lax.broadcasted_iota(jnp.int32, shape, dim)


def place():
    return lax.axis_index("gx"), lax.axis_index("gy")


def window_start(z, ix):
    return jnp.clip(ix - 4, 0, z.nx - z.wide) if z.wide < z.nx else 0


def spots(z, ix, iy):
    own = (ix - window_start(z, ix)) * z.ny + iy
    return [own] + [jnp.clip(own + step, 0, z.wide * z.ny - 1) for step in z.steps]


def send_faces(z, faces, sent):
    for i, at in enumerate(place()):
        even = at % 2 == 0
        low, high = faces[2 * i], faces[2 * i + 1]
        sent[2 * i][...] = jnp.where(even, high, low)
        sent[2 * i + 1][...] = jnp.where(even, low, high)
        sent[2 * i].push()
        sent[2 * i + 1].push()


def across_faces(z, got):
    found = []
    for i, at in enumerate(place()):
        even = at % 2 == 0
        first, second = got[2 * i][...], got[2 * i + 1][...]
        found += [jnp.where(even, second, first), jnp.where(even, first, second)]
    return found


def exchange(sent):
    got = []
    for i in SWAPS:
        axis = AXES[i // 2]
        pairs = []
        for low in range(i % 2, lax.axis_size(axis) - 1, 2):
            pairs += [(low, low + 1), (low + 1, low)]
        got.append(lax.ppermute(sent[i], axis, pairs))
    return got


def prepare(z, traces, counts, padded, masks, *sent):
    padded[...] = jnp.zeros(padded.shape, F32)
    for f in range(4):
        for j in range(z.modes):
            padded[f, j : j + 1, 0 : z.face] = traces[0, 0, j, f : f + 1]
    for i, at in enumerate(place()):
        even = at % 2 == 0
        low, high = padded[2 * i], padded[2 * i + 1]
        sent[2 * i][...] = jnp.where(even, high, low)
        sent[2 * i + 1][...] = jnp.where(even, low, high)
    row, lane = iota(masks.shape, 0), iota(masks.shape, 1)
    live = jnp.zeros(masks.shape, F32)
    for f in range(4):
        live = jnp.where((row == f) & (lane < counts[0, 0, f]), 1.0, live)
    masks[...] = live


def blocks_of(z):
    found = []
    for low in range(0, z.order, BLOCK):
        high = min(low + BLOCK, z.order)
        first, last = low // z.face, (high - 1) // z.face
        found.append((low, high, first * z.face // 128 * 128, min(-(-(last + 1) * z.face // 128) * 128, z.order)))
    return found


def arrange(z, maps, ops, primal, primal_packed, arranged, flat, half):
    flat[...] = jnp.zeros_like(flat)
    flat[0:4, 0 : z.face] = maps[0, 0]
    lane = iota((1, z.padded), 1)
    line = jnp.full((1, z.padded), -1, jnp.int32)
    signs = jnp.zeros((1, z.padded), F32)
    for f in range(4):
        moved = pltpu.roll(flat[...], f * z.face, 1)[f : f + 1] if f else flat[0:1]
        here = (lane >= f * z.face) & (lane < (f + 1) * z.face)
        line = jnp.where(here, moved + f * z.face, line)
        signs = jnp.where(here, SIGNS[f], signs)
    column = jnp.transpose(jnp.broadcast_to(line, (8, z.padded)))[:, 0:1]
    spread = []
    for low, high, first, last in blocks_of(z):
        hit = (iota((last - first, high - low), 1) + low) == column[first:last]
        spread.append(hit.astype(F32).astype(BF16))
    for low, high, first, last in blocks_of(z):
        hit = (iota((high - low, last - first), 0) + low) == line[:, first:last]
        collect = jnp.where(hit, signs[:, first:last], 0.0).astype(BF16)
        half[low:high, :] = dot(collect, ops[0, 0, first:last, :], precision=None).astype(BF16)
    values = primal[0, 0]
    parts = []
    for _ in range(3):
        parts.append(values.astype(BF16))
        values = values - parts[-1].astype(F32)
    pieces = jnp.concatenate(parts, axis=0)
    n = z.cases
    for (low, high, first, last), there in zip(blocks_of(z), spread):
        three = dot(pieces[:, first:last], there, precision=None)
        primal_packed[:, low:high] = three[0:n] + (three[n : 2 * n] + three[2 * n :])
    primal_packed.push()
    for (low, high, first, last), there in zip(blocks_of(z), spread):
        arranged[:, low:high] = dot(half[:, first:last], there, precision=None).astype(BF16)


def invert(z, loads, padded, masks, local_tile, aug, small):
    diagonal = sum(dot(padded[f] * masks[f : f + 1], padded[f], (1, 1)) for f in range(4))
    row, col = iota((8, 128), 0), iota((8, 128), 1)
    aug[...] = jnp.where((col == row + 8) & (row < z.modes), 1.0, 0.0).astype(F32)
    aug[:, 0:8] = diagonal
    matrix = aug[...]
    for p in range(z.modes):
        scaled = matrix[p : p + 1, :] / matrix[p : p + 1, p : p + 1]
        taken = matrix[:, p : p + 1] - (row[:, 0:1] == p).astype(F32)
        matrix = matrix - taken * scaled
    inverse = matrix[:, 8:16]
    small[...] = jnp.zeros(small.shape, F32)
    for j in range(z.modes):
        small[j : j + 1, :] = loads[0, j]
    local_tile[...] = jnp.zeros(local_tile.shape, F32)
    local_tile[:, FIRST_LANE : FIRST_LANE + z.cases] = dot(inverse, small[...])
    local_tile[:, INVERSE_LANE : INVERSE_LANE + 8] = inverse


def couple(z, padded, masks, local_tile, got1, got3, got0, got2, sent, live_rows, lift_rows, tile):
    near = across_faces(z, (got0, got1, got2, got3))
    inverse = local_tile[:, INVERSE_LANE : INVERSE_LANE + 8]
    tile[...] = local_tile[...]
    for f in range(4):
        live = padded[f] * masks[f : f + 1]
        lift_rows[f] = jnp.concatenate([live * SIGNS[f], near[f] * masks[f : f + 1] * -SIGNS[f]], axis=0)
        tile[:, 8 * f : 8 * f + 8] = dot(inverse, dot(live, near[f], (1, 1)))
    sent[...] = jnp.broadcast_to(tile[...][None], sent.shape)
    sent.push()
    live_rows[...] = masks[...]


def lifted(z, amplitudes, lift_rows, f):
    pair = jnp.concatenate([amplitudes[0:8], amplitudes[8 * f + 8 : 8 * f + 16]], axis=0)
    return dot(pair, lift_rows[f], (0, 0))


def apply(z, faces, arranged, packed):
    packed[...] = jnp.zeros(packed.shape, F32)
    for f in range(4):
        wide = jnp.concatenate([faces[f], jnp.zeros((z.cases, z.width - z.lanes), F32)], axis=1)
        shift = f * z.face - z.starts[f]
        packed[:, z.starts[f] : z.starts[f] + z.width] += pltpu.roll(wide, shift, 1) if shift else wide
    return dot(packed[:, 0 : z.order].astype(BF16), arranged[...], precision=None)


def unpacked(z, values, packed):
    packed[:, 0 : z.order] = values
    found = []
    for f in range(4):
        part = packed[:, z.starts[f] : z.starts[f] + z.width]
        shift = f * z.face - z.starts[f]
        part = (pltpu.roll(part, z.width - shift, 1) if shift else part)[:, 0 : z.lanes]
        found.append(jnp.where(iota(part.shape, 1) < z.face, part, 0.0))
    return found


def send_coarse(z, faces, rows, scalars, sent, tile):
    tile[...] = jnp.zeros_like(tile)
    mine = jnp.zeros((8, z.cases), F32)
    for f in range(4):
        both = dot(rows[f], faces[f], (1, 1))
        mine = mine + both[0:8]
        tile[:, (1 + f) * z.cases : (2 + f) * z.cases] = both[8:16]
    tile[:, 0 : z.cases] = mine
    send_tile(tile[...], scalars, sent)


def send_tile(values, scalars, sent):
    row, col = iota((8, 128), 0), iota((8, 128), 1)
    for i, scalar in enumerate(scalars):
        values = jnp.where((row == 0) & (col == SCALAR_LANE + i), scalar, values)
    sent[...] = jnp.broadcast_to(values[None], sent.shape)
    sent.push()


def scalar_of(total, i):
    row, col = iota((8, 128), 0), iota((8, 128), 1)
    return jnp.sum(jnp.where((row == 0) & (col == SCALAR_LANE + i), total, 0.0), keepdims=True)


def received_window(z, received):
    ix, _ = place()
    start = window_start(z, ix) * z.ny
    return received[pl.ds(start, z.wide * z.ny)].reshape(z.rows, 128)


def coarse_amplitudes(z, received, solve_rows):
    values = received_window(z, received)
    start = values
    for f in range(4):
        across = pltpu.roll(values, 128 - (1 + (f ^ 1)) * z.cases, 1)
        step = 8 * z.steps[f]
        empty = jnp.zeros((abs(step), 128), F32)
        if step > 0:
            moved = jnp.concatenate([across[step:], empty], axis=0)
        else:
            moved = jnp.concatenate([empty, across[: z.rows + step]], axis=0)
        start = start - moved
    return dot(solve_rows[...], start)[:, 0 : z.cases]


def total(values):
    return jnp.sum(values, keepdims=True)


def face_weights(z):
    ix, iy = place()
    edges = (ix == 0, ix == z.nx - 1, iy == 0, iy == z.ny - 1)
    return [jnp.where(edge, 1.0, 0.5).astype(F32) for edge in edges]


def begin(
    z, lift_rows, primal, received, arranged,
    solve_rows, rows, multipliers, faces, sent, to0, to1, to2, to3,
    matrix, tile, packed,
):
    ix, iy = place()
    near_spots = spots(z, ix, iy)
    values = received_window(z, received)
    lane = iota((z.rows, 128), 1)
    row = iota((z.rows, 128), 0)
    tiled = []
    for f in range(4):
        part = jnp.where(lane // 8 == f, values, 0.0)
        for shift in (64, 32, 16, 8):
            part = part + pltpu.roll(part, shift, 1)
        tiled.append(part)
    for block in range(-(-z.rows // 128)):
        target = (lane + 128 * block) // 8 - row // 8
        part = jnp.zeros((z.rows, 128), F32)
        for f in range(4):
            part = part + jnp.where(target == z.steps[f], tiled[f], 0.0)
        matrix[:, 128 * block : 128 * block + 128] = part
    once = jnp.concatenate([matrix[pl.ds(pl.multiple_of(s * 8, 8), 8), 0 : z.rows] for s in near_spots], axis=0)
    twice = dot(once, matrix[:, 0 : z.rows])
    cols = z.rows
    unit = jnp.concatenate([
        (iota((8, cols), 1) == iota((8, cols), 0) + s * 8).astype(F32) for s in near_spots
    ], axis=0)
    solve = unit + once + twice
    solve_rows[...] = solve
    amplitudes = dot(solve, values)[:, FIRST_LANE : FIRST_LANE + z.cases]
    start = window_start(z, ix) * z.ny
    inverses = [received[pl.ds(start + spot, 1)][0][:, INVERSE_LANE : INVERSE_LANE + 8] for spot in near_spots]
    fields = []
    own = dot(inverses[0], jnp.concatenate([lift_rows[f][0:8] * SIGNS[f] for f in range(4)], axis=1))
    for f in range(4):
        near = dot(inverses[1 + f], lift_rows[f][8:16] * -SIGNS[f])
        rows[f] = jnp.concatenate([own[:, f * z.lanes : (f + 1) * z.lanes], near], axis=0)
        fields.append(lifted(z, amplitudes, lift_rows, f))
        multipliers[f] = fields[f]
    for item in (solve_rows, rows, multipliers):
        item.push()
    image = unpacked(z, primal[...] - apply(z, fields, arranged, packed), packed)
    for f in range(4):
        faces[f] = image[f]
    faces.push()
    send_faces(z, image, (to0, to1, to2, to3))
    send_coarse(z, image, rows, [], sent, tile)


def jumped(z, masks, faces, got):
    near = across_faces(z, got)
    return [masks[f : f + 1] * SIGNS[f] * (faces[f] - near[f]) for f in range(4)]


def first_direction(
    z, solve_rows, lift_rows, faces, masks, rows, got1, got3, got0, got2, received, arranged,
    residual, direction, image, sent, to0, to1, to2, to3,
    tile, packed,
):
    amplitudes = coarse_amplitudes(z, received, solve_rows)
    field = jumped(z, masks, faces, (got0, got1, got2, got3))
    weights = face_weights(z)
    moved = [field[f] - lifted(z, amplitudes, lift_rows, f) for f in range(4)]
    for f in range(4):
        residual[f] = field[f]
        direction[f] = moved[f]
    residual.push()
    direction.push()
    found = unpacked(z, apply(z, moved, arranged, packed), packed)
    for f in range(4):
        image[f] = found[f]
    image.push()
    gamma = total(sum(weights[f] * (field[f] * moved[f]) for f in range(4)))
    curvature = total(sum(SIGNS[f] * (moved[f] * found[f]) for f in range(4)))
    send_faces(z, found, (to0, to1, to2, to3))
    send_coarse(z, found, rows, [gamma, curvature], sent, tile)


def second_direction(
    z, solve_rows, lift_rows, faces, masks, residual, direction, multipliers,
    got1, got3, got0, got2, received, arranged,
    next_multipliers, next_residual, projected, image, fresh, sums, sent, to0, to1, to2, to3,
    packed,
):
    amplitudes = coarse_amplitudes(z, received, solve_rows)
    summed = jnp.sum(received[...], axis=0)
    sums[...] = summed
    alpha = scalar_of(summed, 0) / scalar_of(summed, 1)
    field = jumped(z, masks, faces, (got0, got1, got2, got3))
    weights = face_weights(z)
    left, moved = [], []
    for f in range(4):
        image[f] = field[f]
        next_multipliers[f] = multipliers[f] + alpha * direction[f]
        left.append(residual[f] - alpha * field[f])
        moved.append(direction[f] - alpha * (field[f] - lifted(z, amplitudes, lift_rows, f)))
        next_residual[f] = left[f]
        projected[f] = moved[f]
    for item in (sums, image, next_multipliers, next_residual, projected):
        item.push()
    found = unpacked(z, apply(z, moved, arranged, packed), packed)
    for f in range(4):
        fresh[f] = found[f]
    fresh.push()
    send_faces(z, found, (to0, to1, to2, to3))
    gamma = total(sum(weights[f] * (left[f] * moved[f]) for f in range(4)))
    straight = total(sum(SIGNS[f] * (moved[f] * found[f]) for f in range(4)))
    crossed = total(sum(
        weights[f] * (moved[f] * field[f]) + SIGNS[f] * (direction[f] * found[f]) for f in range(4)
    ))
    send_tile(jnp.zeros((8, 128), F32), [gamma, straight, crossed], sent)


def finish(
    z, sums, faces, masks, residual, image, multipliers, projected, direction,
    got1, got3, got0, got2, received,
    out_multipliers, out_residual,
):
    summed = jnp.sum(received[...], axis=0)
    field = jumped(z, masks, faces, (got0, got1, got2, got3))
    gamma, curvature = scalar_of(sums[...], 0), scalar_of(sums[...], 1)
    fresh, straight, crossed = (scalar_of(summed, i) for i in range(3))
    beta = fresh / gamma
    alpha = fresh / (straight + beta * crossed + beta * beta * curvature)
    for f in range(4):
        step = projected[f] + beta * direction[f]
        out_multipliers[0, 0, f] = (multipliers[f] + alpha * step)[:, 0 : z.face]
        out_residual[0, 0, f] = (residual[f] - alpha * (field[f] + beta * image[f]))[:, 0 : z.face]


class Coming:
    def __init__(self, source, held, semaphore):
        self.held = held
        self.copy = pltpu.make_async_copy(source, held, semaphore)
        self.copy.start()

    def ready(self):
        if self.copy is not None:
            self.copy.wait()
            self.copy = None
        return self.held

    def __getitem__(self, index):
        return self.ready()[index]


class Going:
    def __init__(self, held, target, semaphore):
        self.held = held
        self.copy = pltpu.make_async_copy(held, target, semaphore)
        self.shape, self.dtype = held.shape, held.dtype
        self.started = False

    def __getitem__(self, index):
        return self.held[index]

    def __setitem__(self, index, values):
        self.held[index] = values

    def push(self):
        if not self.started:
            self.copy.start()
            self.started = True


def call(z, kernel, outs, args, scratch=(), flops=0, near=0, kept=0):
    shapes = [jax.ShapeDtypeStruct(shape, dtype) for shape, dtype in outs]
    moved = sum(a.size * a.dtype.itemsize for a in args) + sum(s.size * s.dtype.itemsize for s in shapes)
    far, sent = len(args) - near, len(outs) - kept

    def run(*refs):
        refs = list(refs)
        take = lambda n: [refs.pop(0) for _ in range(n)]
        sources, others, targets, direct = take(far), take(near), take(sent), take(kept)
        held, made, work = take(far), take(sent), take(len(scratch))
        coming = [Coming(a, b, refs[0].at[i]) for i, (a, b) in enumerate(zip(sources, held))]
        going = [Going(a, b, refs[0].at[far + i]) for i, (a, b) in enumerate(zip(made, targets))]
        kernel(z, *coming, *others, *going, *direct, *work)
        for item in going:
            item.push()
        for item in coming:
            item.ready()
        for item in going:
            item.copy.wait()

    near_spec = lambda a: pl.BlockSpec(memory_space=SMEM if a.ndim == 3 and a.size == 4 else VMEM)
    far_spec = pl.BlockSpec(memory_space=pltpu.HBM)
    buffers = [(SMEM if a.size == 4 else VMEM)(a.shape, a.dtype) for a in list(args[:far]) + shapes[:sent]]
    semaphores = [pltpu.SemaphoreType.DMA((far + sent,))] if far + sent else []
    return pl.pallas_call(
        run,
        out_shape=[pltpu.HBM(a.shape, a.dtype) for a in shapes[:sent]] + shapes[sent:],
        in_specs=[far_spec] * far + [near_spec(a) for a in args[far:]],
        out_specs=[far_spec] * sent + [near_spec(a) for a in shapes[sent:]],
        scratch_shapes=buffers + [VMEM(shape, dtype) for shape, dtype in scratch] + semaphores,
        compiler_params=pltpu.CompilerParams(vmem_limit_bytes=24 * 2**20),
        cost_estimate=pl.CostEstimate(flops=flops, bytes_accessed=moved, transcendentals=0),
        name=kernel.__name__,
    )(*[pltpu.with_memory_space_constraint(a, pltpu.HBM) for a in args[:far]], *args[far:])


def gather(values):
    return lax.all_to_all(values, AXES, 0, 0, tiled=True)


def body(ops, traces, primal, loads, maps, counts):
    z = Sizes(lax.axis_size("gx"), lax.axis_size("gy"), traces, loads)
    field = ((4, z.cases, z.lanes), F32)
    mode_rows = ((4, 8, z.lanes), F32)
    pair_rows = ((4, 16, z.lanes), F32)
    live_rows = ((8, z.lanes), F32)
    tile = ((8, 128), F32)
    sent = ((z.count, 8, 128), F32)
    to_faces = [((z.cases, z.lanes), F32)] * 4
    columns = -(-z.rows // 128) * 128
    product_flops = 2 * z.cases * z.order**2

    padded, masks, *trace_faces = call(
        z, prepare, [mode_rows, live_rows] + [((8, z.lanes), F32)] * 4,
        [jnp.transpose(traces, (0, 1, 3, 2, 4)), counts], kept=6,
    )
    got = exchange(trace_faces)
    (local_tile,) = call(
        z, invert, [tile], [jnp.transpose(loads, (0, 2, 1, 3)), padded, masks],
        [tile, ((8, z.cases), F32)], product_flops, near=2, kept=1,
    )
    blocks, masks, lift_rows = call(
        z, couple, [sent, live_rows, pair_rows], [padded, masks, local_tile, *got], [tile], near=7,
    )
    blocks = gather(blocks)
    packed = ((z.cases, z.padded), F32)
    primal_packed, arranged = call(
        z, arrange, [((z.cases, z.order), F32), ((z.order, z.order), BF16)], [maps, ops, primal],
        [((8, z.padded), jnp.int32), ((z.order, z.order), BF16)], 4 * z.order**2 * z.width, kept=1,
    )
    solve_rows, rows, multipliers, faces, coarse, *sent_faces = call(
        z, begin, [((40, z.rows), F32), pair_rows, field, field, sent] + to_faces,
        [lift_rows, primal_packed, blocks, arranged],
        [((z.rows, columns), F32), tile, packed], product_flops, near=2,
    )
    coarse, got = gather(coarse), exchange(sent_faces)
    residual, direction, faces, coarse, *sent_faces = call(
        z, first_direction, [field, field, field, sent] + to_faces,
        [solve_rows, lift_rows, faces, masks, rows, *got, coarse, arranged],
        [tile, packed], product_flops, near=6,
    )
    coarse, got = gather(coarse), exchange(sent_faces)
    multipliers, residual, projected, image, faces, sums, coarse, *sent_faces = call(
        z, second_direction, [field, field, field, field, field, tile, sent] + to_faces,
        [solve_rows, lift_rows, faces, masks, residual, direction, multipliers, *got, coarse, arranged],
        [packed], product_flops, near=6,
    )
    coarse, got = gather(coarse), exchange(sent_faces)
    whole = ((1, 1, 4, z.cases, z.face), F32)
    multipliers, residual = call(
        z, finish, [whole, whole],
        [sums, faces, masks, residual, image, multipliers, projected, direction, *got, coarse], near=5,
    )
    return multipliers, residual


def solution(mesh):
    in_specs = (
        P("gx", "gy", None, None),
        P("gx", "gy", None, None, None),
        P("gx", "gy", None, None),
        P("gx", "gy", None, None),
        P("gx", "gy", None, None),
        P("gx", "gy", None),
    )
    out_specs = (P("gx", "gy", None, None, None), P("gx", "gy", None, None, None))
    return jax.shard_map(body, mesh=mesh, in_specs=in_specs, out_specs=out_specs, check_vma=False)
```
